256 devices in a mesh: tm: 16 (over x_lo, z), sx: 2 (over x_hi), sy: 8 (over y, core).
Axes of the slice: x: 4 (x_hi: 2, x_lo: 2; x = x_hi * 2 + x_lo), y: 4, z: 8, core: 2. Of those that a mesh axis runs over, the one named last changes fastest.
Arguments:
- initial: float32 [2, 512, 4096], P(None, 'sx', 'sy'), may hold values from -1 to 1
- forcing: float32 [2, 512, 4096], P(None, 'sx', 'sy'), may hold values from -3 to 3
- start_guess: float32 [16, 2, 512, 4096], P('tm', None, 'sx', 'sy'), may hold values from -1 to 1
Outputs:
- solution: float32 [32, 2, 512, 4096], P('tm', None, 'sx', 'sy')
The draws below stay inside these ranges and needn't reach their ends.
All inputs are finite; a program needn't handle non-finite values.
Results may differ from the reference program's by a relative error of at most 0.003.
Values sent between devices are 32-bit elements; how exact they have to be, the bound alone decides.
A program may use at most 64 MiB of HBM per device.

```python
import jax
import jax.numpy as jnp

NX = 512
NY = 4096
N_TM = 16


def block_scale(key, shape, pieces, smallest, high):
    def one(dim, blocks):
        heights = jax.random.uniform(jax.random.fold_in(jax.random.fold_in(key, 6), dim), (blocks,), jnp.float32, smallest / len(pieces), high / len(pieces))
        return jnp.repeat(jnp.exp(heights), shape[dim] // blocks).reshape((-1,) + (1,) * (len(shape) - dim - 1))

    loudness = one(*pieces[0])
    for cut in pieces[1:]:
        loudness = loudness * one(*cut)
    return loudness


def noise(rng, dims, width, reach, pieces=(), dtype=jnp.bfloat16):
    values = jax.random.normal(rng, dims, jnp.float32) * width
    if len(pieces) > 0:
        values = block_scale(rng, dims, pieces, -0.22, 0.18) * values
    return jnp.clip(values, min=-reach, max=reach).astype(dtype)


def setup_inputs(seed: int = 0) -> dict:
    splits = jax.random.split(jax.random.key(seed), 4)
    initial = jnp.clip(jax.random.uniform(splits[0], (2, NX, NY), jnp.float32, -1.0, 1.0) * block_scale(splits[0], (2, NX, NY), ((1, 2), (2, 8)), -0.4, 0.0), -1.0, 1.0)
    forcing = noise(splits[1], (2, NX, NY), 0.5, 3.0, ((1, 2), (2, 8)), jnp.float32)
    start_guess = jnp.clip(jax.random.uniform(splits[2], (N_TM, 2, NX, NY), jnp.float32, -1.0, 1.0) * block_scale(splits[2], (N_TM, 2, NX, NY), ((0, 16), (2, 2), (3, 8)), -0.4, 0.0), -1.0, 1.0)
    return dict(initial=initial, forcing=forcing, start_guess=start_guess)


VISCOSITY = 0.5
COURANT = 0.7


def advance(padded, forcing, step_size):
    centre = padded[..., 1:-1, 1:-1]
    west_cell = padded[..., :-2, 1:-1]
    east_cell = padded[..., 2:, 1:-1]
    south_cell = padded[..., 1:-1, :-2]
    north_cell = padded[..., 1:-1, 2:]
    first_speed = centre[..., 0:1, :, :]
    second_speed = centre[..., 1:2, :, :]
    spread = east_cell + west_cell + north_cell + south_cell - 4.0 * centre
    carried = (jnp.maximum(first_speed, 0.0) * (centre - west_cell)
               + jnp.minimum(first_speed, 0.0) * (east_cell - centre)
               + jnp.maximum(second_speed, 0.0) * (centre - south_cell)
               + jnp.minimum(second_speed, 0.0) * (north_cell - centre))
    return centre + step_size * (VISCOSITY * spread - carried + forcing)


def propagate(state, forcing, step_size):
    leading = [(0, 0)] * (state.ndim - 2)
    padded = jnp.pad(state, leading + [(1, 1), (1, 1)], mode="wrap")
    return advance(padded, forcing, step_size)


def vcycle(points, right_side, initial, forcing, step_size):
    if points.shape[0] == 2:
        first_point = propagate(initial, forcing, step_size) + right_side[0]
        second = propagate(first_point, forcing, step_size) + right_side[1]
        return jnp.stack((first_point, second))
    coarse_points = points[1::2]
    before = jnp.concatenate((initial[None], coarse_points[:-1]), axis=0)
    relaxed = propagate(before, forcing, step_size) + right_side[0::2]
    residual = right_side[1::2] - (coarse_points - propagate(relaxed, forcing, step_size))
    coarse_rhs = residual + coarse_points - propagate(before, forcing, 2.0 * step_size)
    coarse = vcycle(coarse_points, coarse_rhs, initial, forcing, 2.0 * step_size)
    prior_again = jnp.concatenate((initial[None], coarse[:-1]), axis=0)
    final_state = propagate(prior_again, forcing, step_size) + right_side[0::2]
    return jnp.stack((final_state, coarse), axis=1).reshape(points.shape)


def reference(initial, forcing, start_guess):
    fine_step = COURANT / (N_TM * (2.0 + 4.0 * VISCOSITY))
    points = jnp.stack((jnp.zeros_like(start_guess), start_guess), axis=1)
    points = points.reshape((2 * N_TM,) + start_guess.shape[1:])
    right_side = jnp.zeros_like(points)
    return vcycle(points, right_side, initial, forcing, fine_step)
```

```python
import jax
import jax.numpy as jnp
from jax import lax
from jax.experimental import pallas as pl
from jax.experimental.pallas import tpu as pltpu
from jax.sharding import PartitionSpec as P

VISCOSITY = 0.5
COURANT = 0.7
MESH = pl.DeviceIdType.MESH
NT = 16
ROWS = 16
COLS = 512
TILES = COLS // 128
STEP = COURANT / (NT * (2.0 + 4.0 * VISCOSITY))
BATCH = (16, 16, 8, 4, 3, 3, 4, 3, 1)
NB = len(BATCH)


def slab_of(t):
    return jnp.where(t < 8, t, 23 - t)


def kernel(initial, forcing, guess, out, *scratch):
    (S, F, R0, T1, G1, G2, G3, G4, Fx, U, O, col_out, col_in) = scratch[:13]
    row_out = scratch[13 : 13 + NB]
    row_in = scratch[13 + NB : 13 + 2 * NB]
    local_sem, fwd_send, fwd_recv, halo_send, halo_recv, ret_send, ret_recv, ret_local = scratch[13 + 2 * NB :]

    me = lax.axis_index("tm")
    sx = lax.axis_index("sx")
    sy = lax.axis_index("sy")
    slab = slab_of(me)
    above = {"tm": slab_of(lax.rem(slab + 1, 16)), "sx": jnp.where(slab == 15, 1 - sx, sx)}
    below = {"tm": slab_of(lax.rem(slab + 15, 16)), "sx": jnp.where(slab == 0, 1 - sx, sx)}
    right = {"sy": lax.rem(sy + 1, 8)}
    left = {"sy": lax.rem(sy + 7, 8)}
    sides = (above, below, right, left)

    def rows_of(t):
        return pl.ds(pl.multiple_of(slab_of(t) * ROWS, ROWS), ROWS)

    own_rows = rows_of(me)

    barrier = pltpu.get_barrier_semaphore()

    def greet(d, c):
        pl.semaphore_signal(barrier, inc=1, device_id={"tm": lax.rem(me + d, NT)}, device_id_type=MESH)
        return c

    lax.fori_loop(1, NT, greet, 0)
    for side in sides:
        pl.semaphore_signal(barrier, inc=1, device_id=side, device_id_type=MESH)

    stage_in = [
        pltpu.make_async_copy(initial.at[:, own_rows, :], S.at[0], local_sem.at[0]),
        pltpu.make_async_copy(forcing.at[:, own_rows, :], F, local_sem.at[1]),
        pltpu.make_async_copy(guess.at[0, :, own_rows, :], S.at[me + 1], local_sem.at[2]),
    ]
    for copy in stage_in:
        copy.start()
    pl.semaphore_wait(barrier, NT - 1 + 4)

    def forward(peer):
        return pltpu.make_async_remote_copy(
            src_ref=guess.at[0, :, rows_of(peer), :],
            dst_ref=S.at[me + 1],
            send_sem=fwd_send.at[peer],
            recv_sem=fwd_recv.at[me],
            device_id={"tm": peer},
            device_id_type=MESH,
        )

    def forwarded(peer):
        return pltpu.make_async_remote_copy(
            src_ref=guess.at[0, :, own_rows, :],
            dst_ref=S.at[peer + 1],
            send_sem=fwd_send.at[peer],
            recv_sem=fwd_recv.at[peer],
            device_id={"tm": peer},
            device_id_type=MESH,
        )

    def start_forward(d, c):
        forward(lax.rem(me + d, NT)).start()
        return c

    lax.fori_loop(1, NT, start_forward, 0)
    for copy in stage_in:
        copy.wait()

    lane = lax.broadcasted_iota(jnp.int32, (ROWS, 128), 1)
    row = lax.broadcasted_iota(jnp.int32, (ROWS, 128), 0)
    blank = jnp.zeros((ROWS, 128), jnp.float32)

    def lanes(j):
        return slice(128 * j, 128 * (j + 1))

    def halo_copies(b):
        copies = []
        for i, side in enumerate(sides):
            src, dst = ((row_out[b], row_in[b]) if i < 2 else (col_out.at[b], col_in.at[b]))
            copies.append(
                pltpu.make_async_remote_copy(
                    src_ref=src.at[i % 2],
                    dst_ref=dst.at[i % 2],
                    send_sem=halo_send.at[b, i],
                    recv_sem=halo_recv.at[b, i],
                    device_id=side,
                    device_id_type=MESH,
                )
            )
        return copies

    def send_halo(b, packed):
        col_out[b, 0] = packed[0]
        col_out[b, 1] = packed[1]
        for copy in halo_copies(b):
            copy.start()

    def wait_halo(b):
        for copy in halo_copies(b):
            copy.wait_recv()

    def pack(b, i, c, j, w, packed):
        row_out[b][0, i, c : c + 1, lanes(j)] = w[ROWS - 1 : ROWS]
        row_out[b][1, i, c : c + 1, lanes(j)] = w[0:1]
        index = 2 * i + c
        last, first = packed
        if j == TILES - 1:
            last = jnp.where(lane == index, pltpu.roll(w, index + 1, 1), last)
        if j == 0:
            first = jnp.where(lane == index, pltpu.roll(w, index, 1), first)
        return last, first

    def rates(source, k, b, i):
        w = [[source[k, c, :, lanes(j)] for c in range(2)] for j in range(TILES)]
        up = [[pltpu.roll(w[j][c], 1, 1) for c in range(2)] for j in range(TILES)]
        down = [[pltpu.roll(w[j][c], 127, 1) for c in range(2)] for j in range(TILES)]
        before = [pltpu.roll(col_in[b, 0], 128 - (2 * i + c), 1) for c in range(2)]
        after = [pltpu.roll(col_in[b, 1], 127 - (2 * i + c), 1) for c in range(2)]
        result = []
        for j in range(TILES):
            first, second = w[j]
            east_w = 0.5 - jnp.minimum(first, 0.0)
            west_w = 0.5 + jnp.maximum(first, 0.0)
            north_w = 0.5 - jnp.minimum(second, 0.0)
            south_w = 0.5 + jnp.maximum(second, 0.0)
            pair = []
            for c in range(2):
                x = w[j][c]
                west = jnp.where(row == 0, row_in[b][0, i, c : c + 1, lanes(j)], pltpu.roll(x, 1, 0))
                east = jnp.where(row == ROWS - 1, row_in[b][1, i, c : c + 1, lanes(j)], pltpu.roll(x, ROWS - 1, 0))
                south = jnp.where(lane == 0, up[j - 1][c] if j > 0 else before[c], up[j][c])
                north = jnp.where(lane == 127, down[j + 1][c] if j < TILES - 1 else after[c], down[j][c])
                pair.append(
                    west_w * (west - x)
                    + east_w * (east - x)
                    + south_w * (south - x)
                    + north_w * (north - x)
                    + F[c, :, lanes(j)]
                )
            result.append(pair)
        return w, result

    def each():
        return [(j, c) for j in range(TILES) for c in range(2)]

    def at(ref, k, c, j):
        return ref[k, c, :, lanes(j)]

    def put(ref, k, c, j, value):
        ref[k, c, :, lanes(j)] = value

    def send_back(slot, k, source):
        @pl.when(me == k)
        def _():
            pltpu.make_async_copy(source, out.at[slot, :, own_rows, :], ret_local.at[slot]).start()

        @pl.when(me != k)
        def _():
            back(slot, k, source).start()

    def back(slot, k, source):
        return pltpu.make_async_remote_copy(
            src_ref=source,
            dst_ref=out.at[slot, :, own_rows, :],
            send_sem=ret_send.at[slot, k],
            recv_sem=ret_recv.at[slot, me],
            device_id={"tm": k},
            device_id_type=MESH,
        )

    def arrive(k, packed):
        @pl.when(jnp.logical_and(k > 0, k - 1 != me))
        def _():
            forwarded(k - 1).wait_recv()

        for j, c in each():
            packed = pack(0, k, c, j, at(S, k, c, j), packed)
        return packed

    send_halo(0, lax.fori_loop(0, 16, arrive, (blank, blank)))

    @pl.when(me != 15)
    def _():
        forwarded(15).wait_recv()

    wait_halo(0)

    def first_step(k, packed):
        w, rate = rates(S, k, 0, k)
        for j, c in each():
            put(R0, k, c, j, rate[j][c])
            new = w[j][c] + STEP * rate[j][c]
            put(T1, k, c, j, new)
            packed = pack(1, k, c, j, new, packed)
        return packed

    send_halo(1, lax.fori_loop(0, 16, first_step, (blank, blank)))
    send_back(0, 0, T1.at[0])
    wait_halo(1)

    def coarse_rhs(g, point, image, base):
        residual = g - (point - image)
        return residual + point - base

    def second_step(m, packed):
        for odd in range(2):
            k = 2 * m + odd
            w, rate = rates(T1, k, 1, k)
            for j, c in each():
                base = at(S, k, c, j) + 2 * STEP * at(R0, k, c, j)
                g = coarse_rhs(0.0, at(S, k + 1, c, j), w[j][c] + STEP * rate[j][c], base)
                put(G1, k + 1, c, j, g)
                if not odd:
                    relaxed = base + g
                    put(Fx, k + 1, c, j, relaxed)
                    packed = pack(2, m, c, j, relaxed, packed)
        return packed

    send_halo(2, lax.fori_loop(0, 8, second_step, (blank, blank)))
    send_back(1, 0, Fx.at[1])
    wait_halo(2)

    def third_step(q, packed):
        for odd in range(2):
            m = 2 * q + odd
            k = 2 * m
            w, rate = rates(Fx, k + 1, 2, m)
            for j, c in each():
                base = at(S, k, c, j) + 4 * STEP * at(R0, k, c, j)
                g = coarse_rhs(at(G1, k + 2, c, j), at(S, k + 2, c, j), w[j][c] + 2 * STEP * rate[j][c], base)
                put(G2, m + 1, c, j, g)
                if not odd:
                    put(O, k + 1, c, j, w[j][c] + STEP * rate[j][c])
                    relaxed = base + g
                    put(Fx, k + 2, c, j, relaxed)
                    packed = pack(3, q, c, j, relaxed, packed)
        return packed

    send_halo(3, lax.fori_loop(0, 4, third_step, (blank, blank)))
    send_back(0, 1, O.at[1])
    send_back(1, 1, Fx.at[2])
    wait_halo(3)

    packed = (blank, blank)
    for q in range(4):
        k = 4 * q
        w, rate = rates(Fx, k + 2, 3, q)
        for j, c in each():
            base = at(S, k, c, j) + 8 * STEP * at(R0, k, c, j)
            g = coarse_rhs(at(G2, 2 * q + 2, c, j), at(S, k + 4, c, j), w[j][c] + 4 * STEP * rate[j][c], base)
            put(G3, q + 1, c, j, g)
            if q % 2 == 0:
                relaxed = base + g
                put(Fx, k + 4, c, j, relaxed)
                packed = pack(4, q // 2, c, j, relaxed, packed)
            if q == 0:
                put(O, 2, c, j, w[j][c] + STEP * rate[j][c])
                new = w[j][c] + 2 * STEP * rate[j][c] + at(G1, 3, c, j)
                put(U, 3, c, j, new)
                packed = pack(4, 2, c, j, new, packed)
    send_halo(4, packed)
    send_back(0, 2, O.at[2])
    send_back(1, 2, U.at[3])
    send_back(1, 3, Fx.at[4])
    wait_halo(4)

    packed = (blank, blank)
    for q in range(2):
        k = 8 * q
        w, rate = rates(Fx, k + 4, 4, q)
        for j, c in each():
            base = at(S, k, c, j) + 16 * STEP * at(R0, k, c, j)
            g = coarse_rhs(at(G3, 2 * q + 2, c, j), at(S, k + 8, c, j), w[j][c] + 8 * STEP * rate[j][c], base)
            if q == 1:
                put(G4, 0, c, j, g)
                continue
            new = base + g
            put(U, 8, c, j, new)
            packed = pack(5, 0, c, j, new, packed)
            put(O, 4, c, j, w[j][c] + STEP * rate[j][c])
            new = w[j][c] + 4 * STEP * rate[j][c] + at(G2, 3, c, j)
            put(U, 6, c, j, new)
            packed = pack(5, 1, c, j, new, packed)
            new = w[j][c] + 2 * STEP * rate[j][c] + at(G1, 5, c, j)
            put(U, 5, c, j, new)
            packed = pack(5, 2, c, j, new, packed)
        if q == 0:
            send_halo(5, packed)
    w, rate = rates(U, 3, 4, 2)
    for j, c in each():
        put(O, 3, c, j, w[j][c] + STEP * rate[j][c])
    for slot, k in ((0, 4), (1, 7), (1, 5), (1, 4), (0, 3)):
        send_back(slot, k, O.at[k] if slot == 0 else U.at[k + 1])

    def ascend(k, b, i, targets, packed):
        w, rate = rates(U, k, b, i)
        for j, c in each():
            put(O, k, c, j, w[j][c] + STEP * rate[j][c])
            for point, factor, (right_side, index), place in targets:
                new = w[j][c] + factor * STEP * rate[j][c] + at(right_side, index, c, j)
                put(U, point, c, j, new)
                if place is not None:
                    packed = pack(b + 1, place, c, j, new, packed)
        return packed

    plan = (
        (
            5,
            (
                (8, 0, ((12, 8, (G3, 3), 0), (10, 4, (G2, 5), 1), (9, 2, (G1, 9), 2), (16, 16, (G4, 0), None))),
                (6, 1, ((7, 2, (G1, 7), 3),)),
                (5, 2, ()),
            ),
        ),
        (
            6,
            (
                (12, 0, ((14, 4, (G2, 7), 0), (13, 2, (G1, 13), 1))),
                (10, 1, ((11, 2, (G1, 11), 2),)),
                (9, 2, ()),
                (7, 3, ()),
            ),
        ),
        (7, ((14, 0, ((15, 2, (G1, 15), 0),)), (13, 1, ()), (11, 2, ()))),
        (8, ((15, 0, ()),)),
    )
    for b, fields in plan:
        wait_halo(b)
        packed = (blank, blank)
        for k, i, targets in fields:
            packed = ascend(k, b, i, targets, packed)
        if b + 1 < NB:
            send_halo(b + 1, packed)
        for k, i, targets in fields:
            send_back(0, k, O.at[k])
            for target in targets:
                send_back(1, target[0] - 1, U.at[target[0]])

    for b in range(NB):
        for copy in halo_copies(b):
            copy.wait_send()

    def finish(peer, c):
        @pl.when(peer != me)
        def _():
            forward(peer).wait_send()
            for slot in range(2):
                back(slot, peer, O.at[0]).wait_send()
                pltpu.make_async_remote_copy(
                    src_ref=O.at[0],
                    dst_ref=out.at[slot, :, rows_of(peer), :],
                    send_sem=ret_send.at[slot, peer],
                    recv_sem=ret_recv.at[slot, peer],
                    device_id={"tm": peer},
                    device_id_type=MESH,
                ).wait_recv()

        return c

    lax.fori_loop(0, NT, finish, 0)
    for slot in range(2):
        pltpu.make_async_copy(O.at[0], out.at[slot, :, own_rows, :], ret_local.at[slot]).wait()


def body(initial, forcing, guess):
    def field(n):
        return pltpu.VMEM((n, 2, ROWS, COLS), jnp.float32)

    scratch = [
        field(17),
        pltpu.VMEM((2, ROWS, COLS), jnp.float32),
        field(16),
        field(16),
        field(17),
        field(9),
        field(5),
        field(1),
        field(17),
        field(17),
        field(16),
        pltpu.VMEM((NB, 2, ROWS, 128), jnp.float32),
        pltpu.VMEM((NB, 2, ROWS, 128), jnp.float32),
    ]
    for _ in range(2):
        scratch += [pltpu.VMEM((2, n, 2, COLS), jnp.float32) for n in BATCH]
    dma = pltpu.SemaphoreType.DMA
    scratch += [dma((3,)), dma((NT,)), dma((NT,)), dma((NB, 4)), dma((NB, 4)), dma((2, NT)), dma((2, NT)), dma((2,))]
    spec = pl.BlockSpec(memory_space=pl.ANY)
    return pl.pallas_call(
        kernel,
        out_shape=jax.ShapeDtypeStruct((2, 2, 256, COLS), jnp.float32),
        in_specs=[spec] * 3,
        out_specs=spec,
        scratch_shapes=scratch,
        compiler_params=pltpu.CompilerParams(
            collective_id=0, has_side_effects=True, vmem_limit_bytes=48 * 1024 * 1024
        ),
        name="cycle",
    )(initial, forcing, guess)


def solution(mesh):
    in_specs = (P(None, "sx", "sy"), P(None, "sx", "sy"), P("tm", None, "sx", "sy"))
    out_specs = P("tm", None, "sx", "sy")
    return jax.shard_map(body, mesh=mesh, in_specs=in_specs, out_specs=out_specs, check_vma=False)
```

```python
import jax
import jax.numpy as jnp
from jax import lax
from jax.experimental import pallas as pl
from jax.experimental.pallas import tpu as pltpu
from jax.sharding import PartitionSpec as P

VISCOSITY = 0.5
COURANT = 0.7
MESH = pl.DeviceIdType.MESH
NT = 16
BLOCK_ROWS, BLOCK_COLS = 256, 512
ROWS, COLS = 32, 256
HALO = 4
HELD_ROWS, HELD_COLS = ROWS + 2 * HALO, COLS + 128
TILES = HELD_COLS // 128
STEP = COURANT / (NT * (2.0 + 4.0 * VISCOSITY))
BATCH = (2, 8, 7, 2, 2)
NB = len(BATCH)
UP, DOWN, RIGHT, LEFT, UP_RIGHT, DOWN_RIGHT, UP_LEFT, DOWN_LEFT = range(8)


def kernel(initial, forcing, guess, out, *scratch):
    (S, F, R0, T1, G1, G2, G3, G4, Fx, U, prior, final, col_out, col_in, corner_in, wide) = scratch[:16]
    (edge_row_out, edge_row_in, edge_col_out, edge_col_in) = scratch[16:20]
    row_out = scratch[20 : 20 + NB]
    row_in = scratch[20 + NB : 20 + 2 * NB]
    (local_sem, fwd_send, fwd_recv, halo_send, halo_recv, ret_send, ret_recv, ret_local, edge_send, edge_recv, final_sem) = (
        scratch[20 + 2 * NB :]
    )

    me = lax.axis_index("tm")
    sx = lax.axis_index("sx")
    sy = lax.axis_index("sy")
    xl = me // 8
    z = lax.rem(me, 8)

    def mirrored(i):
        return jnp.where(sx == 0, i, 7 - i)

    zz = mirrored(z)

    def beside(vertical, horizontal):
        if vertical == 0:
            nz, nsx = z, sx
        elif vertical == 1:
            nz, nsx = jnp.where(zz < 7, mirrored(zz + 1), z), jnp.where(zz < 7, sx, 1 - sx)
        else:
            nz, nsx = jnp.where(zz > 0, mirrored(zz - 1), z), jnp.where(zz > 0, sx, 1 - sx)
        if horizontal == 0:
            nx, nsy = xl, sy
        elif horizontal == 1:
            nx, nsy = 1 - xl, jnp.where(xl == 0, sy, lax.rem(sy + 1, 8))
        else:
            nx, nsy = 1 - xl, jnp.where(xl == 1, sy, lax.rem(sy + 7, 8))
        return {"tm": nx * 8 + nz, "sx": nsx, "sy": nsy}

    sides = [beside(*v) for v in ((1, 0), (-1, 0), (0, 1), (0, -1), (1, 1), (-1, 1), (1, -1), (-1, -1))]
    block_sides = [{"sx": 1 - sx}, {"sy": lax.rem(sy + 1, 8)}, {"sy": lax.rem(sy + 7, 8)}]

    def rows_of(t):
        return pl.ds(pl.multiple_of(mirrored(lax.rem(t, 8)) * ROWS, ROWS), ROWS)

    def cols_of(t):
        return pl.ds(pl.multiple_of((t // 8) * COLS, COLS), COLS)

    own_rows, own_cols = rows_of(me), cols_of(me)

    def prior_rows(t):
        return pl.ds(pl.multiple_of(8 + mirrored(lax.rem(t, 8)) * ROWS, 8), ROWS)

    def core(ref, k):
        return ref.at[k, :, 0:ROWS, 0:COLS]

    barrier = pltpu.get_barrier_semaphore()

    def greet(d, c):
        pl.semaphore_signal(barrier, inc=1, device_id={"tm": lax.rem(me + d, NT)}, device_id_type=MESH)
        return c

    lax.fori_loop(1, NT, greet, 0)
    for side in sides + block_sides:
        pl.semaphore_signal(barrier, inc=1, device_id=side, device_id_type=MESH)

    stage_in = [
        pltpu.make_async_copy(initial.at[:, own_rows, own_cols], core(S, 0), local_sem.at[0]),
        pltpu.make_async_copy(forcing.at[:, own_rows, own_cols], core(F, 0), local_sem.at[1]),
        pltpu.make_async_copy(guess.at[0, :, own_rows, own_cols], core(S, me + 1), local_sem.at[2]),
    ]
    for copy in stage_in:
        copy.start()
    pl.semaphore_wait(barrier, NT - 1 + 8 + 3)

    def forward(peer):
        return pltpu.make_async_remote_copy(
            src_ref=guess.at[0, :, rows_of(peer), cols_of(peer)],
            dst_ref=core(S, me + 1),
            send_sem=fwd_send.at[peer],
            recv_sem=fwd_recv.at[me],
            device_id={"tm": peer},
            device_id_type=MESH,
        )

    def forwarded(peer):
        return pltpu.make_async_remote_copy(
            src_ref=guess.at[0, :, own_rows, own_cols],
            dst_ref=core(S, peer + 1),
            send_sem=fwd_send.at[peer],
            recv_sem=fwd_recv.at[peer],
            device_id={"tm": peer},
            device_id_type=MESH,
        )

    def start_forward(d, c):
        forward(lax.rem(me + d, NT)).start()
        return c

    lax.fori_loop(1, NT, start_forward, 0)

    lane = lax.broadcasted_iota(jnp.int32, (HELD_ROWS, 128), 1)
    core_lane = lax.broadcasted_iota(jnp.int32, (ROWS, 128), 1)
    blank = jnp.zeros((ROWS, 128), jnp.float32)

    def lanes(j):
        return slice(128 * j, 128 * (j + 1))

    def halo_copies(b):
        parts = (
            (UP, row_out[b].at[0], row_in[b].at[1]),
            (DOWN, row_out[b].at[1], row_in[b].at[0]),
            (RIGHT, col_out.at[b, 0], col_in.at[b, 0]),
            (LEFT, col_out.at[b, 1], col_in.at[b, 1]),
            (DOWN_RIGHT, col_out.at[b, 0, 0:8], corner_in.at[b, 0, 0]),
            (UP_RIGHT, col_out.at[b, 0, ROWS - 8 : ROWS], corner_in.at[b, 0, 1]),
            (DOWN_LEFT, col_out.at[b, 1, 0:8], corner_in.at[b, 1, 0]),
            (UP_LEFT, col_out.at[b, 1, ROWS - 8 : ROWS], corner_in.at[b, 1, 1]),
        )
        return [
            pltpu.make_async_remote_copy(
                src_ref=src,
                dst_ref=dst,
                send_sem=halo_send.at[b, i],
                recv_sem=halo_recv.at[b, i],
                device_id=sides[to],
                device_id_type=MESH,
            )
            for i, (to, src, dst) in enumerate(parts)
        ]

    def pack(ref, k, b, i, packed):
        last, first = packed
        for c in range(2):
            row_out[b][0, i, c] = ref[k, c, ROWS - HALO : ROWS, 0:COLS]
            row_out[b][1, i, c] = ref[k, c, 0:HALO, 0:COLS]
            index = 8 * i + HALO * c
            mine = jnp.logical_and(core_lane >= index, core_lane < index + HALO)
            tail = ref[k, c, 0:ROWS, COLS - 128 : COLS]
            head = ref[k, c, 0:ROWS, 0:128]
            last = jnp.where(mine, pltpu.roll(tail, lax.rem(index + HALO, 128), 1), last)
            first = jnp.where(mine, pltpu.roll(head, index, 1), first)
        return last, first

    def send_halo(b, packed):
        col_out[b, 0] = packed[0]
        col_out[b, 1] = packed[1]
        for copy in halo_copies(b):
            copy.start()

    def wait_halo(b):
        for copy in halo_copies(b):
            copy.wait_recv()
        for side in range(2):
            wide[b, side, 0:ROWS] = col_in[b, side]
            wide[b, side, ROWS : ROWS + HALO] = corner_in[b, side, 0, 0:HALO]
            wide[b, side, ROWS + HALO : HELD_ROWS] = corner_in[b, side, 1, HALO:8]

    def unpack(ref, k, b, i):
        for c in range(2):
            ref[k, c, ROWS : ROWS + HALO, 0:COLS] = row_in[b][0, i, c]
            ref[k, c, ROWS + HALO : HELD_ROWS, 0:COLS] = row_in[b][1, i, c]
            index = 8 * i + HALO * c
            after = pltpu.roll(wide[b, 1], lax.rem(128 - index, 128), 1)
            before = pltpu.roll(wide[b, 0], lax.rem(256 - HALO - index, 128), 1)
            ref[k, c, :, COLS:HELD_COLS] = jnp.where(lane < 64, after, before)

    def slopes(first, second):
        return (
            0.5 + jnp.maximum(first, 0.0),
            0.5 - jnp.minimum(first, 0.0),
            0.5 + jnp.maximum(second, 0.0),
            0.5 - jnp.minimum(second, 0.0),
        )

    def rates(ref, k):
        w = [[ref[k, c, :, lanes(j)] for c in range(2)] for j in range(TILES)]
        up = [[pltpu.roll(w[j][c], 1, 1) for c in range(2)] for j in range(TILES)]
        down = [[pltpu.roll(w[j][c], 127, 1) for c in range(2)] for j in range(TILES)]
        result = []
        for j in range(TILES):
            west_w, east_w, south_w, north_w = slopes(*w[j])
            pair = []
            for c in range(2):
                x = w[j][c]
                west = pltpu.roll(x, 1, 0)
                east = pltpu.roll(x, HELD_ROWS - 1, 0)
                south = jnp.where(lane == 0, up[j - 1][c], up[j][c])
                north = jnp.where(lane == 127, down[(j + 1) % TILES][c], down[j][c])
                pair.append(
                    west_w * (west - x)
                    + east_w * (east - x)
                    + south_w * (south - x)
                    + north_w * (north - x)
                    + F[0, c, :, lanes(j)]
                )
            result.append(pair)
        return w, result

    def each():
        return [(j, c) for j in range(TILES) for c in range(2)]

    def at(ref, k, c, j):
        return ref[k, c, :, lanes(j)]

    def put(ref, k, c, j, value):
        ref[k, c, :, lanes(j)] = value

    def back(slot, k):
        if slot == 0:
            dst, to = out.at[1, :, own_rows, own_cols], k - 1
        else:
            dst, to = prior.at[:, prior_rows(me), own_cols], k
        src = core(U, k)
        remote = pltpu.make_async_remote_copy(
            src_ref=src,
            dst_ref=dst,
            send_sem=ret_send.at[slot, k],
            recv_sem=ret_recv.at[slot, me],
            device_id={"tm": to},
            device_id_type=MESH,
        )
        return to, remote, pltpu.make_async_copy(src, dst, ret_local.at[slot])

    def send_back(slot, k):
        to, remote, local = back(slot, k)

        @pl.when(me == to)
        def _():
            local.start()

        @pl.when(me != to)
        def _():
            remote.start()

    for copy in stage_in:
        copy.wait()
    packed = pack(S, 0, 0, 0, (blank, blank))
    send_halo(0, pack(F, 0, 0, 1, packed))

    def arrive(first, b):
        def one(i, packed):
            k = first + i

            @pl.when(k - 1 != me)
            def _():
                forwarded(k - 1).wait_recv()

            return pack(S, k, b, i, packed)

        return one

    send_halo(1, lax.fori_loop(0, 8, arrive(1, 1), (blank, blank)))
    send_halo(2, lax.fori_loop(0, 7, arrive(9, 2), (blank, blank)))

    @pl.when(me != NT - 1)
    def _():
        forwarded(NT - 1).wait_recv()

    for c in range(2):
        S[NT, c, ROWS:HELD_ROWS, :] = jnp.zeros((HELD_ROWS - ROWS, HELD_COLS), jnp.float32)
        S[NT, c, 0:ROWS, COLS:HELD_COLS] = jnp.zeros((ROWS, 128), jnp.float32)

    wait_halo(0)
    unpack(S, 0, 0, 0)
    unpack(F, 0, 0, 1)

    def coarse_rhs(g, point, image, base):
        residual = g - (point - image)
        return residual + point - base

    def descend(half):
        start = 8 * half

        def fine(k, carry):
            w, rate = rates(S, k)
            for j, c in each():
                put(R0, k, c, j, rate[j][c])
                put(T1, k, c, j, w[j][c] + STEP * rate[j][c])
            w, rate = rates(T1, k)
            for j, c in each():
                base = at(S, k, c, j) + 2 * STEP * at(R0, k, c, j)
                g = coarse_rhs(0.0, at(S, k + 1, c, j), w[j][c] + STEP * rate[j][c], base)
                put(G1, k + 1, c, j, g)
                put(Fx, k + 1, c, j, base + g)
            return carry

        lax.fori_loop(start, start + 8, fine, 0)

        def second(m, carry):
            k = 2 * m
            w, rate = rates(Fx, k + 1)
            for j, c in each():
                base = at(S, k, c, j) + 4 * STEP * at(R0, k, c, j)
                g = coarse_rhs(at(G1, k + 2, c, j), at(S, k + 2, c, j), w[j][c] + 2 * STEP * rate[j][c], base)
                put(G2, m + 1, c, j, g)
                put(Fx, k + 2, c, j, base + g)
            return carry

        lax.fori_loop(start // 2, start // 2 + 4, second, 0)

        for q in (2 * half, 2 * half + 1):
            k = 4 * q
            w, rate = rates(Fx, k + 2)
            for j, c in each():
                base = at(S, k, c, j) + 8 * STEP * at(R0, k, c, j)
                g = coarse_rhs(at(G2, 2 * q + 2, c, j), at(S, k + 4, c, j), w[j][c] + 4 * STEP * rate[j][c], base)
                put(G3, q + 1, c, j, g)
                if q % 2 == 0:
                    put(Fx, k + 4, c, j, base + g)
                if q == 0:
                    put(U, 1, c, j, at(Fx, 1, c, j))
                    put(U, 2, c, j, w[j][c])
                    put(U, 3, c, j, w[j][c] + 2 * STEP * rate[j][c] + at(G1, 3, c, j))
                    put(U, 4, c, j, base + g)

    def exchange(b, fields):
        packed = (blank, blank)
        for i, (ref, k) in enumerate(fields):
            packed = pack(ref, k, b, i, packed)
        send_halo(b, packed)
        wait_halo(b)
        for i, (ref, k) in enumerate(fields):
            unpack(ref, k, b, i)

    def ascend(k, targets):
        w, rate = rates(U, k)
        for j, c in each():
            for point, factor, right_side, index in targets:
                put(U, point, c, j, w[j][c] + factor * STEP * rate[j][c] + at(right_side, index, c, j))

    def coarsest(k):
        w, rate = rates(Fx, k + 4)
        for j, c in each():
            base = at(S, k, c, j) + 16 * STEP * at(R0, k, c, j)
            index = (k + 8) // 4
            g = coarse_rhs(at(G3, index, c, j), at(S, k + 8, c, j), w[j][c] + 8 * STEP * rate[j][c], base)
            if k == 0:
                put(U, 8, c, j, base + g)
                put(U, 5, c, j, w[j][c] + 2 * STEP * rate[j][c] + at(G1, 5, c, j))
                put(U, 6, c, j, w[j][c] + 4 * STEP * rate[j][c] + at(G2, 3, c, j))
            else:
                put(G4, 0, c, j, g)

    def return_points(first):
        def one(d, carry):
            k = first + lax.rem(z + d, 8)
            send_back(0, k)

            @pl.when(k < NT)
            def _():
                send_back(1, k)

            return carry

        lax.fori_loop(0, 8, one, 0)

    def halos_of(first, b, n):
        wait_halo(b)

        def one(i, carry):
            unpack(S, first + i, b, i)
            return carry

        lax.fori_loop(0, n, one, 0)

    halos_of(1, 1, 8)
    descend(0)
    exchange(3, ((Fx, 4), (G3, 2)))
    coarsest(0)
    ascend(6, ((7, 2, G1, 7),))
    return_points(1)

    halos_of(9, 2, 7)
    descend(1)
    exchange(4, ((Fx, 12), (G3, 3)))
    coarsest(8)
    ascend(8, ((9, 2, G1, 9), (10, 4, G2, 5), (12, 8, G3, 3), (16, 16, G4, 0)))
    ascend(10, ((11, 2, G1, 11),))
    ascend(12, ((13, 2, G1, 13), (14, 4, G2, 7)))
    ascend(14, ((15, 2, G1, 15),))
    return_points(9)

    @pl.when(me == 0)
    def _():
        copy = pltpu.make_async_copy(initial, prior.at[:, 8 : 8 + BLOCK_ROWS, :], ret_local.at[1])
        copy.start()
        copy.wait()

    def settle(slot):
        def one(peer, c):
            @pl.when(peer != me)
            def _():
                if slot == 0:
                    dst = out.at[1, :, rows_of(peer), cols_of(peer)]
                else:
                    dst = prior.at[:, prior_rows(peer), cols_of(peer)]
                pltpu.make_async_remote_copy(
                    src_ref=core(U, 1),
                    dst_ref=dst,
                    send_sem=ret_send.at[slot, 1],
                    recv_sem=ret_recv.at[slot, peer],
                    device_id={"tm": peer},
                    device_id_type=MESH,
                ).wait_recv()

            return c

        lax.fori_loop(0, NT, one, 0)
        back(slot, 1)[2].wait()

    @pl.when(me != 0)
    def _():
        settle(1)

    def edge_pack(g, packed):
        last, first = packed
        rows = pl.ds(pl.multiple_of(8 + g * ROWS, 8), ROWS)
        for c in range(2):
            index = 2 * g + c
            tail = prior[c, rows, BLOCK_COLS - 128 : BLOCK_COLS]
            head = prior[c, rows, 0:128]
            last = jnp.where(core_lane == index, pltpu.roll(tail, index + 1, 1), last)
            first = jnp.where(core_lane == index, pltpu.roll(head, index, 1), first)
        return last, first

    packed = lax.fori_loop(0, 8, edge_pack, (blank, blank))
    edge_col_out[0], edge_col_out[1] = packed
    for c in range(2):
        edge_row_out[0, c : c + 1, :] = prior[c, 8 + BLOCK_ROWS - 1 : 8 + BLOCK_ROWS, :]
        edge_row_out[1, c : c + 1, :] = prior[c, 8:9, :]
    edges = [
        pltpu.make_async_remote_copy(
            src_ref=src.at[i],
            dst_ref=dst.at[i],
            send_sem=edge_send.at[n],
            recv_sem=edge_recv.at[n],
            device_id=block_sides[to],
            device_id_type=MESH,
        )
        for n, (to, src, dst, i) in enumerate(
            (
                (0, edge_row_out, edge_row_in, 0),
                (0, edge_row_out, edge_row_in, 1),
                (1, edge_col_out, edge_col_in, 0),
                (2, edge_col_out, edge_col_in, 1),
            )
        )
    ]
    for copy in edges:
        copy.start()
    for copy in edges:
        copy.wait_recv()
    for c in range(2):
        prior[c, 7:8, :] = edge_row_in[0, c : c + 1, :]
        prior[c, 8 + BLOCK_ROWS : 9 + BLOCK_ROWS, :] = edge_row_in[1, c : c + 1, :]

    def final_copy(g):
        rows = pl.ds(pl.multiple_of(g * ROWS, ROWS), ROWS)
        return pltpu.make_async_copy(final.at[:, rows, :], out.at[0, :, rows, :], final_sem.at[g])

    block_tiles = BLOCK_COLS // 128

    def last_step(g, carry):
        around = pl.ds(pl.multiple_of(g * ROWS, ROWS), ROWS + 16)
        rows = pl.ds(pl.multiple_of(g * ROWS, ROWS), ROWS)
        y = [[prior[c, around, lanes(j)] for c in range(2)] for j in range(block_tiles)]
        w = [[y[j][c][8 : 8 + ROWS] for c in range(2)] for j in range(block_tiles)]
        up = [[pltpu.roll(w[j][c], 1, 1) for c in range(2)] for j in range(block_tiles)]
        down = [[pltpu.roll(w[j][c], 127, 1) for c in range(2)] for j in range(block_tiles)]
        before = [pltpu.roll(edge_col_in[0], lax.rem(128 - (2 * g + c), 128), 1) for c in range(2)]
        after = [pltpu.roll(edge_col_in[1], 127 - (2 * g + c), 1) for c in range(2)]
        for j in range(block_tiles):
            west_w, east_w, south_w, north_w = slopes(*w[j])
            for c in range(2):
                x = w[j][c]
                west = pltpu.roll(y[j][c], 1, 0)[8 : 8 + ROWS]
                east = pltpu.roll(y[j][c], ROWS + 15, 0)[8 : 8 + ROWS]
                south = jnp.where(core_lane == 0, up[j - 1][c] if j > 0 else before[c], up[j][c])
                north = jnp.where(core_lane == 127, down[j + 1][c] if j < block_tiles - 1 else after[c], down[j][c])
                rate = (
                    west_w * (west - x)
                    + east_w * (east - x)
                    + south_w * (south - x)
                    + north_w * (north - x)
                    + final[c, rows, lanes(j)]
                )
                final[c, rows, lanes(j)] = x + STEP * rate
        final_copy(g).start()
        return carry

    load = pltpu.make_async_copy(forcing, final, local_sem.at[3])
    load.start()
    load.wait()
    lax.fori_loop(0, 8, last_step, 0)

    for b in range(NB):
        for copy in halo_copies(b):
            copy.wait_send()
    for copy in edges:
        copy.wait_send()

    def finish(peer, c):
        @pl.when(peer != me)
        def _():
            forward(peer).wait_send()
            back(0, peer + 1)[1].wait_send()

            @pl.when(peer > 0)
            def _():
                back(1, peer)[1].wait_send()

        return c

    lax.fori_loop(0, NT, finish, 0)
    settle(0)

    def finish_final(g, c):
        final_copy(g).wait()
        return c

    lax.fori_loop(0, 8, finish_final, 0)


def body(initial, forcing, guess):
    f32 = jnp.float32

    def field(n):
        return pltpu.VMEM((n, 2, HELD_ROWS, HELD_COLS), f32)

    scratch = [field(n) for n in (17, 1, 16, 16, 17, 9, 5, 1, 17, 17)]
    scratch += [
        pltpu.VMEM((2, BLOCK_ROWS + 16, BLOCK_COLS), f32),
        pltpu.VMEM((2, BLOCK_ROWS, BLOCK_COLS), f32),
        pltpu.VMEM((NB, 2, ROWS, 128), f32),
        pltpu.VMEM((NB, 2, ROWS, 128), f32),
        pltpu.VMEM((NB, 2, 2, 8, 128), f32),
        pltpu.VMEM((NB, 2, HELD_ROWS, 128), f32),
        pltpu.VMEM((2, 2, BLOCK_COLS), f32),
        pltpu.VMEM((2, 2, BLOCK_COLS), f32),
        pltpu.VMEM((2, ROWS, 128), f32),
        pltpu.VMEM((2, ROWS, 128), f32),
    ]
    for _ in range(2):
        scratch += [pltpu.VMEM((2, n, 2, HALO, COLS), f32) for n in BATCH]
    dma = pltpu.SemaphoreType.DMA
    scratch += [dma((4,)), dma((NT,)), dma((NT,)), dma((NB, 8)), dma((NB, 8)), dma((2, NT + 1)), dma((2, NT)), dma((2,))]
    scratch += [dma((4,)), dma((4,)), dma((8,))]
    spec = pl.BlockSpec(memory_space=pltpu.HBM)
    return pl.pallas_call(
        kernel,
        out_shape=jax.ShapeDtypeStruct((2, 2, BLOCK_ROWS, BLOCK_COLS), f32),
        in_specs=[spec] * 3,
        out_specs=spec,
        scratch_shapes=scratch,
        compiler_params=pltpu.CompilerParams(
            collective_id=0, has_side_effects=True, vmem_limit_bytes=56 * 1024 * 1024
        ),
        name="cycle",
    )(initial, forcing, guess)


def solution(mesh):
    in_specs = (P(None, "sx", "sy"), P(None, "sx", "sy"), P("tm", None, "sx", "sy"))
    out_specs = P("tm", None, "sx", "sy")
    return jax.shard_map(body, mesh=mesh, in_specs=in_specs, out_specs=out_specs, check_vma=False)
```

```python
import jax
import jax.numpy as jnp
from jax import lax
from jax.experimental import pallas as pl
from jax.experimental.pallas import tpu as pltpu
from jax.sharding import PartitionSpec as P

VISCOSITY = 0.5
COURANT = 0.7
MESH = pl.DeviceIdType.MESH
NT = 16
BLOCK_ROWS, BLOCK_COLS = 256, 512
ROWS, COLS = 32, 256
HALO = 4
HELD_ROWS, HELD_COLS = ROWS + 2 * HALO, COLS + 128
TILES = HELD_COLS // 128
STEP = COURANT / (NT * (2.0 + 4.0 * VISCOSITY))
BATCH = (2, 8, 7, 2, 2)
NB = len(BATCH)
UP, DOWN, RIGHT, LEFT, UP_RIGHT, DOWN_RIGHT, UP_LEFT, DOWN_LEFT = range(8)


def kernel(initial, forcing, guess, out, *scratch):
    (S, F, R0, T1, G1, G2, G3, G4, Fx, U, prior, final, col_out, col_in, corner_in, wide) = scratch[:16]
    (edge_row_out, edge_row_in, edge_col_out, edge_col_in) = scratch[16:20]
    row_out = scratch[20 : 20 + NB]
    row_in = scratch[20 + NB : 20 + 2 * NB]
    (local_sem, fwd_send, fwd_recv, halo_send, halo_recv, ret_send, ret_recv, ret_local, hand_send, edge_send, edge_recv, final_sem) = (
        scratch[20 + 2 * NB :]
    )

    me = lax.axis_index("tm")
    sx = lax.axis_index("sx")
    sy = lax.axis_index("sy")
    xl = me // 8
    z = lax.rem(me, 8)

    def mirrored(i):
        return jnp.where(sx == 0, i, 7 - i)

    zz = mirrored(z)

    def beside(vertical, horizontal):
        if vertical == 0:
            nz, nsx = z, sx
        elif vertical == 1:
            nz, nsx = jnp.where(zz < 7, mirrored(zz + 1), z), jnp.where(zz < 7, sx, 1 - sx)
        else:
            nz, nsx = jnp.where(zz > 0, mirrored(zz - 1), z), jnp.where(zz > 0, sx, 1 - sx)
        if horizontal == 0:
            nx, nsy = xl, sy
        elif horizontal == 1:
            nx, nsy = 1 - xl, jnp.where(xl == 0, sy, lax.rem(sy + 1, 8))
        else:
            nx, nsy = 1 - xl, jnp.where(xl == 1, sy, lax.rem(sy + 7, 8))
        return {"tm": nx * 8 + nz, "sx": nsx, "sy": nsy}

    sides = [beside(*v) for v in ((1, 0), (-1, 0), (0, 1), (0, -1), (1, 1), (-1, 1), (1, -1), (-1, -1))]
    block_sides = [{"sx": 1 - sx}, {"sy": lax.rem(sy + 1, 8)}, {"sy": lax.rem(sy + 7, 8)}]

    def rows_of(t):
        return pl.ds(pl.multiple_of(mirrored(lax.rem(t, 8)) * ROWS, ROWS), ROWS)

    def cols_of(t):
        return pl.ds(pl.multiple_of((t // 8) * COLS, COLS), COLS)

    own_rows, own_cols = rows_of(me), cols_of(me)

    def prior_rows(t):
        return pl.ds(pl.multiple_of(8 + mirrored(lax.rem(t, 8)) * ROWS, 8), ROWS)

    def core(ref, k):
        return ref.at[k, :, 0:ROWS, 0:COLS]

    barrier = pltpu.get_barrier_semaphore()

    def greet(d, c):
        pl.semaphore_signal(barrier, inc=1, device_id={"tm": lax.rem(me + d, NT)}, device_id_type=MESH)
        return c

    lax.fori_loop(1, NT, greet, 0)
    for side in sides + block_sides:
        pl.semaphore_signal(barrier, inc=1, device_id=side, device_id_type=MESH)

    stage_in = [
        pltpu.make_async_copy(initial.at[:, own_rows, own_cols], core(S, 0), local_sem.at[0]),
        pltpu.make_async_copy(forcing.at[:, own_rows, own_cols], core(F, 0), local_sem.at[1]),
        pltpu.make_async_copy(guess.at[0, :, own_rows, own_cols], core(S, me + 1), local_sem.at[2]),
    ]
    for copy in stage_in:
        copy.start()
    pl.semaphore_wait(barrier, NT - 1 + 8 + 3)

    def forward(peer):
        return pltpu.make_async_remote_copy(
            src_ref=guess.at[0, :, rows_of(peer), cols_of(peer)],
            dst_ref=core(S, me + 1),
            send_sem=fwd_send.at[peer],
            recv_sem=fwd_recv.at[me],
            device_id={"tm": peer},
            device_id_type=MESH,
        )

    def forwarded(peer):
        return pltpu.make_async_remote_copy(
            src_ref=guess.at[0, :, own_rows, own_cols],
            dst_ref=core(S, peer + 1),
            send_sem=fwd_send.at[peer],
            recv_sem=fwd_recv.at[peer],
            device_id={"tm": peer},
            device_id_type=MESH,
        )

    def start_forward(d, c):
        forward(lax.rem(me + d, NT)).start()
        return c

    lax.fori_loop(1, NT, start_forward, 0)
    load = pltpu.make_async_copy(forcing, final, local_sem.at[3])
    load.start()

    lane = lax.broadcasted_iota(jnp.int32, (HELD_ROWS, 128), 1)
    core_lane = lax.broadcasted_iota(jnp.int32, (ROWS, 128), 1)
    blank = jnp.zeros((ROWS, 128), jnp.float32)

    def lanes(j):
        return slice(128 * j, 128 * (j + 1))

    def halo_copies(b):
        parts = (
            (UP, row_out[b].at[0], row_in[b].at[1]),
            (DOWN, row_out[b].at[1], row_in[b].at[0]),
            (RIGHT, col_out.at[b, 0], col_in.at[b, 0]),
            (LEFT, col_out.at[b, 1], col_in.at[b, 1]),
            (DOWN_RIGHT, col_out.at[b, 0, 0:8], corner_in.at[b, 0, 0]),
            (UP_RIGHT, col_out.at[b, 0, ROWS - 8 : ROWS], corner_in.at[b, 0, 1]),
            (DOWN_LEFT, col_out.at[b, 1, 0:8], corner_in.at[b, 1, 0]),
            (UP_LEFT, col_out.at[b, 1, ROWS - 8 : ROWS], corner_in.at[b, 1, 1]),
        )
        return [
            pltpu.make_async_remote_copy(
                src_ref=src,
                dst_ref=dst,
                send_sem=halo_send.at[b, i],
                recv_sem=halo_recv.at[b, i],
                device_id=sides[to],
                device_id_type=MESH,
            )
            for i, (to, src, dst) in enumerate(parts)
        ]

    def pack(ref, k, b, i, packed):
        last, first = packed
        for c in range(2):
            row_out[b][0, i, c] = ref[k, c, ROWS - HALO : ROWS, 0:COLS]
            row_out[b][1, i, c] = ref[k, c, 0:HALO, 0:COLS]
            index = 8 * i + HALO * c
            mine = jnp.logical_and(core_lane >= index, core_lane < index + HALO)
            tail = ref[k, c, 0:ROWS, COLS - 128 : COLS]
            head = ref[k, c, 0:ROWS, 0:128]
            last = jnp.where(mine, pltpu.roll(tail, lax.rem(index + HALO, 128), 1), last)
            first = jnp.where(mine, pltpu.roll(head, index, 1), first)
        return last, first

    def send_halo(b, packed):
        col_out[b, 0] = packed[0]
        col_out[b, 1] = packed[1]
        for copy in halo_copies(b):
            copy.start()

    def wait_halo(b):
        for copy in halo_copies(b):
            copy.wait_recv()
        for side in range(2):
            wide[b, side, 0:ROWS] = col_in[b, side]
            wide[b, side, ROWS : ROWS + HALO] = corner_in[b, side, 0, 0:HALO]
            wide[b, side, ROWS + HALO : HELD_ROWS] = corner_in[b, side, 1, HALO:8]

    def unpack(ref, k, b, i):
        for c in range(2):
            ref[k, c, ROWS : ROWS + HALO, 0:COLS] = row_in[b][0, i, c]
            ref[k, c, ROWS + HALO : HELD_ROWS, 0:COLS] = row_in[b][1, i, c]
            index = 8 * i + HALO * c
            after = pltpu.roll(wide[b, 1], lax.rem(128 - index, 128), 1)
            before = pltpu.roll(wide[b, 0], lax.rem(256 - HALO - index, 128), 1)
            ref[k, c, :, COLS:HELD_COLS] = jnp.where(lane < 64, after, before)

    def slopes(first, second):
        return (
            0.5 + jnp.maximum(first, 0.0),
            0.5 - jnp.minimum(first, 0.0),
            0.5 + jnp.maximum(second, 0.0),
            0.5 - jnp.minimum(second, 0.0),
        )

    def rates(ref, k):
        w = [[ref[k, c, :, lanes(j)] for c in range(2)] for j in range(TILES)]
        up = [[pltpu.roll(w[j][c], 1, 1) for c in range(2)] for j in range(TILES)]
        down = [[pltpu.roll(w[j][c], 127, 1) for c in range(2)] for j in range(TILES)]
        result = []
        for j in range(TILES):
            west_w, east_w, south_w, north_w = slopes(*w[j])
            pair = []
            for c in range(2):
                x = w[j][c]
                west = pltpu.roll(x, 1, 0)
                east = pltpu.roll(x, HELD_ROWS - 1, 0)
                south = jnp.where(lane == 0, up[j - 1][c], up[j][c])
                north = jnp.where(lane == 127, down[(j + 1) % TILES][c], down[j][c])
                pair.append(
                    west_w * (west - x)
                    + east_w * (east - x)
                    + south_w * (south - x)
                    + north_w * (north - x)
                    + F[0, c, :, lanes(j)]
                )
            result.append(pair)
        return w, result

    def each():
        return [(j, c) for j in range(TILES) for c in range(2)]

    def at(ref, k, c, j):
        return ref[k, c, :, lanes(j)]

    def put(ref, k, c, j, value):
        ref[k, c, :, lanes(j)] = value

    def landing(slot, t):
        if slot == 0:
            return out.at[1, :, rows_of(t), cols_of(t)]
        return prior.at[:, prior_rows(t), cols_of(t)]

    def first_slot(k, t):
        away = lax.rem(lax.rem(t, 8) - lax.rem(k - 1, 8) + 8, 8)
        return jnp.where(jnp.logical_and(k < NT, jnp.logical_and(away >= 1, away <= 4)), 1, 0)

    def back(slot, k):
        return pltpu.make_async_remote_copy(
            src_ref=core(U, k),
            dst_ref=landing(slot, me),
            send_sem=ret_send.at[k],
            recv_sem=ret_recv.at[slot, me],
            device_id={"tm": k - 1 + slot},
            device_id_type=MESH,
        )

    def own(slot):
        return pltpu.make_async_copy(core(U, me + 1 - slot), landing(slot, me), ret_local.at[slot])

    def send_back(k):
        for slot in range(2):

            @pl.when(first_slot(k, me) == slot)
            def _(slot=slot):
                @pl.when(me == k - 1 + slot)
                def _():
                    own(slot).start()

                @pl.when(me != k - 1 + slot)
                def _():
                    back(slot, k).start()

    def hand_on(slot, t):
        return pltpu.make_async_remote_copy(
            src_ref=landing(slot, t),
            dst_ref=landing(1 - slot, t),
            send_sem=hand_send.at[slot, t],
            recv_sem=ret_recv.at[1 - slot, t],
            device_id={"tm": jnp.clip(me + 1 - 2 * slot, 0, NT - 1)},
            device_id_type=MESH,
        )

    def wait_landed(slot, t, local):
        if local:

            @pl.when(t == me)
            def _():
                own(slot).wait()

        @pl.when(t != me)
        def _():
            pltpu.make_async_remote_copy(
                src_ref=core(U, 1),
                dst_ref=landing(slot, t),
                send_sem=ret_send.at[1],
                recv_sem=ret_recv.at[slot, t],
                device_id={"tm": t},
                device_id_type=MESH,
            ).wait_recv()

    def near(slot, i):
        step = i // 2
        along = lax.rem(z + 8 - step, 8) if slot == 0 else lax.rem(z + step, 8)
        return lax.rem(i, 2) * 8 + along

    def far(slot, i):
        step = 1 + i // 2
        along = lax.rem(z + step, 8) if slot == 0 else lax.rem(z + 8 - step, 8)
        return lax.rem(i, 2) * 8 + along

    for copy in stage_in:
        copy.wait()
    packed = pack(S, 0, 0, 0, (blank, blank))
    send_halo(0, pack(F, 0, 0, 1, packed))

    def arrive(first, b):
        def one(i, packed):
            k = first + i

            @pl.when(k - 1 != me)
            def _():
                forwarded(k - 1).wait_recv()

            return pack(S, k, b, i, packed)

        return one

    send_halo(1, lax.fori_loop(0, 8, arrive(1, 1), (blank, blank)))
    send_halo(2, lax.fori_loop(0, 7, arrive(9, 2), (blank, blank)))

    @pl.when(me != NT - 1)
    def _():
        forwarded(NT - 1).wait_recv()

    for c in range(2):
        S[NT, c, ROWS:HELD_ROWS, :] = jnp.zeros((HELD_ROWS - ROWS, HELD_COLS), jnp.float32)
        S[NT, c, 0:ROWS, COLS:HELD_COLS] = jnp.zeros((ROWS, 128), jnp.float32)

    wait_halo(0)
    unpack(S, 0, 0, 0)
    unpack(F, 0, 0, 1)

    def coarse_rhs(g, point, image, base):
        residual = g - (point - image)
        return residual + point - base

    def descend(half):
        start = 8 * half

        def fine(k, carry):
            w, rate = rates(S, k)
            for j, c in each():
                put(R0, k, c, j, rate[j][c])
                put(T1, k, c, j, w[j][c] + STEP * rate[j][c])
            w, rate = rates(T1, k)
            for j, c in each():
                base = at(S, k, c, j) + 2 * STEP * at(R0, k, c, j)
                g = coarse_rhs(0.0, at(S, k + 1, c, j), w[j][c] + STEP * rate[j][c], base)
                put(G1, k + 1, c, j, g)
                put(Fx, k + 1, c, j, base + g)
            return carry

        lax.fori_loop(start, start + 8, fine, 0)

        def second(m, carry):
            k = 2 * m
            w, rate = rates(Fx, k + 1)
            for j, c in each():
                base = at(S, k, c, j) + 4 * STEP * at(R0, k, c, j)
                g = coarse_rhs(at(G1, k + 2, c, j), at(S, k + 2, c, j), w[j][c] + 2 * STEP * rate[j][c], base)
                put(G2, m + 1, c, j, g)
                put(Fx, k + 2, c, j, base + g)
            return carry

        lax.fori_loop(start // 2, start // 2 + 4, second, 0)

        for q in (2 * half, 2 * half + 1):
            k = 4 * q
            w, rate = rates(Fx, k + 2)
            for j, c in each():
                base = at(S, k, c, j) + 8 * STEP * at(R0, k, c, j)
                g = coarse_rhs(at(G2, 2 * q + 2, c, j), at(S, k + 4, c, j), w[j][c] + 4 * STEP * rate[j][c], base)
                put(G3, q + 1, c, j, g)
                if q % 2 == 0:
                    put(Fx, k + 4, c, j, base + g)
                if q == 0:
                    put(U, 1, c, j, at(Fx, 1, c, j))
                    put(U, 2, c, j, w[j][c])
                    put(U, 3, c, j, w[j][c] + 2 * STEP * rate[j][c] + at(G1, 3, c, j))
                    put(U, 4, c, j, base + g)

    def exchange(b, fields):
        packed = (blank, blank)
        for i, (ref, k) in enumerate(fields):
            packed = pack(ref, k, b, i, packed)
        send_halo(b, packed)

    def exchanged(b, fields):
        wait_halo(b)
        for i, (ref, k) in enumerate(fields):
            unpack(ref, k, b, i)

    def ascend(k, targets):
        w, rate = rates(U, k)
        for j, c in each():
            for point, factor, right_side, index in targets:
                put(U, point, c, j, w[j][c] + factor * STEP * rate[j][c] + at(right_side, index, c, j))

    def coarsest(k):
        w, rate = rates(Fx, k + 4)
        for j, c in each():
            base = at(S, k, c, j) + 16 * STEP * at(R0, k, c, j)
            index = (k + 8) // 4
            g = coarse_rhs(at(G3, index, c, j), at(S, k + 8, c, j), w[j][c] + 8 * STEP * rate[j][c], base)
            if k == 0:
                put(U, 8, c, j, base + g)
                put(U, 5, c, j, w[j][c] + 2 * STEP * rate[j][c] + at(G1, 5, c, j))
                put(U, 6, c, j, w[j][c] + 4 * STEP * rate[j][c] + at(G2, 3, c, j))
            else:
                put(G4, 0, c, j, g)

    def return_points(first):
        def one(d, carry):
            k = first + lax.rem(z + d, 8)
            send_back(k)
            return carry

        lax.fori_loop(0, 8, one, 0)

    def halos_of(first, b, n):
        wait_halo(b)

        def one(i, carry):
            unpack(S, first + i, b, i)
            return carry

        lax.fori_loop(0, n, one, 0)

    halos_of(1, 1, 8)
    descend(0)
    fields_a = ((Fx, 4), (G3, 2))
    fields_b = ((Fx, 12), (G3, 3))
    exchange(3, fields_a)
    halos_of(9, 2, 7)
    descend(1)
    exchange(4, fields_b)
    exchanged(3, fields_a)
    coarsest(0)
    ascend(6, ((7, 2, G1, 7),))
    return_points(1)
    exchanged(4, fields_b)
    coarsest(8)
    ascend(8, ((9, 2, G1, 9), (10, 4, G2, 5), (12, 8, G3, 3), (16, 16, G4, 0)))
    ascend(10, ((11, 2, G1, 11),))
    ascend(12, ((13, 2, G1, 13), (14, 4, G2, 7)))
    ascend(14, ((15, 2, G1, 15),))
    return_points(9)

    def pass_on(i, carry):
        @pl.when(me < NT - 1)
        def _():
            wait_landed(0, near(0, i), True)
            hand_on(0, near(0, i)).start()

        @pl.when(me > 0)
        def _():
            wait_landed(1, near(1, i), True)
            hand_on(1, near(1, i)).start()

        return carry

    lax.fori_loop(0, 8, pass_on, 0)

    @pl.when(me == 0)
    def _():
        copy = pltpu.make_async_copy(initial, prior.at[:, 8 : 8 + BLOCK_ROWS, :], ret_local.at[1])
        copy.start()
        copy.wait()

    def rest(slot):
        def one(i, carry):
            wait_landed(slot, far(slot, i), False)
            return carry

        lax.fori_loop(0, 8, one, 0)

    @pl.when(me > 0)
    def _():
        rest(1)

    def edge_pack(g, packed):
        last, first = packed
        rows = pl.ds(pl.multiple_of(8 + g * ROWS, 8), ROWS)
        for c in range(2):
            index = 2 * g + c
            tail = prior[c, rows, BLOCK_COLS - 128 : BLOCK_COLS]
            head = prior[c, rows, 0:128]
            last = jnp.where(core_lane == index, pltpu.roll(tail, index + 1, 1), last)
            first = jnp.where(core_lane == index, pltpu.roll(head, index, 1), first)
        return last, first

    packed = lax.fori_loop(0, 8, edge_pack, (blank, blank))
    edge_col_out[0], edge_col_out[1] = packed
    for c in range(2):
        edge_row_out[0, c : c + 1, :] = prior[c, 8 + BLOCK_ROWS - 1 : 8 + BLOCK_ROWS, :]
        edge_row_out[1, c : c + 1, :] = prior[c, 8:9, :]
    edges = [
        pltpu.make_async_remote_copy(
            src_ref=src.at[i],
            dst_ref=dst.at[i],
            send_sem=edge_send.at[n],
            recv_sem=edge_recv.at[n],
            device_id=block_sides[to],
            device_id_type=MESH,
        )
        for n, (to, src, dst, i) in enumerate(
            (
                (0, edge_row_out, edge_row_in, 0),
                (0, edge_row_out, edge_row_in, 1),
                (1, edge_col_out, edge_col_in, 0),
                (2, edge_col_out, edge_col_in, 1),
            )
        )
    ]
    for copy in edges:
        copy.start()
    for copy in edges:
        copy.wait_recv()
    for c in range(2):
        prior[c, 7:8, :] = edge_row_in[0, c : c + 1, :]
        prior[c, 8 + BLOCK_ROWS : 9 + BLOCK_ROWS, :] = edge_row_in[1, c : c + 1, :]

    def final_copy(g):
        rows = pl.ds(pl.multiple_of(g * ROWS, ROWS), ROWS)
        return pltpu.make_async_copy(final.at[:, rows, :], out.at[0, :, rows, :], final_sem.at[g])

    block_tiles = BLOCK_COLS // 128

    def last_step(g, carry):
        around = pl.ds(pl.multiple_of(g * ROWS, ROWS), ROWS + 16)
        rows = pl.ds(pl.multiple_of(g * ROWS, ROWS), ROWS)
        y = [[prior[c, around, lanes(j)] for c in range(2)] for j in range(block_tiles)]
        w = [[y[j][c][8 : 8 + ROWS] for c in range(2)] for j in range(block_tiles)]
        up = [[pltpu.roll(w[j][c], 1, 1) for c in range(2)] for j in range(block_tiles)]
        down = [[pltpu.roll(w[j][c], 127, 1) for c in range(2)] for j in range(block_tiles)]
        before = [pltpu.roll(edge_col_in[0], lax.rem(128 - (2 * g + c), 128), 1) for c in range(2)]
        after = [pltpu.roll(edge_col_in[1], 127 - (2 * g + c), 1) for c in range(2)]
        for j in range(block_tiles):
            west_w, east_w, south_w, north_w = slopes(*w[j])
            for c in range(2):
                x = w[j][c]
                west = pltpu.roll(y[j][c], 1, 0)[8 : 8 + ROWS]
                east = pltpu.roll(y[j][c], ROWS + 15, 0)[8 : 8 + ROWS]
                south = jnp.where(core_lane == 0, up[j - 1][c] if j > 0 else before[c], up[j][c])
                north = jnp.where(core_lane == 127, down[j + 1][c] if j < block_tiles - 1 else after[c], down[j][c])
                rate = (
                    west_w * (west - x)
                    + east_w * (east - x)
                    + south_w * (south - x)
                    + north_w * (north - x)
                    + final[c, rows, lanes(j)]
                )
                final[c, rows, lanes(j)] = x + STEP * rate
        final_copy(g).start()
        return carry

    load.wait()
    lax.fori_loop(0, 8, last_step, 0)

    for b in range(NB):
        for copy in halo_copies(b):
            copy.wait_send()
    for copy in edges:
        copy.wait_send()

    def finish(i, c):
        @pl.when(i != me)
        def _():
            forward(i).wait_send()

        k = i + 1
        for slot in range(2):

            @pl.when(jnp.logical_and(first_slot(k, me) == slot, me != k - 1 + slot))
            def _(slot=slot):
                back(slot, k).wait_send()

        return c

    lax.fori_loop(0, NT, finish, 0)

    def finish_handed(i, c):
        @pl.when(me < NT - 1)
        def _():
            hand_on(0, near(0, i)).wait_send()

        @pl.when(me > 0)
        def _():
            hand_on(1, near(1, i)).wait_send()

        return c

    lax.fori_loop(0, 8, finish_handed, 0)

    @pl.when(me < NT - 1)
    def _():
        rest(0)

    @pl.when(me == NT - 1)
    def _():
        def one(t, c):
            wait_landed(0, t, True)
            return c

        lax.fori_loop(0, NT, one, 0)

    def finish_final(g, c):
        final_copy(g).wait()
        return c

    lax.fori_loop(0, 8, finish_final, 0)


def body(initial, forcing, guess):
    f32 = jnp.float32

    def field(n):
        return pltpu.VMEM((n, 2, HELD_ROWS, HELD_COLS), f32)

    scratch = [field(n) for n in (17, 1, 16, 16, 17, 9, 5, 1, 17, 17)]
    scratch += [
        pltpu.VMEM((2, BLOCK_ROWS + 16, BLOCK_COLS), f32),
        pltpu.VMEM((2, BLOCK_ROWS, BLOCK_COLS), f32),
        pltpu.VMEM((NB, 2, ROWS, 128), f32),
        pltpu.VMEM((NB, 2, ROWS, 128), f32),
        pltpu.VMEM((NB, 2, 2, 8, 128), f32),
        pltpu.VMEM((NB, 2, HELD_ROWS, 128), f32),
        pltpu.VMEM((2, 2, BLOCK_COLS), f32),
        pltpu.VMEM((2, 2, BLOCK_COLS), f32),
        pltpu.VMEM((2, ROWS, 128), f32),
        pltpu.VMEM((2, ROWS, 128), f32),
    ]
    for _ in range(2):
        scratch += [pltpu.VMEM((2, n, 2, HALO, COLS), f32) for n in BATCH]
    dma = pltpu.SemaphoreType.DMA
    scratch += [dma((4,)), dma((NT,)), dma((NT,)), dma((NB, 8)), dma((NB, 8)), dma((NT + 1,)), dma((2, NT)), dma((2,))]
    scratch += [dma((2, NT)), dma((4,)), dma((4,)), dma((8,))]
    spec = pl.BlockSpec(memory_space=pltpu.HBM)
    return pl.pallas_call(
        kernel,
        out_shape=jax.ShapeDtypeStruct((2, 2, BLOCK_ROWS, BLOCK_COLS), f32),
        in_specs=[spec] * 3,
        out_specs=pl.BlockSpec(memory_space=pl.ANY),
        scratch_shapes=scratch,
        compiler_params=pltpu.CompilerParams(
            collective_id=0, has_side_effects=True, vmem_limit_bytes=32 * 1024 * 1024
        ),
        name="cycle",
    )(initial, forcing, guess)


def solution(mesh):
    in_specs = (P(None, "sx", "sy"), P(None, "sx", "sy"), P("tm", None, "sx", "sy"))
    out_specs = P("tm", None, "sx", "sy")
    return jax.shard_map(body, mesh=mesh, in_specs=in_specs, out_specs=out_specs, check_vma=False)
```

```python
import jax
import jax.numpy as jnp
from jax import lax
from jax.experimental import pallas as pl
from jax.experimental.pallas import tpu as pltpu
from jax.sharding import PartitionSpec as P

VISCOSITY = 0.5
COURANT = 0.7
MESH = pl.DeviceIdType.MESH
NT = 16
BLOCK_ROWS, BLOCK_COLS = 256, 512
ROWS, COLS = 32, 256
HALO = 4
HELD_ROWS, HELD_COLS = ROWS + 2 * HALO, COLS + 128
TILES = HELD_COLS // 128
STEP = COURANT / (NT * (2.0 + 4.0 * VISCOSITY))
BATCH = (2, 8, 7, 2, 2)
NB = len(BATCH)
UP, DOWN, RIGHT, LEFT, UP_RIGHT, DOWN_RIGHT, UP_LEFT, DOWN_LEFT = range(8)


def kernel(initial, forcing, guess, out, *scratch):
    (S, F, R0, T1, G1, G2, G3, G4, Fx, U, prior, block_forcing, col_out, col_in, corner_in, wide) = scratch[:16]
    (edge_row_out, edge_row_in, edge_col_out, edge_col_in) = scratch[16:20]
    row_out = scratch[20 : 20 + NB]
    row_in = scratch[20 + NB : 20 + 2 * NB]
    (local_sem, fwd_send, fwd_recv, halo_send, halo_recv, ret_send, ret_recv, ret_local, hand_send, edge_send, edge_recv) = (
        scratch[20 + 2 * NB :]
    )

    me = lax.axis_index("tm")
    sx = lax.axis_index("sx")
    sy = lax.axis_index("sy")
    xl = me // 8
    z = lax.rem(me, 8)

    def mirrored(i):
        return jnp.where(sx == 0, i, 7 - i)

    zz = mirrored(z)

    def beside(vertical, horizontal):
        if vertical == 0:
            nz, nsx = z, sx
        elif vertical == 1:
            nz, nsx = jnp.where(zz < 7, mirrored(zz + 1), z), jnp.where(zz < 7, sx, 1 - sx)
        else:
            nz, nsx = jnp.where(zz > 0, mirrored(zz - 1), z), jnp.where(zz > 0, sx, 1 - sx)
        if horizontal == 0:
            nx, nsy = xl, sy
        elif horizontal == 1:
            nx, nsy = 1 - xl, jnp.where(xl == 0, sy, lax.rem(sy + 1, 8))
        else:
            nx, nsy = 1 - xl, jnp.where(xl == 1, sy, lax.rem(sy + 7, 8))
        return {"tm": nx * 8 + nz, "sx": nsx, "sy": nsy}

    sides = [beside(*v) for v in ((1, 0), (-1, 0), (0, 1), (0, -1), (1, 1), (-1, 1), (1, -1), (-1, -1))]
    block_sides = [{"sx": 1 - sx}, {"sy": lax.rem(sy + 1, 8)}, {"sy": lax.rem(sy + 7, 8)}]

    def rows_of(t):
        return pl.ds(pl.multiple_of(mirrored(lax.rem(t, 8)) * ROWS, ROWS), ROWS)

    def cols_of(t):
        return pl.ds(pl.multiple_of((t // 8) * COLS, COLS), COLS)

    own_rows, own_cols = rows_of(me), cols_of(me)

    def prior_rows(t):
        return pl.ds(pl.multiple_of(8 + mirrored(lax.rem(t, 8)) * ROWS, 8), ROWS)

    def core(ref, k):
        return ref.at[k, :, 0:ROWS, 0:COLS]

    barrier = pltpu.get_barrier_semaphore()

    def greet(d, c):
        pl.semaphore_signal(barrier, inc=1, device_id={"tm": lax.rem(me + d, NT)}, device_id_type=MESH)
        return c

    lax.fori_loop(1, NT, greet, 0)
    for side in sides + block_sides:
        pl.semaphore_signal(barrier, inc=1, device_id=side, device_id_type=MESH)

    stage_in = [
        pltpu.make_async_copy(initial.at[:, own_rows, own_cols], core(S, 0), local_sem.at[0]),
        pltpu.make_async_copy(forcing.at[:, own_rows, own_cols], core(F, 0), local_sem.at[1]),
        pltpu.make_async_copy(guess.at[0, :, own_rows, own_cols], core(S, me + 1), local_sem.at[2]),
    ]
    for copy in stage_in:
        copy.start()
    pl.semaphore_wait(barrier, NT - 1 + 8 + 3)

    def forward(peer):
        return pltpu.make_async_remote_copy(
            src_ref=guess.at[0, :, rows_of(peer), cols_of(peer)],
            dst_ref=core(S, me + 1),
            send_sem=fwd_send.at[peer],
            recv_sem=fwd_recv.at[me],
            device_id={"tm": peer},
            device_id_type=MESH,
        )

    def forwarded(peer):
        return pltpu.make_async_remote_copy(
            src_ref=guess.at[0, :, own_rows, own_cols],
            dst_ref=core(S, peer + 1),
            send_sem=fwd_send.at[peer],
            recv_sem=fwd_recv.at[peer],
            device_id={"tm": peer},
            device_id_type=MESH,
        )

    def start_forward(d, c):
        forward(lax.rem(me + d, NT)).start()
        return c

    lax.fori_loop(1, NT, start_forward, 0)
    load = pltpu.make_async_copy(forcing, block_forcing, local_sem.at[3])
    load.start()

    lane = lax.broadcasted_iota(jnp.int32, (HELD_ROWS, 128), 1)
    core_lane = lax.broadcasted_iota(jnp.int32, (ROWS, 128), 1)
    blank = jnp.zeros((ROWS, 128), jnp.float32)

    def lanes(j):
        return slice(128 * j, 128 * (j + 1))

    def halo_copies(b):
        parts = (
            (UP, row_out[b].at[0], row_in[b].at[1]),
            (DOWN, row_out[b].at[1], row_in[b].at[0]),
            (RIGHT, col_out.at[b, 0], col_in.at[b, 0]),
            (LEFT, col_out.at[b, 1], col_in.at[b, 1]),
            (DOWN_RIGHT, col_out.at[b, 0, 0:8], corner_in.at[b, 0, 0]),
            (UP_RIGHT, col_out.at[b, 0, ROWS - 8 : ROWS], corner_in.at[b, 0, 1]),
            (DOWN_LEFT, col_out.at[b, 1, 0:8], corner_in.at[b, 1, 0]),
            (UP_LEFT, col_out.at[b, 1, ROWS - 8 : ROWS], corner_in.at[b, 1, 1]),
        )
        return [
            pltpu.make_async_remote_copy(
                src_ref=src,
                dst_ref=dst,
                send_sem=halo_send.at[b, i],
                recv_sem=halo_recv.at[b, i],
                device_id=sides[to],
                device_id_type=MESH,
            )
            for i, (to, src, dst) in enumerate(parts)
        ]

    def pack(ref, k, b, i, packed):
        last, first = packed
        for c in range(2):
            row_out[b][0, i, c] = ref[k, c, ROWS - HALO : ROWS, 0:COLS]
            row_out[b][1, i, c] = ref[k, c, 0:HALO, 0:COLS]
            index = 8 * i + HALO * c
            mine = jnp.logical_and(core_lane >= index, core_lane < index + HALO)
            tail = ref[k, c, 0:ROWS, COLS - 128 : COLS]
            head = ref[k, c, 0:ROWS, 0:128]
            last = jnp.where(mine, pltpu.roll(tail, lax.rem(index + HALO, 128), 1), last)
            first = jnp.where(mine, pltpu.roll(head, index, 1), first)
        return last, first

    def send_halo(b, packed):
        col_out[b, 0] = packed[0]
        col_out[b, 1] = packed[1]
        for copy in halo_copies(b):
            copy.start()

    def wait_halo(b):
        for copy in halo_copies(b):
            copy.wait_recv()
        for side in range(2):
            wide[b, side, 0:ROWS] = col_in[b, side]
            wide[b, side, ROWS : ROWS + HALO] = corner_in[b, side, 0, 0:HALO]
            wide[b, side, ROWS + HALO : HELD_ROWS] = corner_in[b, side, 1, HALO:8]

    def unpack(ref, k, b, i):
        for c in range(2):
            ref[k, c, ROWS : ROWS + HALO, 0:COLS] = row_in[b][0, i, c]
            ref[k, c, ROWS + HALO : HELD_ROWS, 0:COLS] = row_in[b][1, i, c]
            index = 8 * i + HALO * c
            after = pltpu.roll(wide[b, 1], lax.rem(128 - index, 128), 1)
            before = pltpu.roll(wide[b, 0], lax.rem(256 - HALO - index, 128), 1)
            ref[k, c, :, COLS:HELD_COLS] = jnp.where(lane < 64, after, before)

    def slopes(first, second):
        return (
            0.5 + jnp.maximum(first, 0.0),
            0.5 - jnp.minimum(first, 0.0),
            0.5 + jnp.maximum(second, 0.0),
            0.5 - jnp.minimum(second, 0.0),
        )

    def rates(ref, k):
        w = [[ref[k, c, :, lanes(j)] for c in range(2)] for j in range(TILES)]
        up = [[pltpu.roll(w[j][c], 1, 1) for c in range(2)] for j in range(TILES)]
        down = [[pltpu.roll(w[j][c], 127, 1) for c in range(2)] for j in range(TILES)]
        result = []
        for j in range(TILES):
            west_w, east_w, south_w, north_w = slopes(*w[j])
            pair = []
            for c in range(2):
                x = w[j][c]
                west = pltpu.roll(x, 1, 0)
                east = pltpu.roll(x, HELD_ROWS - 1, 0)
                south = jnp.where(lane == 0, up[j - 1][c], up[j][c])
                north = jnp.where(lane == 127, down[(j + 1) % TILES][c], down[j][c])
                pair.append(
                    west_w * (west - x)
                    + east_w * (east - x)
                    + south_w * (south - x)
                    + north_w * (north - x)
                    + F[0, c, :, lanes(j)]
                )
            result.append(pair)
        return w, result

    def each():
        return [(j, c) for j in range(TILES) for c in range(2)]

    def at(ref, k, c, j):
        return ref[k, c, :, lanes(j)]

    def put(ref, k, c, j, value):
        ref[k, c, :, lanes(j)] = value

    def landing(slot, t):
        if slot == 0:
            return out.at[1, :, rows_of(t), cols_of(t)]
        return prior.at[:, prior_rows(t), cols_of(t)]

    def first_slot(k, t):
        away = lax.rem(lax.rem(t, 8) - lax.rem(k - 1, 8) + 8, 8)
        return jnp.where(jnp.logical_and(k < NT, jnp.logical_and(away >= 1, away <= 4)), 1, 0)

    def back(slot, k):
        return pltpu.make_async_remote_copy(
            src_ref=core(U, k),
            dst_ref=landing(slot, me),
            send_sem=ret_send.at[k],
            recv_sem=ret_recv.at[slot, me],
            device_id={"tm": k - 1 + slot},
            device_id_type=MESH,
        )

    def own(slot):
        return pltpu.make_async_copy(core(U, me + 1 - slot), landing(slot, me), ret_local.at[slot])

    def send_back(k):
        for slot in range(2):

            @pl.when(first_slot(k, me) == slot)
            def _(slot=slot):
                @pl.when(me == k - 1 + slot)
                def _():
                    own(slot).start()

                @pl.when(me != k - 1 + slot)
                def _():
                    back(slot, k).start()

    def hand_on(slot, t):
        return pltpu.make_async_remote_copy(
            src_ref=landing(slot, t),
            dst_ref=landing(1 - slot, t),
            send_sem=hand_send.at[slot, t],
            recv_sem=ret_recv.at[1 - slot, t],
            device_id={"tm": jnp.clip(me + 1 - 2 * slot, 0, NT - 1)},
            device_id_type=MESH,
        )

    def wait_landed(slot, t, local):
        if local:

            @pl.when(t == me)
            def _():
                own(slot).wait()

        @pl.when(t != me)
        def _():
            pltpu.make_async_remote_copy(
                src_ref=core(U, 1),
                dst_ref=landing(slot, t),
                send_sem=ret_send.at[1],
                recv_sem=ret_recv.at[slot, t],
                device_id={"tm": t},
                device_id_type=MESH,
            ).wait_recv()

    def near(slot, i):
        step = i // 2
        along = lax.rem(z + 8 - step, 8) if slot == 0 else lax.rem(z + step, 8)
        return lax.rem(i, 2) * 8 + along

    def far(slot, i):
        step = 1 + i // 2
        along = lax.rem(z + step, 8) if slot == 0 else lax.rem(z + 8 - step, 8)
        return lax.rem(i, 2) * 8 + along

    for copy in stage_in:
        copy.wait()
    packed = pack(S, 0, 0, 0, (blank, blank))
    send_halo(0, pack(F, 0, 0, 1, packed))

    def arrive(first, b):
        def one(i, packed):
            k = first + i

            @pl.when(k - 1 != me)
            def _():
                forwarded(k - 1).wait_recv()

            return pack(S, k, b, i, packed)

        return one

    send_halo(1, lax.fori_loop(0, 8, arrive(1, 1), (blank, blank)))
    send_halo(2, lax.fori_loop(0, 7, arrive(9, 2), (blank, blank)))

    @pl.when(me != NT - 1)
    def _():
        forwarded(NT - 1).wait_recv()

    for c in range(2):
        S[NT, c, ROWS:HELD_ROWS, :] = jnp.zeros((HELD_ROWS - ROWS, HELD_COLS), jnp.float32)
        S[NT, c, 0:ROWS, COLS:HELD_COLS] = jnp.zeros((ROWS, 128), jnp.float32)

    wait_halo(0)
    unpack(S, 0, 0, 0)
    unpack(F, 0, 0, 1)

    def coarse_rhs(g, point, image, base):
        residual = g - (point - image)
        return residual + point - base

    def descend(q):
        def fine(i, carry):
            k = 4 * q + i
            w, rate = rates(S, k)
            for j, c in each():
                put(R0, k, c, j, rate[j][c])
                put(T1, k, c, j, w[j][c] + STEP * rate[j][c])
            w, rate = rates(T1, k)
            for j, c in each():
                base = at(S, k, c, j) + 2 * STEP * at(R0, k, c, j)
                g = coarse_rhs(0.0, at(S, k + 1, c, j), w[j][c] + STEP * rate[j][c], base)
                put(G1, k + 1, c, j, g)
                put(Fx, k + 1, c, j, base + g)
            return carry

        lax.fori_loop(0, 4, fine, 0)

        def second(i, carry):
            m = 2 * q + i
            k = 2 * m
            w, rate = rates(Fx, k + 1)
            for j, c in each():
                base = at(S, k, c, j) + 4 * STEP * at(R0, k, c, j)
                g = coarse_rhs(at(G1, k + 2, c, j), at(S, k + 2, c, j), w[j][c] + 2 * STEP * rate[j][c], base)
                put(G2, m + 1, c, j, g)
                put(Fx, k + 2, c, j, base + g)
            return carry

        lax.fori_loop(0, 2, second, 0)

        k = 4 * q
        w, rate = rates(Fx, k + 2)
        for j, c in each():
            base = at(S, k, c, j) + 8 * STEP * at(R0, k, c, j)
            g = coarse_rhs(at(G2, 2 * q + 2, c, j), at(S, k + 4, c, j), w[j][c] + 4 * STEP * rate[j][c], base)
            put(G3, q + 1, c, j, g)
            put(Fx, k + 4, c, j, base + g)
            put(U, k + 1, c, j, at(Fx, k + 1, c, j))
            put(U, k + 2, c, j, w[j][c])
            put(U, k + 3, c, j, w[j][c] + 2 * STEP * rate[j][c] + at(G1, k + 3, c, j))
            put(U, k + 4, c, j, base + g)

    def exchange(b, fields):
        packed = (blank, blank)
        for i, (ref, k) in enumerate(fields):
            packed = pack(ref, k, b, i, packed)
        send_halo(b, packed)

    def exchanged(b, fields):
        wait_halo(b)
        for i, (ref, k) in enumerate(fields):
            unpack(ref, k, b, i)

    def ascend(k, targets):
        w, rate = rates(U, k)
        for j, c in each():
            for point, factor, right_side, index in targets:
                put(U, point, c, j, w[j][c] + factor * STEP * rate[j][c] + at(right_side, index, c, j))

    def coarsest(k):
        w, rate = rates(Fx, k + 4)
        for j, c in each():
            base = at(S, k, c, j) + 16 * STEP * at(R0, k, c, j)
            index = (k + 8) // 4
            g = coarse_rhs(at(G3, index, c, j), at(S, k + 8, c, j), w[j][c] + 8 * STEP * rate[j][c], base)
            if k == 0:
                put(U, 8, c, j, base + g)
                put(U, 5, c, j, w[j][c] + 2 * STEP * rate[j][c] + at(G1, 5, c, j))
                put(U, 6, c, j, w[j][c] + 4 * STEP * rate[j][c] + at(G2, 3, c, j))
            else:
                put(G4, 0, c, j, g)

    def return_points(first, n):
        def one(d, carry):
            send_back(first + lax.rem(z + d, n))
            return carry

        lax.fori_loop(0, n, one, 0)

    def halos_of(first, b, n):
        wait_halo(b)

        def one(i, carry):
            unpack(S, first + i, b, i)
            return carry

        lax.fori_loop(0, n, one, 0)

    halos_of(1, 1, 8)
    descend(0)
    descend(1)
    fields_a = ((Fx, 4), (G3, 2))
    fields_b = ((Fx, 12), (G3, 3))
    exchange(3, fields_a)
    halos_of(9, 2, 7)
    descend(2)
    descend(3)
    exchange(4, fields_b)
    exchanged(3, fields_a)
    coarsest(0)
    ascend(6, ((7, 2, G1, 7),))
    return_points(1, 8)
    exchanged(4, fields_b)
    coarsest(8)
    ascend(8, ((9, 2, G1, 9), (10, 4, G2, 5), (12, 8, G3, 3), (16, 16, G4, 0)))
    ascend(10, ((11, 2, G1, 11),))
    ascend(12, ((13, 2, G1, 13), (14, 4, G2, 7)))
    ascend(14, ((15, 2, G1, 15),))
    return_points(9, 8)

    def pass_on(i, carry):
        @pl.when(me < NT - 1)
        def _():
            wait_landed(0, near(0, i), True)
            hand_on(0, near(0, i)).start()

        @pl.when(me > 0)
        def _():
            wait_landed(1, near(1, i), True)
            hand_on(1, near(1, i)).start()

        return carry

    lax.fori_loop(0, 8, pass_on, 0)

    @pl.when(me == 0)
    def _():
        copy = pltpu.make_async_copy(initial, prior.at[:, 8 : 8 + BLOCK_ROWS, :], ret_local.at[1])
        copy.start()
        copy.wait()

    def rest(slot):
        def one(i, carry):
            wait_landed(slot, far(slot, i), False)
            return carry

        lax.fori_loop(0, 8, one, 0)

    @pl.when(me > 0)
    def _():
        rest(1)

    def edge_pack(g, packed):
        last, first = packed
        rows = pl.ds(pl.multiple_of(8 + g * ROWS, 8), ROWS)
        for c in range(2):
            index = 2 * g + c
            tail = prior[c, rows, BLOCK_COLS - 128 : BLOCK_COLS]
            head = prior[c, rows, 0:128]
            last = jnp.where(core_lane == index, pltpu.roll(tail, index + 1, 1), last)
            first = jnp.where(core_lane == index, pltpu.roll(head, index, 1), first)
        return last, first

    packed = lax.fori_loop(0, 8, edge_pack, (blank, blank))
    edge_col_out[0], edge_col_out[1] = packed
    for c in range(2):
        edge_row_out[0, c : c + 1, :] = prior[c, 8 + BLOCK_ROWS - 1 : 8 + BLOCK_ROWS, :]
        edge_row_out[1, c : c + 1, :] = prior[c, 8:9, :]
    edges = [
        pltpu.make_async_remote_copy(
            src_ref=src.at[i],
            dst_ref=dst.at[i],
            send_sem=edge_send.at[n],
            recv_sem=edge_recv.at[n],
            device_id=block_sides[to],
            device_id_type=MESH,
        )
        for n, (to, src, dst, i) in enumerate(
            (
                (0, edge_row_out, edge_row_in, 0),
                (0, edge_row_out, edge_row_in, 1),
                (1, edge_col_out, edge_col_in, 0),
                (2, edge_col_out, edge_col_in, 1),
            )
        )
    ]
    for copy in edges:
        copy.start()
    for copy in edges:
        copy.wait_recv()
    for c in range(2):
        prior[c, 7:8, :] = edge_row_in[0, c : c + 1, :]
        prior[c, 8 + BLOCK_ROWS : 9 + BLOCK_ROWS, :] = edge_row_in[1, c : c + 1, :]

    block_tiles = BLOCK_COLS // 128

    def last_step(g, carry):
        around = pl.ds(pl.multiple_of(g * ROWS, ROWS), ROWS + 16)
        rows = pl.ds(pl.multiple_of(g * ROWS, ROWS), ROWS)
        y = [[prior[c, around, lanes(j)] for c in range(2)] for j in range(block_tiles)]
        w = [[y[j][c][8 : 8 + ROWS] for c in range(2)] for j in range(block_tiles)]
        up = [[pltpu.roll(w[j][c], 1, 1) for c in range(2)] for j in range(block_tiles)]
        down = [[pltpu.roll(w[j][c], 127, 1) for c in range(2)] for j in range(block_tiles)]
        before = [pltpu.roll(edge_col_in[0], lax.rem(128 - (2 * g + c), 128), 1) for c in range(2)]
        after = [pltpu.roll(edge_col_in[1], 127 - (2 * g + c), 1) for c in range(2)]
        for j in range(block_tiles):
            west_w, east_w, south_w, north_w = slopes(*w[j])
            for c in range(2):
                x = w[j][c]
                west = pltpu.roll(y[j][c], 1, 0)[8 : 8 + ROWS]
                east = pltpu.roll(y[j][c], ROWS + 15, 0)[8 : 8 + ROWS]
                south = jnp.where(core_lane == 0, up[j - 1][c] if j > 0 else before[c], up[j][c])
                north = jnp.where(core_lane == 127, down[j + 1][c] if j < block_tiles - 1 else after[c], down[j][c])
                rate = (
                    west_w * (west - x)
                    + east_w * (east - x)
                    + south_w * (south - x)
                    + north_w * (north - x)
                    + block_forcing[c, rows, lanes(j)]
                )
                out[0, c, rows, lanes(j)] = x + STEP * rate
        return carry

    load.wait()
    lax.fori_loop(0, 8, last_step, 0)

    for b in range(NB):
        for copy in halo_copies(b):
            copy.wait_send()
    for copy in edges:
        copy.wait_send()

    def finish(i, c):
        @pl.when(i != me)
        def _():
            forward(i).wait_send()

        k = i + 1
        for slot in range(2):

            @pl.when(jnp.logical_and(first_slot(k, me) == slot, me != k - 1 + slot))
            def _(slot=slot):
                back(slot, k).wait_send()

        return c

    lax.fori_loop(0, NT, finish, 0)

    def finish_handed(i, c):
        @pl.when(me < NT - 1)
        def _():
            hand_on(0, near(0, i)).wait_send()

        @pl.when(me > 0)
        def _():
            hand_on(1, near(1, i)).wait_send()

        return c

    lax.fori_loop(0, 8, finish_handed, 0)

    @pl.when(me < NT - 1)
    def _():
        rest(0)

    @pl.when(me == NT - 1)
    def _():
        def one(t, c):
            wait_landed(0, t, True)
            return c

        lax.fori_loop(0, NT, one, 0)


def body(initial, forcing, guess):
    f32 = jnp.float32

    def field(n):
        return pltpu.VMEM((n, 2, HELD_ROWS, HELD_COLS), f32)

    scratch = [field(n) for n in (17, 1, 16, 16, 17, 9, 5, 1, 17, 17)]
    scratch += [
        pltpu.VMEM((2, BLOCK_ROWS + 16, BLOCK_COLS), f32),
        pltpu.VMEM((2, BLOCK_ROWS, BLOCK_COLS), f32),
        pltpu.VMEM((NB, 2, ROWS, 128), f32),
        pltpu.VMEM((NB, 2, ROWS, 128), f32),
        pltpu.VMEM((NB, 2, 2, 8, 128), f32),
        pltpu.VMEM((NB, 2, HELD_ROWS, 128), f32),
        pltpu.VMEM((2, 2, BLOCK_COLS), f32),
        pltpu.VMEM((2, 2, BLOCK_COLS), f32),
        pltpu.VMEM((2, ROWS, 128), f32),
        pltpu.VMEM((2, ROWS, 128), f32),
    ]
    for _ in range(2):
        scratch += [pltpu.VMEM((2, n, 2, HALO, COLS), f32) for n in BATCH]
    dma = pltpu.SemaphoreType.DMA
    scratch += [dma((4,)), dma((NT,)), dma((NT,)), dma((NB, 8)), dma((NB, 8)), dma((NT + 1,)), dma((2, NT)), dma((2,))]
    scratch += [dma((2, NT)), dma((4,)), dma((4,))]
    spec = pl.BlockSpec(memory_space=pltpu.HBM)
    return pl.pallas_call(
        kernel,
        out_shape=pltpu.VMEM((2, 2, BLOCK_ROWS, BLOCK_COLS), f32),
        in_specs=[spec] * 3,
        out_specs=pl.BlockSpec(memory_space=pltpu.VMEM),
        scratch_shapes=scratch,
        compiler_params=pltpu.CompilerParams(
            collective_id=0, has_side_effects=True, vmem_limit_bytes=32 * 1024 * 1024
        ),
        name="cycle",
    )(*(pltpu.with_memory_space_constraint(x, pltpu.HBM) for x in (initial, forcing, guess)))


def solution(mesh):
    in_specs = (P(None, "sx", "sy"), P(None, "sx", "sy"), P("tm", None, "sx", "sy"))
    out_specs = P("tm", None, "sx", "sy")
    return jax.shard_map(body, mesh=mesh, in_specs=in_specs, out_specs=out_specs, check_vma=False)
```

```python
import jax
import jax.numpy as jnp
from jax import lax
from jax.experimental import pallas as pl
from jax.experimental.pallas import tpu as pltpu
from jax.sharding import PartitionSpec as P

VISCOSITY = 0.5
COURANT = 0.7
MESH = pl.DeviceIdType.MESH
NT = 16
BLOCK_ROWS, BLOCK_COLS = 256, 512
ROWS, COLS = 32, 256
HALO = 4
HELD_ROWS, HELD_COLS = ROWS + 2 * HALO, COLS + 128
TILES = HELD_COLS // 128
STEP = COURANT / (NT * (2.0 + 4.0 * VISCOSITY))
BATCH = (2, 8, 7, 2, 2)
NB = len(BATCH)
UP, DOWN, RIGHT, LEFT, UP_RIGHT, DOWN_RIGHT, UP_LEFT, DOWN_LEFT = range(8)


def kernel(initial, forcing, guess, out, *scratch):
    (S, F, R0, T1, G1, G2, G3, G4, Fx, U, prior, block_forcing, col_out, col_in, corner_in, wide) = scratch[:16]
    row_out = scratch[16 : 16 + NB]
    row_in = scratch[16 + NB : 16 + 2 * NB]
    (local_sem, fwd_send, fwd_recv, halo_send, halo_recv, ret_send, ret_recv, ret_local, hand_send, edge_send, edge_recv, end_send, end_recv) = (
        scratch[16 + 2 * NB :]
    )

    me = lax.axis_index("tm")
    sx = lax.axis_index("sx")
    sy = lax.axis_index("sy")
    xl = me // 8
    z = lax.rem(me, 8)

    def mirrored(i):
        return jnp.where(sx == 0, i, 7 - i)

    zz = mirrored(z)

    def beside(vertical, horizontal):
        if vertical == 0:
            nz, nsx = z, sx
        elif vertical == 1:
            nz, nsx = jnp.where(zz < 7, mirrored(zz + 1), z), jnp.where(zz < 7, sx, 1 - sx)
        else:
            nz, nsx = jnp.where(zz > 0, mirrored(zz - 1), z), jnp.where(zz > 0, sx, 1 - sx)
        if horizontal == 0:
            nx, nsy = xl, sy
        elif horizontal == 1:
            nx, nsy = 1 - xl, jnp.where(xl == 0, sy, lax.rem(sy + 1, 8))
        else:
            nx, nsy = 1 - xl, jnp.where(xl == 1, sy, lax.rem(sy + 7, 8))
        return {"tm": nx * 8 + nz, "sx": nsx, "sy": nsy}

    sides = [beside(*v) for v in ((1, 0), (-1, 0), (0, 1), (0, -1), (1, 1), (-1, 1), (1, -1), (-1, -1))]
    block_sides = [{"sx": 1 - sx}, {"sy": lax.rem(sy + 1, 8)}, {"sy": lax.rem(sy + 7, 8)}]

    def rows_of(t):
        return pl.ds(pl.multiple_of(mirrored(lax.rem(t, 8)) * ROWS, ROWS), ROWS)

    def cols_of(t):
        return pl.ds(pl.multiple_of((t // 8) * COLS, COLS), COLS)

    own_rows, own_cols = rows_of(me), cols_of(me)

    def prior_rows(t):
        return pl.ds(pl.multiple_of(8 + mirrored(lax.rem(t, 8)) * ROWS, 8), ROWS)

    def prior_cols(t):
        return pl.ds(pl.multiple_of(128 + (t // 8) * COLS, 128), COLS)

    def core(ref, k):
        return ref.at[k, :, 0:ROWS, 0:COLS]

    barrier = pltpu.get_barrier_semaphore()

    def greet(d, c):
        pl.semaphore_signal(barrier, inc=1, device_id={"tm": lax.rem(me + d, NT)}, device_id_type=MESH)
        return c

    lax.fori_loop(1, NT, greet, 0)
    for side in sides + block_sides:
        pl.semaphore_signal(barrier, inc=1, device_id=side, device_id_type=MESH)

    stage_in = [
        pltpu.make_async_copy(initial.at[:, own_rows, own_cols], core(S, 0), local_sem.at[0]),
        pltpu.make_async_copy(forcing.at[:, own_rows, own_cols], core(F, 0), local_sem.at[1]),
        pltpu.make_async_copy(guess.at[0, :, own_rows, own_cols], core(S, me + 1), local_sem.at[2]),
    ]
    for copy in stage_in:
        copy.start()
    pl.semaphore_wait(barrier, NT - 1 + 8 + 3)

    def forward(peer):
        return pltpu.make_async_remote_copy(
            src_ref=guess.at[0, :, rows_of(peer), cols_of(peer)],
            dst_ref=core(S, me + 1),
            send_sem=fwd_send.at[peer],
            recv_sem=fwd_recv.at[me],
            device_id={"tm": peer},
            device_id_type=MESH,
        )

    def forwarded(peer):
        return pltpu.make_async_remote_copy(
            src_ref=guess.at[0, :, own_rows, own_cols],
            dst_ref=core(S, peer + 1),
            send_sem=fwd_send.at[peer],
            recv_sem=fwd_recv.at[peer],
            device_id={"tm": peer},
            device_id_type=MESH,
        )

    def start_forward(d, c):
        forward(lax.rem(me + d, NT)).start()
        return c

    forward(lax.rem(xl + 1, 2) * 8 + lax.rem(z + 4, 8)).start()
    forward(lax.rem(xl + 0, 2) * 8 + lax.rem(z + 4, 8)).start()
    forward(lax.rem(xl + 1, 2) * 8 + lax.rem(z + 1, 8)).start()
    forward(lax.rem(xl + 1, 2) * 8 + lax.rem(z + 7, 8)).start()
    forward(lax.rem(xl + 1, 2) * 8 + lax.rem(z + 3, 8)).start()
    forward(lax.rem(xl + 1, 2) * 8 + lax.rem(z + 5, 8)).start()
    forward(lax.rem(xl + 0, 2) * 8 + lax.rem(z + 1, 8)).start()
    forward(lax.rem(xl + 0, 2) * 8 + lax.rem(z + 7, 8)).start()
    forward(lax.rem(xl + 0, 2) * 8 + lax.rem(z + 3, 8)).start()
    forward(lax.rem(xl + 0, 2) * 8 + lax.rem(z + 5, 8)).start()
    forward(lax.rem(xl + 1, 2) * 8 + lax.rem(z + 2, 8)).start()
    forward(lax.rem(xl + 1, 2) * 8 + lax.rem(z + 6, 8)).start()
    forward(lax.rem(xl + 0, 2) * 8 + lax.rem(z + 2, 8)).start()
    forward(lax.rem(xl + 0, 2) * 8 + lax.rem(z + 6, 8)).start()
    forward(lax.rem(xl + 1, 2) * 8 + lax.rem(z + 0, 8)).start()
    load = pltpu.make_async_copy(forcing, block_forcing, local_sem.at[3])
    load.start()

    lane = lax.broadcasted_iota(jnp.int32, (HELD_ROWS, 128), 1)
    core_lane = lax.broadcasted_iota(jnp.int32, (ROWS, 128), 1)
    blank = jnp.zeros((ROWS, 128), jnp.float32)

    def lanes(j):
        return slice(128 * j, 128 * (j + 1))

    def halo_copies(b):
        parts = (
            (UP, row_out[b].at[0], row_in[b].at[1]),
            (DOWN, row_out[b].at[1], row_in[b].at[0]),
            (RIGHT, col_out.at[b, 0], col_in.at[b, 0]),
            (LEFT, col_out.at[b, 1], col_in.at[b, 1]),
            (DOWN_RIGHT, col_out.at[b, 0, 0:8], corner_in.at[b, 0, 0]),
            (UP_RIGHT, col_out.at[b, 0, ROWS - 8 : ROWS], corner_in.at[b, 0, 1]),
            (DOWN_LEFT, col_out.at[b, 1, 0:8], corner_in.at[b, 1, 0]),
            (UP_LEFT, col_out.at[b, 1, ROWS - 8 : ROWS], corner_in.at[b, 1, 1]),
        )
        return [
            pltpu.make_async_remote_copy(
                src_ref=src,
                dst_ref=dst,
                send_sem=halo_send.at[b, i],
                recv_sem=halo_recv.at[b, i],
                device_id=sides[to],
                device_id_type=MESH,
            )
            for i, (to, src, dst) in enumerate(parts)
        ]

    def pack(ref, k, b, i, packed):
        last, first = packed
        for c in range(2):
            row_out[b][0, i, c] = ref[k, c, ROWS - HALO : ROWS, 0:COLS]
            row_out[b][1, i, c] = ref[k, c, 0:HALO, 0:COLS]
            index = 8 * i + HALO * c
            mine = jnp.logical_and(core_lane >= index, core_lane < index + HALO)
            tail = ref[k, c, 0:ROWS, COLS - 128 : COLS]
            head = ref[k, c, 0:ROWS, 0:128]
            last = jnp.where(mine, pltpu.roll(tail, lax.rem(index + HALO, 128), 1), last)
            first = jnp.where(mine, pltpu.roll(head, index, 1), first)
        return last, first

    def send_halo(b, packed):
        col_out[b, 0] = packed[0]
        col_out[b, 1] = packed[1]
        for copy in halo_copies(b):
            copy.start()

    def wait_halo(b):
        for copy in halo_copies(b):
            copy.wait_recv()
        for side in range(2):
            wide[b, side, 0:ROWS] = col_in[b, side]
            wide[b, side, ROWS : ROWS + HALO] = corner_in[b, side, 0, 0:HALO]
            wide[b, side, ROWS + HALO : HELD_ROWS] = corner_in[b, side, 1, HALO:8]

    def unpack(ref, k, b, i):
        for c in range(2):
            ref[k, c, ROWS : ROWS + HALO, 0:COLS] = row_in[b][0, i, c]
            ref[k, c, ROWS + HALO : HELD_ROWS, 0:COLS] = row_in[b][1, i, c]
            index = 8 * i + HALO * c
            after = pltpu.roll(wide[b, 1], lax.rem(128 - index, 128), 1)
            before = pltpu.roll(wide[b, 0], lax.rem(256 - HALO - index, 128), 1)
            ref[k, c, :, COLS:HELD_COLS] = jnp.where(lane < 64, after, before)

    def slopes(first, second):
        return (
            0.5 + jnp.maximum(first, 0.0),
            0.5 - jnp.minimum(first, 0.0),
            0.5 + jnp.maximum(second, 0.0),
            0.5 - jnp.minimum(second, 0.0),
        )

    def rates(ref, k):
        w = [[ref[k, c, :, lanes(j)] for c in range(2)] for j in range(TILES)]
        up = [[pltpu.roll(w[j][c], 1, 1) for c in range(2)] for j in range(TILES)]
        down = [[pltpu.roll(w[j][c], 127, 1) for c in range(2)] for j in range(TILES)]
        result = []
        for j in range(TILES):
            west_w, east_w, south_w, north_w = slopes(*w[j])
            pair = []
            for c in range(2):
                x = w[j][c]
                west = pltpu.roll(x, 1, 0)
                east = pltpu.roll(x, HELD_ROWS - 1, 0)
                south = jnp.where(lane == 0, up[j - 1][c], up[j][c])
                north = jnp.where(lane == 127, down[(j + 1) % TILES][c], down[j][c])
                pair.append(
                    west_w * (west - x)
                    + east_w * (east - x)
                    + south_w * (south - x)
                    + north_w * (north - x)
                    + F[0, c, :, lanes(j)]
                )
            result.append(pair)
        return w, result

    def each():
        return [(j, c) for j in range(TILES) for c in range(2)]

    def at(ref, k, c, j):
        return ref[k, c, :, lanes(j)]

    def put(ref, k, c, j, value):
        ref[k, c, :, lanes(j)] = value

    def landing(slot, t):
        if slot == 0:
            return out.at[1, :, rows_of(t), cols_of(t)]
        return prior.at[:, prior_rows(t), prior_cols(t)]

    def first_slot(k, t):
        away = lax.rem(lax.rem(t, 8) - lax.rem(k - 1, 8) + 8, 8)
        return jnp.where(jnp.logical_and(k < NT, jnp.logical_and(away >= 1, away <= 4)), 1, 0)

    def back(slot, k):
        return pltpu.make_async_remote_copy(
            src_ref=core(U, k),
            dst_ref=landing(slot, me),
            send_sem=ret_send.at[k],
            recv_sem=ret_recv.at[slot, me],
            device_id={"tm": k - 1 + slot},
            device_id_type=MESH,
        )

    def own(slot):
        return pltpu.make_async_copy(core(U, me + 1 - slot), landing(slot, me), ret_local.at[slot])

    def send_back(k):
        for slot in range(2):

            @pl.when(first_slot(k, me) == slot)
            def _(slot=slot):
                @pl.when(me == k - 1 + slot)
                def _():
                    own(slot).start()

                @pl.when(me != k - 1 + slot)
                def _():
                    back(slot, k).start()

    def hand_on(slot, t):
        return pltpu.make_async_remote_copy(
            src_ref=landing(slot, t),
            dst_ref=landing(1 - slot, t),
            send_sem=hand_send.at[slot, t],
            recv_sem=ret_recv.at[1 - slot, t],
            device_id={"tm": jnp.clip(me + 1 - 2 * slot, 0, NT - 1)},
            device_id_type=MESH,
        )

    def wait_landed(slot, t, local):
        if local:

            @pl.when(t == me)
            def _():
                own(slot).wait()

        @pl.when(t != me)
        def _():
            pltpu.make_async_remote_copy(
                src_ref=core(U, 1),
                dst_ref=landing(slot, t),
                send_sem=ret_send.at[1],
                recv_sem=ret_recv.at[slot, t],
                device_id={"tm": t},
                device_id_type=MESH,
            ).wait_recv()

    def near(slot, i):
        step = i // 2
        along = lax.rem(z + 8 - step, 8) if slot == 0 else lax.rem(z + step, 8)
        return lax.rem(i, 2) * 8 + along

    def far(slot, i):
        step = 1 + i // 2
        along = lax.rem(z + step, 8) if slot == 0 else lax.rem(z + 8 - step, 8)
        return lax.rem(i, 2) * 8 + along

    for copy in stage_in:
        copy.wait()
    packed = pack(S, 0, 0, 0, (blank, blank))
    send_halo(0, pack(F, 0, 0, 1, packed))

    def arrive(first, b):
        def one(i, packed):
            k = first + i

            @pl.when(k - 1 != me)
            def _():
                forwarded(k - 1).wait_recv()

            return pack(S, k, b, i, packed)

        return one

    send_halo(1, lax.fori_loop(0, 8, arrive(1, 1), (blank, blank)))
    send_halo(2, lax.fori_loop(0, 7, arrive(9, 2), (blank, blank)))

    @pl.when(me != NT - 1)
    def _():
        forwarded(NT - 1).wait_recv()

    for c in range(2):
        S[NT, c, ROWS:HELD_ROWS, :] = jnp.zeros((HELD_ROWS - ROWS, HELD_COLS), jnp.float32)
        S[NT, c, 0:ROWS, COLS:HELD_COLS] = jnp.zeros((ROWS, 128), jnp.float32)

    wait_halo(0)
    unpack(S, 0, 0, 0)
    unpack(F, 0, 0, 1)

    def coarse_rhs(g, point, image, base):
        residual = g - (point - image)
        return residual + point - base

    def descend(q):
        def fine(i, carry):
            k = 4 * q + i
            w, rate = rates(S, k)
            for j, c in each():
                put(R0, k, c, j, rate[j][c])
                put(T1, k, c, j, w[j][c] + STEP * rate[j][c])
            w, rate = rates(T1, k)
            for j, c in each():
                base = at(S, k, c, j) + 2 * STEP * at(R0, k, c, j)
                g = coarse_rhs(0.0, at(S, k + 1, c, j), w[j][c] + STEP * rate[j][c], base)
                put(G1, k + 1, c, j, g)
                put(Fx, k + 1, c, j, base + g)
            return carry

        lax.fori_loop(0, 4, fine, 0)

        def second(i, carry):
            m = 2 * q + i
            k = 2 * m
            w, rate = rates(Fx, k + 1)
            for j, c in each():
                base = at(S, k, c, j) + 4 * STEP * at(R0, k, c, j)
                g = coarse_rhs(at(G1, k + 2, c, j), at(S, k + 2, c, j), w[j][c] + 2 * STEP * rate[j][c], base)
                put(G2, m + 1, c, j, g)
                put(Fx, k + 2, c, j, base + g)
            return carry

        lax.fori_loop(0, 2, second, 0)

        k = 4 * q
        w, rate = rates(Fx, k + 2)
        for j, c in each():
            base = at(S, k, c, j) + 8 * STEP * at(R0, k, c, j)
            g = coarse_rhs(at(G2, 2 * q + 2, c, j), at(S, k + 4, c, j), w[j][c] + 4 * STEP * rate[j][c], base)
            put(G3, q + 1, c, j, g)
            put(Fx, k + 4, c, j, base + g)
            put(U, k + 1, c, j, at(Fx, k + 1, c, j))
            put(U, k + 2, c, j, w[j][c])
            put(U, k + 3, c, j, w[j][c] + 2 * STEP * rate[j][c] + at(G1, k + 3, c, j))
            put(U, k + 4, c, j, base + g)

    def exchange(b, fields):
        packed = (blank, blank)
        for i, (ref, k) in enumerate(fields):
            packed = pack(ref, k, b, i, packed)
        send_halo(b, packed)

    def exchanged(b, fields):
        wait_halo(b)
        for i, (ref, k) in enumerate(fields):
            unpack(ref, k, b, i)

    def ascend(k, targets):
        w, rate = rates(U, k)
        for j, c in each():
            for point, factor, right_side, index in targets:
                put(U, point, c, j, w[j][c] + factor * STEP * rate[j][c] + at(right_side, index, c, j))

    def coarsest(k):
        w, rate = rates(Fx, k + 4)
        for j, c in each():
            base = at(S, k, c, j) + 16 * STEP * at(R0, k, c, j)
            index = (k + 8) // 4
            g = coarse_rhs(at(G3, index, c, j), at(S, k + 8, c, j), w[j][c] + 8 * STEP * rate[j][c], base)
            if k == 0:
                put(U, 8, c, j, base + g)
                put(U, 5, c, j, w[j][c] + 2 * STEP * rate[j][c] + at(G1, 5, c, j))
                put(U, 6, c, j, w[j][c] + 4 * STEP * rate[j][c] + at(G2, 3, c, j))
            else:
                put(G4, 0, c, j, g)

    def return_points(first, offsets=(3, -4, 0, -1, 2, -3, 1, -2)):
        for offset in offsets:
            send_back(first + lax.rem(z + offset + 8, 8))

    def halos_of(first, b, n):
        wait_halo(b)

        def one(i, carry):
            unpack(S, first + i, b, i)
            return carry

        lax.fori_loop(0, n, one, 0)

    fields_a = ((Fx, 4), (G3, 2))
    fields_b = ((Fx, 12), (G3, 3))
    halos_of(1, 1, 8)
    descend(0)
    descend(1)
    exchange(3, fields_a)
    halos_of(9, 2, 7)
    descend(2)
    exchange(4, fields_b)
    exchanged(3, fields_a)
    coarsest(0)
    ascend(6, ((7, 2, G1, 7),))
    return_points(1)
    descend(3)
    exchanged(4, fields_b)
    coarsest(8)
    ascend(8, ((9, 2, G1, 9), (10, 4, G2, 5), (12, 8, G3, 3), (16, 16, G4, 0)))
    ascend(10, ((11, 2, G1, 11),))
    ascend(12, ((13, 2, G1, 13), (14, 4, G2, 7)))
    ascend(14, ((15, 2, G1, 15),))
    return_points(9)

    def side_edge(t):
        first = t // 8 == 0
        return pltpu.make_async_remote_copy(
            src_ref=prior.at[:, prior_rows(t), pl.ds(pl.multiple_of(jnp.where(first, 128, BLOCK_COLS), 128), 128)],
            dst_ref=prior.at[:, prior_rows(t), pl.ds(pl.multiple_of(jnp.where(first, 128 + BLOCK_COLS, 0), 128), 128)],
            send_sem=edge_send.at[t],
            recv_sem=edge_recv.at[t],
            device_id={"sy": lax.rem(sy + jnp.where(first, 7, 1), 8)},
            device_id_type=MESH,
        )

    def end_edge(t, last):
        src, dst = (BLOCK_ROWS, 0) if last else (8, 8 + BLOCK_ROWS)
        return pltpu.make_async_remote_copy(
            src_ref=prior.at[:, src : src + 8, prior_cols(t)],
            dst_ref=prior.at[:, dst : dst + 8, prior_cols(t)],
            send_sem=end_send.at[2 * (t // 8) + last],
            recv_sem=end_recv.at[2 * (t // 8) + last],
            device_id=block_sides[0],
            device_id_type=MESH,
        )

    def send_edges(t):
        side_edge(t).start()
        for last in range(2):

            @pl.when(mirrored(lax.rem(t, 8)) == 7 * last)
            def _(last=last):
                end_edge(t, last).start()

    @pl.when(me == 0)
    def _():
        def one(t, carry):
            send_edges(t)
            return carry

        copy = pltpu.make_async_copy(
            initial, prior.at[:, 8 : 8 + BLOCK_ROWS, 128 : 128 + BLOCK_COLS], ret_local.at[1]
        )
        copy.start()
        copy.wait()
        lax.fori_loop(0, NT, one, 0)

    def pass_on(i, carry):
        @pl.when(me < NT - 1)
        def _():
            wait_landed(0, near(0, i), True)
            hand_on(0, near(0, i)).start()

        @pl.when(me > 0)
        def _():
            wait_landed(1, near(1, i), True)
            hand_on(1, near(1, i)).start()
            send_edges(near(1, i))

        return carry

    lax.fori_loop(0, 8, pass_on, 0)

    def rest(slot):
        def one(i, carry):
            wait_landed(slot, far(slot, i), False)
            if slot == 1:
                send_edges(far(slot, i))
            return carry

        lax.fori_loop(0, 8, one, 0)

    @pl.when(me > 0)
    def _():
        rest(1)

    block_tiles = BLOCK_COLS // 128

    def last_step(i, carry):
        along = lax.rem(z + jnp.where(i < 4, i, 11 - i), 8)
        g = mirrored(along)
        side_edge(along).wait_recv()
        side_edge(8 + along).wait_recv()
        for last in range(2):

            @pl.when(g == 7 - 7 * last)
            def _(last=last):
                end_edge(0, last).wait_recv()
                end_edge(8, last).wait_recv()

        around = pl.ds(pl.multiple_of(g * ROWS, ROWS), ROWS + 16)
        rows = pl.ds(pl.multiple_of(g * ROWS, ROWS), ROWS)
        inner = pl.ds(pl.multiple_of(8 + g * ROWS, 8), ROWS)
        y = [[prior[c, around, lanes(j + 1)] for c in range(2)] for j in range(block_tiles)]
        w = [[y[j][c][8 : 8 + ROWS] for c in range(2)] for j in range(block_tiles)]
        up = [[pltpu.roll(w[j][c], 1, 1) for c in range(2)] for j in range(block_tiles)]
        down = [[pltpu.roll(w[j][c], 127, 1) for c in range(2)] for j in range(block_tiles)]
        before = [pltpu.roll(prior[c, inner, lanes(0)], 1, 1) for c in range(2)]
        after = [pltpu.roll(prior[c, inner, lanes(block_tiles + 1)], 127, 1) for c in range(2)]
        for j in range(block_tiles):
            west_w, east_w, south_w, north_w = slopes(*w[j])
            for c in range(2):
                x = w[j][c]
                west = pltpu.roll(y[j][c], 1, 0)[8 : 8 + ROWS]
                east = pltpu.roll(y[j][c], ROWS + 15, 0)[8 : 8 + ROWS]
                south = jnp.where(core_lane == 0, up[j - 1][c] if j > 0 else before[c], up[j][c])
                north = jnp.where(core_lane == 127, down[j + 1][c] if j < block_tiles - 1 else after[c], down[j][c])
                rate = (
                    west_w * (west - x)
                    + east_w * (east - x)
                    + south_w * (south - x)
                    + north_w * (north - x)
                    + block_forcing[c, rows, lanes(j)]
                )
                out[0, c, rows, lanes(j)] = x + STEP * rate
        return carry

    load.wait()
    lax.fori_loop(0, 8, last_step, 0)

    for b in range(NB):
        for copy in halo_copies(b):
            copy.wait_send()
    def finish_edges(t, c):
        side_edge(t).wait_send()
        return c

    lax.fori_loop(0, NT, finish_edges, 0)
    for t in (0, 8):
        for last in range(2):
            end_edge(t, last).wait_send()

    def finish(i, c):
        @pl.when(i != me)
        def _():
            forward(i).wait_send()

        k = i + 1
        for slot in range(2):

            @pl.when(jnp.logical_and(first_slot(k, me) == slot, me != k - 1 + slot))
            def _(slot=slot):
                back(slot, k).wait_send()

        return c

    lax.fori_loop(0, NT, finish, 0)

    def finish_handed(i, c):
        @pl.when(me < NT - 1)
        def _():
            hand_on(0, near(0, i)).wait_send()

        @pl.when(me > 0)
        def _():
            hand_on(1, near(1, i)).wait_send()

        return c

    lax.fori_loop(0, 8, finish_handed, 0)

    @pl.when(me < NT - 1)
    def _():
        rest(0)

    @pl.when(me == NT - 1)
    def _():
        def one(t, c):
            wait_landed(0, t, True)
            return c

        lax.fori_loop(0, NT, one, 0)


def body(initial, forcing, guess):
    f32 = jnp.float32

    def field(n):
        return pltpu.VMEM((n, 2, HELD_ROWS, HELD_COLS), f32)

    scratch = [field(n) for n in (17, 1, 16, 16, 17, 9, 5, 1, 17, 17)]
    scratch += [
        pltpu.VMEM((2, BLOCK_ROWS + 16, BLOCK_COLS + 256), f32),
        pltpu.VMEM((2, BLOCK_ROWS, BLOCK_COLS), f32),
        pltpu.VMEM((NB, 2, ROWS, 128), f32),
        pltpu.VMEM((NB, 2, ROWS, 128), f32),
        pltpu.VMEM((NB, 2, 2, 8, 128), f32),
        pltpu.VMEM((NB, 2, HELD_ROWS, 128), f32),
    ]
    for _ in range(2):
        scratch += [pltpu.VMEM((2, n, 2, HALO, COLS), f32) for n in BATCH]
    dma = pltpu.SemaphoreType.DMA
    scratch += [dma((4,)), dma((NT,)), dma((NT,)), dma((NB, 8)), dma((NB, 8)), dma((NT + 1,)), dma((2, NT)), dma((2,))]
    scratch += [dma((2, NT)), dma((NT,)), dma((NT,)), dma((4,)), dma((4,))]
    spec = pl.BlockSpec(memory_space=pltpu.HBM)
    return pl.pallas_call(
        kernel,
        out_shape=pltpu.VMEM((2, 2, BLOCK_ROWS, BLOCK_COLS), f32),
        in_specs=[spec] * 3,
        out_specs=pl.BlockSpec(memory_space=pltpu.VMEM),
        scratch_shapes=scratch,
        compiler_params=pltpu.CompilerParams(
            collective_id=0, has_side_effects=True, vmem_limit_bytes=32 * 1024 * 1024
        ),
        name="cycle",
    )(*(pltpu.with_memory_space_constraint(x, pltpu.HBM) for x in (initial, forcing, guess)))


def solution(mesh):
    in_specs = (P(None, "sx", "sy"), P(None, "sx", "sy"), P("tm", None, "sx", "sy"))
    out_specs = P("tm", None, "sx", "sy")
    return jax.shard_map(body, mesh=mesh, in_specs=in_specs, out_specs=out_specs, check_vma=False)
```

```python
import jax
import jax.numpy as jnp
from jax import lax
from jax.experimental import pallas as pl
from jax.experimental.pallas import tpu as pltpu
from jax.sharding import PartitionSpec as P

VISCOSITY = 0.5
COURANT = 0.7
MESH = pl.DeviceIdType.MESH
NT = 16
BLOCK_ROWS, BLOCK_COLS = 256, 512
ROWS, COLS = 32, 256
HALO = 4
HELD_ROWS, HELD_COLS = ROWS + 2 * HALO, COLS + 128
TILES = HELD_COLS // 128
STEP = COURANT / (NT * (2.0 + 4.0 * VISCOSITY))
BATCH = (2, 4, 4, 7, 2, 2)
NB = len(BATCH)
UP, DOWN, RIGHT, LEFT, UP_RIGHT, DOWN_RIGHT, UP_LEFT, DOWN_LEFT = range(8)


def kernel(initial, forcing, guess, out, *scratch):
    (S, F, R0, T1, G1, G2, G3, G4, Fx, U, prior, block_forcing, col_out, col_in, corner_in, wide) = scratch[:16]
    row_out = scratch[16 : 16 + NB]
    row_in = scratch[16 + NB : 16 + 2 * NB]
    (local_sem, fwd_send, fwd_recv, halo_send, halo_recv, ret_send, ret_recv, ret_local, hand_send, edge_send, edge_recv, end_send, end_recv) = (
        scratch[16 + 2 * NB :]
    )

    me = lax.axis_index("tm")
    sx = lax.axis_index("sx")
    sy = lax.axis_index("sy")
    xl = me // 8
    z = lax.rem(me, 8)

    def mirrored(i):
        return jnp.where(sx == 0, i, 7 - i)

    zz = mirrored(z)

    def beside(vertical, horizontal):
        if vertical == 0:
            nz, nsx = z, sx
        elif vertical == 1:
            nz, nsx = jnp.where(zz < 7, mirrored(zz + 1), z), jnp.where(zz < 7, sx, 1 - sx)
        else:
            nz, nsx = jnp.where(zz > 0, mirrored(zz - 1), z), jnp.where(zz > 0, sx, 1 - sx)
        if horizontal == 0:
            nx, nsy = xl, sy
        elif horizontal == 1:
            nx, nsy = 1 - xl, jnp.where(xl == 0, sy, lax.rem(sy + 1, 8))
        else:
            nx, nsy = 1 - xl, jnp.where(xl == 1, sy, lax.rem(sy + 7, 8))
        return {"tm": nx * 8 + nz, "sx": nsx, "sy": nsy}

    sides = [beside(*v) for v in ((1, 0), (-1, 0), (0, 1), (0, -1), (1, 1), (-1, 1), (1, -1), (-1, -1))]
    block_sides = [{"sx": 1 - sx}, {"sy": lax.rem(sy + 1, 8)}, {"sy": lax.rem(sy + 7, 8)}]

    def rows_of(t):
        return pl.ds(pl.multiple_of(mirrored(lax.rem(t, 8)) * ROWS, ROWS), ROWS)

    def cols_of(t):
        return pl.ds(pl.multiple_of((t // 8) * COLS, COLS), COLS)

    own_rows, own_cols = rows_of(me), cols_of(me)

    def prior_rows(t):
        return pl.ds(pl.multiple_of(8 + mirrored(lax.rem(t, 8)) * ROWS, 8), ROWS)

    def prior_cols(t):
        return pl.ds(pl.multiple_of(128 + (t // 8) * COLS, 128), COLS)

    def core(ref, k):
        return ref.at[k, :, 0:ROWS, 0:COLS]

    barrier = pltpu.get_barrier_semaphore()

    def greet(d, c):
        pl.semaphore_signal(barrier, inc=1, device_id={"tm": lax.rem(me + d, NT)}, device_id_type=MESH)
        return c

    lax.fori_loop(1, NT, greet, 0)
    for side in sides + block_sides:
        pl.semaphore_signal(barrier, inc=1, device_id=side, device_id_type=MESH)

    stage_in = [
        pltpu.make_async_copy(initial.at[:, own_rows, own_cols], core(S, 0), local_sem.at[0]),
        pltpu.make_async_copy(forcing.at[:, own_rows, own_cols], core(F, 0), local_sem.at[1]),
        pltpu.make_async_copy(guess.at[0, :, own_rows, own_cols], core(S, me + 1), local_sem.at[2]),
    ]
    for copy in stage_in:
        copy.start()
    pl.semaphore_wait(barrier, NT - 1 + 8 + 3)

    def forward(peer):
        return pltpu.make_async_remote_copy(
            src_ref=guess.at[0, :, rows_of(peer), cols_of(peer)],
            dst_ref=core(S, me + 1),
            send_sem=fwd_send.at[peer],
            recv_sem=fwd_recv.at[me],
            device_id={"tm": peer},
            device_id_type=MESH,
        )

    def forwarded(peer):
        return pltpu.make_async_remote_copy(
            src_ref=guess.at[0, :, own_rows, own_cols],
            dst_ref=core(S, peer + 1),
            send_sem=fwd_send.at[peer],
            recv_sem=fwd_recv.at[peer],
            device_id={"tm": peer},
            device_id_type=MESH,
        )

    def start_forward(d, c):
        forward(lax.rem(me + d, NT)).start()
        return c

    forward(lax.rem(xl + 1, 2) * 8 + lax.rem(z + 4, 8)).start()
    forward(lax.rem(xl + 0, 2) * 8 + lax.rem(z + 4, 8)).start()
    forward(lax.rem(xl + 1, 2) * 8 + lax.rem(z + 1, 8)).start()
    forward(lax.rem(xl + 1, 2) * 8 + lax.rem(z + 7, 8)).start()
    forward(lax.rem(xl + 1, 2) * 8 + lax.rem(z + 3, 8)).start()
    forward(lax.rem(xl + 1, 2) * 8 + lax.rem(z + 5, 8)).start()
    forward(lax.rem(xl + 0, 2) * 8 + lax.rem(z + 1, 8)).start()
    forward(lax.rem(xl + 0, 2) * 8 + lax.rem(z + 7, 8)).start()
    forward(lax.rem(xl + 0, 2) * 8 + lax.rem(z + 3, 8)).start()
    forward(lax.rem(xl + 0, 2) * 8 + lax.rem(z + 5, 8)).start()
    forward(lax.rem(xl + 1, 2) * 8 + lax.rem(z + 2, 8)).start()
    forward(lax.rem(xl + 1, 2) * 8 + lax.rem(z + 6, 8)).start()
    forward(lax.rem(xl + 0, 2) * 8 + lax.rem(z + 2, 8)).start()
    forward(lax.rem(xl + 0, 2) * 8 + lax.rem(z + 6, 8)).start()
    forward(lax.rem(xl + 1, 2) * 8 + lax.rem(z + 0, 8)).start()
    load = pltpu.make_async_copy(forcing, block_forcing, local_sem.at[3])
    load.start()

    lane = lax.broadcasted_iota(jnp.int32, (HELD_ROWS, 128), 1)
    core_lane = lax.broadcasted_iota(jnp.int32, (ROWS, 128), 1)
    blank = jnp.zeros((ROWS, 128), jnp.float32)

    def lanes(j):
        return slice(128 * j, 128 * (j + 1))

    def halo_copies(b):
        parts = (
            (UP, row_out[b].at[0], row_in[b].at[1]),
            (DOWN, row_out[b].at[1], row_in[b].at[0]),
            (RIGHT, col_out.at[b, 0], col_in.at[b, 0]),
            (LEFT, col_out.at[b, 1], col_in.at[b, 1]),
            (DOWN_RIGHT, col_out.at[b, 0, 0:8], corner_in.at[b, 0, 0]),
            (UP_RIGHT, col_out.at[b, 0, ROWS - 8 : ROWS], corner_in.at[b, 0, 1]),
            (DOWN_LEFT, col_out.at[b, 1, 0:8], corner_in.at[b, 1, 0]),
            (UP_LEFT, col_out.at[b, 1, ROWS - 8 : ROWS], corner_in.at[b, 1, 1]),
        )
        return [
            pltpu.make_async_remote_copy(
                src_ref=src,
                dst_ref=dst,
                send_sem=halo_send.at[b, i],
                recv_sem=halo_recv.at[b, i],
                device_id=sides[to],
                device_id_type=MESH,
            )
            for i, (to, src, dst) in enumerate(parts)
        ]

    def pack(ref, k, b, i, packed):
        last, first = packed
        for c in range(2):
            row_out[b][0, i, c] = ref[k, c, ROWS - HALO : ROWS, 0:COLS]
            row_out[b][1, i, c] = ref[k, c, 0:HALO, 0:COLS]
            index = 8 * i + HALO * c
            mine = jnp.logical_and(core_lane >= index, core_lane < index + HALO)
            tail = ref[k, c, 0:ROWS, COLS - 128 : COLS]
            head = ref[k, c, 0:ROWS, 0:128]
            last = jnp.where(mine, pltpu.roll(tail, lax.rem(index + HALO, 128), 1), last)
            first = jnp.where(mine, pltpu.roll(head, index, 1), first)
        return last, first

    def send_halo(b, packed):
        col_out[b, 0] = packed[0]
        col_out[b, 1] = packed[1]
        for copy in halo_copies(b):
            copy.start()

    def wait_halo(b):
        for copy in halo_copies(b):
            copy.wait_recv()
        for side in range(2):
            wide[b, side, 0:ROWS] = col_in[b, side]
            wide[b, side, ROWS : ROWS + HALO] = corner_in[b, side, 0, 0:HALO]
            wide[b, side, ROWS + HALO : HELD_ROWS] = corner_in[b, side, 1, HALO:8]

    def unpack(ref, k, b, i):
        for c in range(2):
            ref[k, c, ROWS : ROWS + HALO, 0:COLS] = row_in[b][0, i, c]
            ref[k, c, ROWS + HALO : HELD_ROWS, 0:COLS] = row_in[b][1, i, c]
            index = 8 * i + HALO * c
            after = pltpu.roll(wide[b, 1], lax.rem(128 - index, 128), 1)
            before = pltpu.roll(wide[b, 0], lax.rem(256 - HALO - index, 128), 1)
            ref[k, c, :, COLS:HELD_COLS] = jnp.where(lane < 64, after, before)

    def slopes(first, second):
        return (
            0.5 + jnp.maximum(first, 0.0),
            0.5 - jnp.minimum(first, 0.0),
            0.5 + jnp.maximum(second, 0.0),
            0.5 - jnp.minimum(second, 0.0),
        )

    def rates(ref, k):
        w = [[ref[k, c, :, lanes(j)] for c in range(2)] for j in range(TILES)]
        up = [[pltpu.roll(w[j][c], 1, 1) for c in range(2)] for j in range(TILES)]
        down = [[pltpu.roll(w[j][c], 127, 1) for c in range(2)] for j in range(TILES)]
        result = []
        for j in range(TILES):
            west_w, east_w, south_w, north_w = slopes(*w[j])
            pair = []
            for c in range(2):
                x = w[j][c]
                west = pltpu.roll(x, 1, 0)
                east = pltpu.roll(x, HELD_ROWS - 1, 0)
                south = jnp.where(lane == 0, up[j - 1][c], up[j][c])
                north = jnp.where(lane == 127, down[(j + 1) % TILES][c], down[j][c])
                pair.append(
                    west_w * (west - x)
                    + east_w * (east - x)
                    + south_w * (south - x)
                    + north_w * (north - x)
                    + F[0, c, :, lanes(j)]
                )
            result.append(pair)
        return w, result

    def each():
        return [(j, c) for j in range(TILES) for c in range(2)]

    def at(ref, k, c, j):
        return ref[k, c, :, lanes(j)]

    def put(ref, k, c, j, value):
        ref[k, c, :, lanes(j)] = value

    def landing(slot, t):
        if slot == 0:
            return out.at[1, :, rows_of(t), cols_of(t)]
        return prior.at[:, prior_rows(t), prior_cols(t)]

    def first_slot(k, t):
        away = lax.rem(lax.rem(t, 8) - lax.rem(k - 1, 8) + 8, 8)
        return jnp.where(jnp.logical_and(k < NT, jnp.logical_and(away >= 1, away <= 4)), 1, 0)

    def back(slot, k):
        return pltpu.make_async_remote_copy(
            src_ref=core(U, k),
            dst_ref=landing(slot, me),
            send_sem=ret_send.at[k],
            recv_sem=ret_recv.at[slot, me],
            device_id={"tm": k - 1 + slot},
            device_id_type=MESH,
        )

    def own(slot):
        return pltpu.make_async_copy(core(U, me + 1 - slot), landing(slot, me), ret_local.at[slot])

    def send_back(k):
        for slot in range(2):

            @pl.when(first_slot(k, me) == slot)
            def _(slot=slot):
                @pl.when(me == k - 1 + slot)
                def _():
                    own(slot).start()

                @pl.when(me != k - 1 + slot)
                def _():
                    back(slot, k).start()

    def hand_on(slot, t):
        return pltpu.make_async_remote_copy(
            src_ref=landing(slot, t),
            dst_ref=landing(1 - slot, t),
            send_sem=hand_send.at[slot, t],
            recv_sem=ret_recv.at[1 - slot, t],
            device_id={"tm": jnp.clip(me + 1 - 2 * slot, 0, NT - 1)},
            device_id_type=MESH,
        )

    def wait_landed(slot, t, local):
        if local:

            @pl.when(t == me)
            def _():
                own(slot).wait()

        @pl.when(t != me)
        def _():
            pltpu.make_async_remote_copy(
                src_ref=core(U, 1),
                dst_ref=landing(slot, t),
                send_sem=ret_send.at[1],
                recv_sem=ret_recv.at[slot, t],
                device_id={"tm": t},
                device_id_type=MESH,
            ).wait_recv()

    def near(slot, i):
        step = i // 2
        along = lax.rem(z + 8 - step, 8) if slot == 0 else lax.rem(z + step, 8)
        return lax.rem(i, 2) * 8 + along

    def far(slot, i):
        step = 1 + i // 2
        along = lax.rem(z + step, 8) if slot == 0 else lax.rem(z + 8 - step, 8)
        return lax.rem(i, 2) * 8 + along

    for copy in stage_in:
        copy.wait()
    packed = pack(S, 0, 0, 0, (blank, blank))
    send_halo(0, pack(F, 0, 0, 1, packed))

    arrivals = ((1, 1, 4), (5, 2, 4), (9, 3, 7))

    def arrive(first, b):
        def one(i, packed):
            k = first + i

            @pl.when(k - 1 != me)
            def _():
                forwarded(k - 1).wait_recv()

            return pack(S, k, b, i, packed)

        return one

    for first, b, n in arrivals:
        send_halo(b, lax.fori_loop(0, n, arrive(first, b), (blank, blank)))

    @pl.when(me != NT - 1)
    def _():
        forwarded(NT - 1).wait_recv()

    for c in range(2):
        S[NT, c, ROWS:HELD_ROWS, :] = jnp.zeros((HELD_ROWS - ROWS, HELD_COLS), jnp.float32)
        S[NT, c, 0:ROWS, COLS:HELD_COLS] = jnp.zeros((ROWS, 128), jnp.float32)

    wait_halo(0)
    unpack(S, 0, 0, 0)
    unpack(F, 0, 0, 1)

    def coarse_rhs(g, point, image, base):
        residual = g - (point - image)
        return residual + point - base

    def descend(q):
        def fine(k, relaxes):
            w, rate = rates(S, k)
            for j, c in each():
                put(R0, k, c, j, rate[j][c])
                put(T1, k, c, j, w[j][c] + STEP * rate[j][c])
            w, rate = rates(T1, k)
            for j, c in each():
                base = at(S, k, c, j) + 2 * STEP * at(R0, k, c, j)
                g = coarse_rhs(0.0, at(S, k + 1, c, j), w[j][c] + STEP * rate[j][c], base)
                put(G1, k + 1, c, j, g)
                if relaxes:
                    put(Fx, k + 1, c, j, base + g)

        def fine_pair(i, carry):
            fine(4 * q + 2 * i, True)
            fine(4 * q + 2 * i + 1, False)
            return carry

        lax.fori_loop(0, 2, fine_pair, 0)

        def second(i, carry):
            m = 2 * q + i
            k = 2 * m
            w, rate = rates(Fx, k + 1)
            for j, c in each():
                base = at(S, k, c, j) + 4 * STEP * at(R0, k, c, j)
                g = coarse_rhs(at(G1, k + 2, c, j), at(S, k + 2, c, j), w[j][c] + 2 * STEP * rate[j][c], base)
                put(G2, m + 1, c, j, g)
                put(Fx, k + 2, c, j, base + g)
            return carry

        lax.fori_loop(0, 2, second, 0)

        k = 4 * q
        w, rate = rates(Fx, k + 2)
        for j, c in each():
            base = at(S, k, c, j) + 8 * STEP * at(R0, k, c, j)
            g = coarse_rhs(at(G2, 2 * q + 2, c, j), at(S, k + 4, c, j), w[j][c] + 4 * STEP * rate[j][c], base)
            put(G3, q + 1, c, j, g)
            put(Fx, k + 4, c, j, base + g)
            if q > 0:
                continue
            put(U, k + 1, c, j, at(Fx, k + 1, c, j))
            put(U, k + 2, c, j, w[j][c])
            put(U, k + 3, c, j, w[j][c] + 2 * STEP * rate[j][c] + at(G1, k + 3, c, j))
            put(U, k + 4, c, j, base + g)

    def exchange(b, fields):
        packed = (blank, blank)
        for i, (ref, k) in enumerate(fields):
            packed = pack(ref, k, b, i, packed)
        send_halo(b, packed)

    def exchanged(b, fields):
        wait_halo(b)
        for i, (ref, k) in enumerate(fields):
            unpack(ref, k, b, i)

    def ascend(k, targets):
        w, rate = rates(U, k)
        for j, c in each():
            for point, factor, right_side, index in targets:
                put(U, point, c, j, w[j][c] + factor * STEP * rate[j][c] + at(right_side, index, c, j))

    def coarsest(k):
        w, rate = rates(Fx, k + 4)
        for j, c in each():
            base = at(S, k, c, j) + 16 * STEP * at(R0, k, c, j)
            index = (k + 8) // 4
            g = coarse_rhs(at(G3, index, c, j), at(S, k + 8, c, j), w[j][c] + 8 * STEP * rate[j][c], base)
            if k == 0:
                put(U, 8, c, j, base + g)
                put(U, 5, c, j, w[j][c] + 2 * STEP * rate[j][c] + at(G1, 5, c, j))
                put(U, 6, c, j, w[j][c] + 4 * STEP * rate[j][c] + at(G2, 3, c, j))
            else:
                put(G4, 0, c, j, g)

    def return_points(first, offsets=(3, -4, 0, -1, 2, -3, 1, -2)):
        for offset in offsets:
            send_back(first + lax.rem(z + offset + 8, 8))

    def halos_of(first, b, n):
        wait_halo(b)

        def one(i, carry):
            unpack(S, first + i, b, i)
            return carry

        lax.fori_loop(0, n, one, 0)

    fields_a = ((Fx, 4), (G3, 2))
    fields_b = ((Fx, 12), (G3, 3))
    halos_of(*arrivals[0])
    descend(0)
    halos_of(*arrivals[1])
    descend(1)
    exchange(4, fields_a)
    halos_of(*arrivals[2])
    descend(2)
    exchange(5, fields_b)
    exchanged(4, fields_a)
    coarsest(0)
    ascend(6, ((7, 2, G1, 7),))
    return_points(1)
    descend(3)
    exchanged(5, fields_b)
    coarsest(8)
    ascend(8, ((9, 2, G1, 9), (10, 4, G2, 5), (12, 8, G3, 3), (16, 16, G4, 0)))
    ascend(10, ((11, 2, G1, 11),))
    ascend(12, ((13, 2, G1, 13), (14, 4, G2, 7)))
    ascend(14, ((15, 2, G1, 15),))
    return_points(9)

    def side_edge(t):
        first = t // 8 == 0
        return pltpu.make_async_remote_copy(
            src_ref=prior.at[:, prior_rows(t), pl.ds(pl.multiple_of(jnp.where(first, 128, BLOCK_COLS), 128), 128)],
            dst_ref=prior.at[:, prior_rows(t), pl.ds(pl.multiple_of(jnp.where(first, 128 + BLOCK_COLS, 0), 128), 128)],
            send_sem=edge_send.at[t],
            recv_sem=edge_recv.at[t],
            device_id={"sy": lax.rem(sy + jnp.where(first, 7, 1), 8)},
            device_id_type=MESH,
        )

    def end_edge(t, last):
        src, dst = (BLOCK_ROWS, 0) if last else (8, 8 + BLOCK_ROWS)
        return pltpu.make_async_remote_copy(
            src_ref=prior.at[:, src : src + 8, prior_cols(t)],
            dst_ref=prior.at[:, dst : dst + 8, prior_cols(t)],
            send_sem=end_send.at[2 * (t // 8) + last],
            recv_sem=end_recv.at[2 * (t // 8) + last],
            device_id=block_sides[0],
            device_id_type=MESH,
        )

    def send_edges(t):
        side_edge(t).start()
        for last in range(2):

            @pl.when(mirrored(lax.rem(t, 8)) == 7 * last)
            def _(last=last):
                end_edge(t, last).start()

    @pl.when(me == 0)
    def _():
        def one(t, carry):
            send_edges(t)
            return carry

        copy = pltpu.make_async_copy(
            initial, prior.at[:, 8 : 8 + BLOCK_ROWS, 128 : 128 + BLOCK_COLS], ret_local.at[1]
        )
        copy.start()
        copy.wait()
        lax.fori_loop(0, NT, one, 0)

    def pass_on(i, carry):
        @pl.when(me < NT - 1)
        def _():
            wait_landed(0, near(0, i), True)
            hand_on(0, near(0, i)).start()

        @pl.when(me > 0)
        def _():
            wait_landed(1, near(1, i), True)
            hand_on(1, near(1, i)).start()
            send_edges(near(1, i))

        return carry

    lax.fori_loop(0, 8, pass_on, 0)

    def rest(slot):
        def one(i, carry):
            wait_landed(slot, far(slot, i), False)
            if slot == 1:
                send_edges(far(slot, i))
            return carry

        lax.fori_loop(0, 8, one, 0)

    @pl.when(me > 0)
    def _():
        rest(1)

    block_tiles = BLOCK_COLS // 128

    def last_step(i, carry):
        along = lax.rem(z + jnp.where(i < 4, i, 11 - i), 8)
        g = mirrored(along)
        side_edge(along).wait_recv()
        side_edge(8 + along).wait_recv()
        for last in range(2):

            @pl.when(g == 7 - 7 * last)
            def _(last=last):
                end_edge(0, last).wait_recv()
                end_edge(8, last).wait_recv()

        around = pl.ds(pl.multiple_of(g * ROWS, ROWS), ROWS + 16)
        rows = pl.ds(pl.multiple_of(g * ROWS, ROWS), ROWS)
        inner = pl.ds(pl.multiple_of(8 + g * ROWS, 8), ROWS)
        y = [[prior[c, around, lanes(j + 1)] for c in range(2)] for j in range(block_tiles)]
        w = [[y[j][c][8 : 8 + ROWS] for c in range(2)] for j in range(block_tiles)]
        up = [[pltpu.roll(w[j][c], 1, 1) for c in range(2)] for j in range(block_tiles)]
        down = [[pltpu.roll(w[j][c], 127, 1) for c in range(2)] for j in range(block_tiles)]
        before = [pltpu.roll(prior[c, inner, lanes(0)], 1, 1) for c in range(2)]
        after = [pltpu.roll(prior[c, inner, lanes(block_tiles + 1)], 127, 1) for c in range(2)]
        for j in range(block_tiles):
            west_w, east_w, south_w, north_w = slopes(*w[j])
            for c in range(2):
                x = w[j][c]
                west = pltpu.roll(y[j][c], 1, 0)[8 : 8 + ROWS]
                east = pltpu.roll(y[j][c], ROWS + 15, 0)[8 : 8 + ROWS]
                south = jnp.where(core_lane == 0, up[j - 1][c] if j > 0 else before[c], up[j][c])
                north = jnp.where(core_lane == 127, down[j + 1][c] if j < block_tiles - 1 else after[c], down[j][c])
                rate = (
                    west_w * (west - x)
                    + east_w * (east - x)
                    + south_w * (south - x)
                    + north_w * (north - x)
                    + block_forcing[c, rows, lanes(j)]
                )
                out[0, c, rows, lanes(j)] = x + STEP * rate
        return carry

    load.wait()
    lax.fori_loop(0, 8, last_step, 0)

    for b in range(NB):
        for copy in halo_copies(b):
            copy.wait_send()
    def finish_edges(t, c):
        side_edge(t).wait_send()
        return c

    lax.fori_loop(0, NT, finish_edges, 0)
    for t in (0, 8):
        for last in range(2):
            end_edge(t, last).wait_send()

    def finish(i, c):
        @pl.when(i != me)
        def _():
            forward(i).wait_send()

        k = i + 1
        for slot in range(2):

            @pl.when(jnp.logical_and(first_slot(k, me) == slot, me != k - 1 + slot))
            def _(slot=slot):
                back(slot, k).wait_send()

        return c

    lax.fori_loop(0, NT, finish, 0)

    def finish_handed(i, c):
        @pl.when(me < NT - 1)
        def _():
            hand_on(0, near(0, i)).wait_send()

        @pl.when(me > 0)
        def _():
            hand_on(1, near(1, i)).wait_send()

        return c

    lax.fori_loop(0, 8, finish_handed, 0)

    @pl.when(me < NT - 1)
    def _():
        rest(0)

    @pl.when(me == NT - 1)
    def _():
        def one(t, c):
            wait_landed(0, t, True)
            return c

        lax.fori_loop(0, NT, one, 0)


def body(initial, forcing, guess):
    f32 = jnp.float32

    def field(n):
        return pltpu.VMEM((n, 2, HELD_ROWS, HELD_COLS), f32)

    scratch = [field(n) for n in (17, 1, 16, 16, 17, 9, 5, 1, 17, 17)]
    scratch += [
        pltpu.VMEM((2, BLOCK_ROWS + 16, BLOCK_COLS + 256), f32),
        pltpu.VMEM((2, BLOCK_ROWS, BLOCK_COLS), f32),
        pltpu.VMEM((NB, 2, ROWS, 128), f32),
        pltpu.VMEM((NB, 2, ROWS, 128), f32),
        pltpu.VMEM((NB, 2, 2, 8, 128), f32),
        pltpu.VMEM((NB, 2, HELD_ROWS, 128), f32),
    ]
    for _ in range(2):
        scratch += [pltpu.VMEM((2, n, 2, HALO, COLS), f32) for n in BATCH]
    dma = pltpu.SemaphoreType.DMA
    scratch += [dma((4,)), dma((NT,)), dma((NT,)), dma((NB, 8)), dma((NB, 8)), dma((NT + 1,)), dma((2, NT)), dma((2,))]
    scratch += [dma((2, NT)), dma((NT,)), dma((NT,)), dma((4,)), dma((4,))]
    spec = pl.BlockSpec(memory_space=pltpu.HBM)
    return pl.pallas_call(
        kernel,
        out_shape=pltpu.VMEM((2, 2, BLOCK_ROWS, BLOCK_COLS), f32),
        in_specs=[spec] * 3,
        out_specs=pl.BlockSpec(memory_space=pltpu.VMEM),
        scratch_shapes=scratch,
        compiler_params=pltpu.CompilerParams(
            collective_id=0, has_side_effects=True, vmem_limit_bytes=32 * 1024 * 1024
        ),
        name="cycle",
    )(*(pltpu.with_memory_space_constraint(x, pltpu.HBM) for x in (initial, forcing, guess)))


def solution(mesh):
    in_specs = (P(None, "sx", "sy"), P(None, "sx", "sy"), P("tm", None, "sx", "sy"))
    out_specs = P("tm", None, "sx", "sy")
    return jax.shard_map(body, mesh=mesh, in_specs=in_specs, out_specs=out_specs, check_vma=False)
```

```python
import jax
import jax.numpy as jnp
from jax import lax
from jax.experimental import pallas as pl
from jax.experimental.pallas import tpu as pltpu
from jax.sharding import PartitionSpec as P

VISCOSITY = 0.5
COURANT = 0.7
MESH = pl.DeviceIdType.MESH
NT = 16
BLOCK_ROWS, BLOCK_COLS = 256, 512
ROWS, COLS = 32, 256
HALO = 4
HELD_ROWS, HELD_COLS = ROWS + 2 * HALO, COLS + 128
TILES = HELD_COLS // 128
STEP = COURANT / (NT * (2.0 + 4.0 * VISCOSITY))
BATCH = (2, 4, 4, 7, 2, 2)
NB = len(BATCH)
UP, DOWN, RIGHT, LEFT, UP_RIGHT, DOWN_RIGHT, UP_LEFT, DOWN_LEFT = range(8)


def kernel(initial, forcing, guess, out, *scratch):
    (S, F, R0, T1, G1, G2, G3, G4, Fx, U, prior, block_forcing, col_out, col_in, corner_in, wide) = scratch[:16]
    row_out = scratch[16 : 16 + NB]
    row_in = scratch[16 + NB : 16 + 2 * NB]
    (local_sem, fwd_send, fwd_recv, halo_send, halo_recv, ret_send, ret_recv, ret_local, hand_send, edge_send, edge_recv, end_send, end_recv) = (
        scratch[16 + 2 * NB :]
    )

    me = lax.axis_index("tm")
    sx = lax.axis_index("sx")
    sy = lax.axis_index("sy")
    xl = me // 8
    z = lax.rem(me, 8)

    def mirrored(i):
        return jnp.where(sx == 0, i, 7 - i)

    zz = mirrored(z)

    def beside(vertical, horizontal):
        if vertical == 0:
            nz, nsx = z, sx
        elif vertical == 1:
            nz, nsx = jnp.where(zz < 7, mirrored(zz + 1), z), jnp.where(zz < 7, sx, 1 - sx)
        else:
            nz, nsx = jnp.where(zz > 0, mirrored(zz - 1), z), jnp.where(zz > 0, sx, 1 - sx)
        if horizontal == 0:
            nx, nsy = xl, sy
        elif horizontal == 1:
            nx, nsy = 1 - xl, jnp.where(xl == 0, sy, lax.rem(sy + 1, 8))
        else:
            nx, nsy = 1 - xl, jnp.where(xl == 1, sy, lax.rem(sy + 7, 8))
        return {"tm": nx * 8 + nz, "sx": nsx, "sy": nsy}

    sides = [beside(*v) for v in ((1, 0), (-1, 0), (0, 1), (0, -1), (1, 1), (-1, 1), (1, -1), (-1, -1))]
    block_sides = [{"sx": 1 - sx}, {"sy": lax.rem(sy + 1, 8)}, {"sy": lax.rem(sy + 7, 8)}]

    def rows_of(t):
        return pl.ds(pl.multiple_of(mirrored(lax.rem(t, 8)) * ROWS, ROWS), ROWS)

    def cols_of(t):
        return pl.ds(pl.multiple_of((t // 8) * COLS, COLS), COLS)

    own_rows, own_cols = rows_of(me), cols_of(me)

    def prior_rows(t):
        return pl.ds(pl.multiple_of(8 + mirrored(lax.rem(t, 8)) * ROWS, 8), ROWS)

    def prior_cols(t):
        return pl.ds(pl.multiple_of(128 + (t // 8) * COLS, 128), COLS)

    def core(ref, k):
        return ref.at[k, :, 0:ROWS, 0:COLS]

    barrier = pltpu.get_barrier_semaphore()

    def greet(d, c):
        pl.semaphore_signal(barrier, inc=1, device_id={"tm": lax.rem(me + d, NT)}, device_id_type=MESH)
        return c

    lax.fori_loop(1, NT, greet, 0)
    for side in sides + block_sides:
        pl.semaphore_signal(barrier, inc=1, device_id=side, device_id_type=MESH)

    stage_in = [
        pltpu.make_async_copy(initial.at[:, own_rows, own_cols], core(S, 0), local_sem.at[0]),
        pltpu.make_async_copy(forcing.at[:, own_rows, own_cols], core(F, 0), local_sem.at[1]),
        pltpu.make_async_copy(guess.at[0, :, own_rows, own_cols], core(S, me + 1), local_sem.at[2]),
    ]
    for copy in stage_in:
        copy.start()
    pl.semaphore_wait(barrier, NT - 1 + 8 + 3)

    def forward(peer):
        return pltpu.make_async_remote_copy(
            src_ref=guess.at[0, :, rows_of(peer), cols_of(peer)],
            dst_ref=core(S, me + 1),
            send_sem=fwd_send.at[peer],
            recv_sem=fwd_recv.at[me],
            device_id={"tm": peer},
            device_id_type=MESH,
        )

    def forwarded(peer):
        return pltpu.make_async_remote_copy(
            src_ref=guess.at[0, :, own_rows, own_cols],
            dst_ref=core(S, peer + 1),
            send_sem=fwd_send.at[peer],
            recv_sem=fwd_recv.at[peer],
            device_id={"tm": peer},
            device_id_type=MESH,
        )

    def start_forward(d, c):
        forward(lax.rem(me + d, NT)).start()
        return c

    forward(lax.rem(xl + 1, 2) * 8 + lax.rem(z + 4, 8)).start()
    forward(lax.rem(xl + 0, 2) * 8 + lax.rem(z + 4, 8)).start()
    forward(lax.rem(xl + 1, 2) * 8 + lax.rem(z + 1, 8)).start()
    forward(lax.rem(xl + 1, 2) * 8 + lax.rem(z + 7, 8)).start()
    forward(lax.rem(xl + 1, 2) * 8 + lax.rem(z + 3, 8)).start()
    forward(lax.rem(xl + 1, 2) * 8 + lax.rem(z + 5, 8)).start()
    forward(lax.rem(xl + 0, 2) * 8 + lax.rem(z + 1, 8)).start()
    forward(lax.rem(xl + 0, 2) * 8 + lax.rem(z + 7, 8)).start()
    forward(lax.rem(xl + 0, 2) * 8 + lax.rem(z + 3, 8)).start()
    forward(lax.rem(xl + 0, 2) * 8 + lax.rem(z + 5, 8)).start()
    forward(lax.rem(xl + 1, 2) * 8 + lax.rem(z + 2, 8)).start()
    forward(lax.rem(xl + 1, 2) * 8 + lax.rem(z + 6, 8)).start()
    forward(lax.rem(xl + 0, 2) * 8 + lax.rem(z + 2, 8)).start()
    forward(lax.rem(xl + 0, 2) * 8 + lax.rem(z + 6, 8)).start()
    forward(lax.rem(xl + 1, 2) * 8 + lax.rem(z + 0, 8)).start()
    load = pltpu.make_async_copy(forcing, block_forcing, local_sem.at[3])
    load.start()

    lane = lax.broadcasted_iota(jnp.int32, (HELD_ROWS, 128), 1)
    core_lane = lax.broadcasted_iota(jnp.int32, (ROWS, 128), 1)
    blank = jnp.zeros((ROWS, 128), jnp.float32)

    def lanes(j):
        return slice(128 * j, 128 * (j + 1))

    def halo_copies(b):
        parts = (
            (UP, row_out[b].at[0], row_in[b].at[1]),
            (DOWN, row_out[b].at[1], row_in[b].at[0]),
            (RIGHT, col_out.at[b, 0], col_in.at[b, 0]),
            (LEFT, col_out.at[b, 1], col_in.at[b, 1]),
            (DOWN_RIGHT, col_out.at[b, 0, 0:8], corner_in.at[b, 0, 0]),
            (UP_RIGHT, col_out.at[b, 0, ROWS - 8 : ROWS], corner_in.at[b, 0, 1]),
            (DOWN_LEFT, col_out.at[b, 1, 0:8], corner_in.at[b, 1, 0]),
            (UP_LEFT, col_out.at[b, 1, ROWS - 8 : ROWS], corner_in.at[b, 1, 1]),
        )
        return [
            pltpu.make_async_remote_copy(
                src_ref=src,
                dst_ref=dst,
                send_sem=halo_send.at[b, i],
                recv_sem=halo_recv.at[b, i],
                device_id=sides[to],
                device_id_type=MESH,
            )
            for i, (to, src, dst) in enumerate(parts)
        ]

    def pack(ref, k, b, i, packed):
        last, first = packed
        for c in range(2):
            row_out[b][0, i, c] = ref[k, c, ROWS - HALO : ROWS, 0:COLS]
            row_out[b][1, i, c] = ref[k, c, 0:HALO, 0:COLS]
            index = 8 * i + HALO * c
            mine = jnp.logical_and(core_lane >= index, core_lane < index + HALO)
            tail = ref[k, c, 0:ROWS, COLS - 128 : COLS]
            head = ref[k, c, 0:ROWS, 0:128]
            last = jnp.where(mine, pltpu.roll(tail, lax.rem(index + HALO, 128), 1), last)
            first = jnp.where(mine, pltpu.roll(head, index, 1), first)
        return last, first

    def send_halo(b, packed):
        col_out[b, 0] = packed[0]
        col_out[b, 1] = packed[1]
        for copy in halo_copies(b):
            copy.start()

    def wait_halo(b):
        for copy in halo_copies(b):
            copy.wait_recv()
        for side in range(2):
            wide[b, side, 0:ROWS] = col_in[b, side]
            wide[b, side, ROWS : ROWS + HALO] = corner_in[b, side, 0, 0:HALO]
            wide[b, side, ROWS + HALO : HELD_ROWS] = corner_in[b, side, 1, HALO:8]

    def unpack(ref, k, b, i):
        for c in range(2):
            ref[k, c, ROWS : ROWS + HALO, 0:COLS] = row_in[b][0, i, c]
            ref[k, c, ROWS + HALO : HELD_ROWS, 0:COLS] = row_in[b][1, i, c]
            index = 8 * i + HALO * c
            after = pltpu.roll(wide[b, 1], lax.rem(128 - index, 128), 1)
            before = pltpu.roll(wide[b, 0], lax.rem(256 - HALO - index, 128), 1)
            ref[k, c, :, COLS:HELD_COLS] = jnp.where(lane < 64, after, before)

    def slopes(first, second):
        return (
            0.5 + jnp.maximum(first, 0.0),
            0.5 - jnp.minimum(first, 0.0),
            0.5 + jnp.maximum(second, 0.0),
            0.5 - jnp.minimum(second, 0.0),
        )

    def rates(ref, k):
        w = [[ref[k, c, :, lanes(j)] for c in range(2)] for j in range(TILES)]
        up = [[pltpu.roll(w[j][c], 1, 1) for c in range(2)] for j in range(TILES)]
        down = [[pltpu.roll(w[j][c], 127, 1) for c in range(2)] for j in range(TILES)]
        result = []
        for j in range(TILES):
            west_w, east_w, south_w, north_w = slopes(*w[j])
            pair = []
            for c in range(2):
                x = w[j][c]
                west = pltpu.roll(x, 1, 0)
                east = pltpu.roll(x, HELD_ROWS - 1, 0)
                south = jnp.where(lane == 0, up[j - 1][c], up[j][c])
                north = jnp.where(lane == 127, down[(j + 1) % TILES][c], down[j][c])
                pair.append(
                    west_w * (west - x)
                    + east_w * (east - x)
                    + south_w * (south - x)
                    + north_w * (north - x)
                    + F[0, c, :, lanes(j)]
                )
            result.append(pair)
        return w, result

    def each(halo=True):
        return [(j, c) for j in range(TILES if halo else TILES - 1) for c in range(2)]

    def at(ref, k, c, j):
        return ref[k, c, :, lanes(j)]

    def put(ref, k, c, j, value):
        ref[k, c, :, lanes(j)] = value

    def landing(slot, t):
        if slot == 0:
            return out.at[1, :, rows_of(t), cols_of(t)]
        return prior.at[:, prior_rows(t), prior_cols(t)]

    def first_slot(k, t):
        away = lax.rem(lax.rem(t, 8) - lax.rem(k - 1, 8) + 8, 8)
        return jnp.where(jnp.logical_and(k < NT, jnp.logical_and(away >= 1, away <= 4)), 1, 0)

    def back(slot, k):
        return pltpu.make_async_remote_copy(
            src_ref=core(U, k),
            dst_ref=landing(slot, me),
            send_sem=ret_send.at[k],
            recv_sem=ret_recv.at[slot, me],
            device_id={"tm": k - 1 + slot},
            device_id_type=MESH,
        )

    def own(slot):
        return pltpu.make_async_copy(core(U, me + 1 - slot), landing(slot, me), ret_local.at[slot])

    def send_back(k):
        for slot in range(2):

            @pl.when(first_slot(k, me) == slot)
            def _(slot=slot):
                @pl.when(me == k - 1 + slot)
                def _():
                    own(slot).start()

                @pl.when(me != k - 1 + slot)
                def _():
                    back(slot, k).start()

    def hand_on(slot, t):
        return pltpu.make_async_remote_copy(
            src_ref=landing(slot, t),
            dst_ref=landing(1 - slot, t),
            send_sem=hand_send.at[slot, t],
            recv_sem=ret_recv.at[1 - slot, t],
            device_id={"tm": jnp.clip(me + 1 - 2 * slot, 0, NT - 1)},
            device_id_type=MESH,
        )

    def wait_landed(slot, t, local):
        if local:

            @pl.when(t == me)
            def _():
                own(slot).wait()

        @pl.when(t != me)
        def _():
            pltpu.make_async_remote_copy(
                src_ref=core(U, 1),
                dst_ref=landing(slot, t),
                send_sem=ret_send.at[1],
                recv_sem=ret_recv.at[slot, t],
                device_id={"tm": t},
                device_id_type=MESH,
            ).wait_recv()

    def near(slot, i):
        step = i // 2
        along = lax.rem(z + 8 - step, 8) if slot == 0 else lax.rem(z + step, 8)
        return lax.rem(i, 2) * 8 + along

    def far(slot, i):
        step = 1 + i // 2
        along = lax.rem(z + step, 8) if slot == 0 else lax.rem(z + 8 - step, 8)
        return lax.rem(i, 2) * 8 + along

    for copy in stage_in:
        copy.wait()
    packed = pack(S, 0, 0, 0, (blank, blank))
    send_halo(0, pack(F, 0, 0, 1, packed))

    arrivals = ((1, 1, 4), (5, 2, 4), (9, 3, 7))

    def arrive(first, b):
        def one(i, packed):
            k = first + i

            @pl.when(k - 1 != me)
            def _():
                forwarded(k - 1).wait_recv()

            return pack(S, k, b, i, packed)

        return one

    for first, b, n in arrivals:
        send_halo(b, lax.fori_loop(0, n, arrive(first, b), (blank, blank)))

    @pl.when(me != NT - 1)
    def _():
        forwarded(NT - 1).wait_recv()

    for c in range(2):
        S[NT, c, ROWS:HELD_ROWS, :] = jnp.zeros((HELD_ROWS - ROWS, HELD_COLS), jnp.float32)
        S[NT, c, 0:ROWS, COLS:HELD_COLS] = jnp.zeros((ROWS, 128), jnp.float32)

    wait_halo(0)
    unpack(S, 0, 0, 0)
    unpack(F, 0, 0, 1)

    def coarse_rhs(g, point, image, base):
        residual = g - (point - image)
        return residual + point - base

    def fine(k, relaxes):
        w, rate = rates(S, k)
        for j, c in each():
            put(R0, k, c, j, rate[j][c])
            put(T1, k, c, j, w[j][c] + STEP * rate[j][c])
        w, rate = rates(T1, k)
        for j, c in each():
            base = at(S, k, c, j) + 2 * STEP * at(R0, k, c, j)
            g = coarse_rhs(0.0, at(S, k + 1, c, j), w[j][c] + STEP * rate[j][c], base)
            put(G1, k + 1, c, j, g)
            if relaxes:
                put(Fx, k + 1, c, j, base + g)

    def descend(q):
        def fine_pair(i, carry):
            fine(4 * q + 2 * i, True)
            fine(4 * q + 2 * i + 1, False)
            return carry

        if q == 0:
            fine(1, False)
        lax.fori_loop(0 if q > 0 else 1, 2, fine_pair, 0)

        def second(i, carry):
            m = 2 * q + i
            k = 2 * m
            w, rate = rates(Fx, k + 1)
            for j, c in each():
                base = at(S, k, c, j) + 4 * STEP * at(R0, k, c, j)
                g = coarse_rhs(at(G1, k + 2, c, j), at(S, k + 2, c, j), w[j][c] + 2 * STEP * rate[j][c], base)
                put(G2, m + 1, c, j, g)
                put(Fx, k + 2, c, j, base + g)
            return carry

        lax.fori_loop(0, 2, second, 0)

        k = 4 * q
        w, rate = rates(Fx, k + 2)
        for j, c in each(halo=False):
            base = at(S, k, c, j) + 8 * STEP * at(R0, k, c, j)
            g = coarse_rhs(at(G2, 2 * q + 2, c, j), at(S, k + 4, c, j), w[j][c] + 4 * STEP * rate[j][c], base)
            put(G3, q + 1, c, j, g)
            put(Fx, k + 4, c, j, base + g)
            if q > 0:
                continue
            put(U, k + 1, c, j, at(Fx, k + 1, c, j))
            put(U, k + 2, c, j, w[j][c])
            put(U, k + 3, c, j, w[j][c] + 2 * STEP * rate[j][c] + at(G1, k + 3, c, j))
            put(U, k + 4, c, j, base + g)

    def exchange(b, fields):
        packed = (blank, blank)
        for i, (ref, k) in enumerate(fields):
            packed = pack(ref, k, b, i, packed)
        send_halo(b, packed)

    def exchanged(b, fields):
        wait_halo(b)
        for i, (ref, k) in enumerate(fields):
            unpack(ref, k, b, i)

    def ascend(k, targets, halo=True):
        w, rate = rates(U, k)
        for j, c in each(halo):
            for point, factor, right_side, index in targets:
                put(U, point, c, j, w[j][c] + factor * STEP * rate[j][c] + at(right_side, index, c, j))

    def coarsest(k):
        w, rate = rates(Fx, k + 4)
        for j, c in each(halo=k == 0):
            base = at(S, k, c, j) + 16 * STEP * at(R0, k, c, j)
            index = (k + 8) // 4
            g = coarse_rhs(at(G3, index, c, j), at(S, k + 8, c, j), w[j][c] + 8 * STEP * rate[j][c], base)
            if k == 0:
                put(U, 8, c, j, base + g)
                put(U, 5, c, j, w[j][c] + 2 * STEP * rate[j][c] + at(G1, 5, c, j))
                put(U, 6, c, j, w[j][c] + 4 * STEP * rate[j][c] + at(G2, 3, c, j))
            else:
                put(G4, 0, c, j, g)

    def return_points(first, offsets=(3, -4, 0, -1, 2, -3, 1, -2)):
        for offset in offsets:
            send_back(first + lax.rem(z + offset + 8, 8))

    def halos_of(first, b, n):
        wait_halo(b)

        def one(i, carry):
            unpack(S, first + i, b, i)
            return carry

        lax.fori_loop(0, n, one, 0)

    fields_a = ((Fx, 4), (G3, 2))
    fields_b = ((Fx, 12), (G3, 3))
    fine(0, True)
    halos_of(*arrivals[0])
    descend(0)
    halos_of(*arrivals[1])
    descend(1)
    exchange(4, fields_a)
    halos_of(*arrivals[2])
    descend(2)
    exchange(5, fields_b)
    exchanged(4, fields_a)
    coarsest(0)
    ascend(6, ((7, 2, G1, 7),), halo=False)
    return_points(1)
    descend(3)
    exchanged(5, fields_b)
    coarsest(8)
    ascend(8, ((9, 2, G1, 9), (10, 4, G2, 5), (12, 8, G3, 3), (16, 16, G4, 0)))
    ascend(10, ((11, 2, G1, 11),), halo=False)
    ascend(12, ((13, 2, G1, 13), (14, 4, G2, 7)))
    ascend(14, ((15, 2, G1, 15),), halo=False)
    return_points(9)

    def side_edge(t):
        first = t // 8 == 0
        return pltpu.make_async_remote_copy(
            src_ref=prior.at[:, prior_rows(t), pl.ds(pl.multiple_of(jnp.where(first, 128, BLOCK_COLS), 128), 128)],
            dst_ref=prior.at[:, prior_rows(t), pl.ds(pl.multiple_of(jnp.where(first, 128 + BLOCK_COLS, 0), 128), 128)],
            send_sem=edge_send.at[t],
            recv_sem=edge_recv.at[t],
            device_id={"sy": lax.rem(sy + jnp.where(first, 7, 1), 8)},
            device_id_type=MESH,
        )

    def end_edge(t, last):
        src, dst = (BLOCK_ROWS, 0) if last else (8, 8 + BLOCK_ROWS)
        return pltpu.make_async_remote_copy(
            src_ref=prior.at[:, src : src + 8, prior_cols(t)],
            dst_ref=prior.at[:, dst : dst + 8, prior_cols(t)],
            send_sem=end_send.at[2 * (t // 8) + last],
            recv_sem=end_recv.at[2 * (t // 8) + last],
            device_id=block_sides[0],
            device_id_type=MESH,
        )

    def send_edges(t):
        side_edge(t).start()
        for last in range(2):

            @pl.when(mirrored(lax.rem(t, 8)) == 7 * last)
            def _(last=last):
                end_edge(t, last).start()

    @pl.when(me == 0)
    def _():
        def one(t, carry):
            send_edges(t)
            return carry

        copy = pltpu.make_async_copy(
            initial, prior.at[:, 8 : 8 + BLOCK_ROWS, 128 : 128 + BLOCK_COLS], ret_local.at[1]
        )
        copy.start()
        copy.wait()
        lax.fori_loop(0, NT, one, 0)

    def pass_on(i, carry):
        @pl.when(me < NT - 1)
        def _():
            wait_landed(0, near(0, i), True)
            hand_on(0, near(0, i)).start()

        @pl.when(me > 0)
        def _():
            wait_landed(1, near(1, i), True)
            hand_on(1, near(1, i)).start()
            send_edges(near(1, i))

        return carry

    lax.fori_loop(0, 8, pass_on, 0)

    def rest(slot):
        def one(i, carry):
            wait_landed(slot, far(slot, i), False)
            if slot == 1:
                send_edges(far(slot, i))
            return carry

        lax.fori_loop(0, 8, one, 0)

    @pl.when(me > 0)
    def _():
        rest(1)

    block_tiles = BLOCK_COLS // 128

    def last_step(i, carry):
        along = lax.rem(z + jnp.where(i < 4, i, 11 - i), 8)
        g = mirrored(along)
        side_edge(along).wait_recv()
        side_edge(8 + along).wait_recv()
        for last in range(2):

            @pl.when(g == 7 - 7 * last)
            def _(last=last):
                end_edge(0, last).wait_recv()
                end_edge(8, last).wait_recv()

        around = pl.ds(pl.multiple_of(g * ROWS, ROWS), ROWS + 16)
        rows = pl.ds(pl.multiple_of(g * ROWS, ROWS), ROWS)
        inner = pl.ds(pl.multiple_of(8 + g * ROWS, 8), ROWS)
        y = [[prior[c, around, lanes(j + 1)] for c in range(2)] for j in range(block_tiles)]
        w = [[y[j][c][8 : 8 + ROWS] for c in range(2)] for j in range(block_tiles)]
        up = [[pltpu.roll(w[j][c], 1, 1) for c in range(2)] for j in range(block_tiles)]
        down = [[pltpu.roll(w[j][c], 127, 1) for c in range(2)] for j in range(block_tiles)]
        before = [pltpu.roll(prior[c, inner, lanes(0)], 1, 1) for c in range(2)]
        after = [pltpu.roll(prior[c, inner, lanes(block_tiles + 1)], 127, 1) for c in range(2)]
        for j in range(block_tiles):
            west_w, east_w, south_w, north_w = slopes(*w[j])
            for c in range(2):
                x = w[j][c]
                west = pltpu.roll(y[j][c], 1, 0)[8 : 8 + ROWS]
                east = pltpu.roll(y[j][c], ROWS + 15, 0)[8 : 8 + ROWS]
                south = jnp.where(core_lane == 0, up[j - 1][c] if j > 0 else before[c], up[j][c])
                north = jnp.where(core_lane == 127, down[j + 1][c] if j < block_tiles - 1 else after[c], down[j][c])
                rate = (
                    west_w * (west - x)
                    + east_w * (east - x)
                    + south_w * (south - x)
                    + north_w * (north - x)
                    + block_forcing[c, rows, lanes(j)]
                )
                out[0, c, rows, lanes(j)] = x + STEP * rate
        return carry

    load.wait()
    lax.fori_loop(0, 8, last_step, 0)

    for b in range(NB):
        for copy in halo_copies(b):
            copy.wait_send()
    def finish_edges(t, c):
        side_edge(t).wait_send()
        return c

    lax.fori_loop(0, NT, finish_edges, 0)
    for t in (0, 8):
        for last in range(2):
            end_edge(t, last).wait_send()

    def finish(i, c):
        @pl.when(i != me)
        def _():
            forward(i).wait_send()

        k = i + 1
        for slot in range(2):

            @pl.when(jnp.logical_and(first_slot(k, me) == slot, me != k - 1 + slot))
            def _(slot=slot):
                back(slot, k).wait_send()

        return c

    lax.fori_loop(0, NT, finish, 0)

    def finish_handed(i, c):
        @pl.when(me < NT - 1)
        def _():
            hand_on(0, near(0, i)).wait_send()

        @pl.when(me > 0)
        def _():
            hand_on(1, near(1, i)).wait_send()

        return c

    lax.fori_loop(0, 8, finish_handed, 0)

    @pl.when(me < NT - 1)
    def _():
        rest(0)

    @pl.when(me == NT - 1)
    def _():
        def one(t, c):
            wait_landed(0, t, True)
            return c

        lax.fori_loop(0, NT, one, 0)


def body(initial, forcing, guess):
    f32 = jnp.float32

    def field(n):
        return pltpu.VMEM((n, 2, HELD_ROWS, HELD_COLS), f32)

    scratch = [field(n) for n in (17, 1, 16, 16, 17, 9, 5, 1, 17, 17)]
    scratch += [
        pltpu.VMEM((2, BLOCK_ROWS + 16, BLOCK_COLS + 256), f32),
        pltpu.VMEM((2, BLOCK_ROWS, BLOCK_COLS), f32),
        pltpu.VMEM((NB, 2, ROWS, 128), f32),
        pltpu.VMEM((NB, 2, ROWS, 128), f32),
        pltpu.VMEM((NB, 2, 2, 8, 128), f32),
        pltpu.VMEM((NB, 2, HELD_ROWS, 128), f32),
    ]
    for _ in range(2):
        scratch += [pltpu.VMEM((2, n, 2, HALO, COLS), f32) for n in BATCH]
    dma = pltpu.SemaphoreType.DMA
    scratch += [dma((4,)), dma((NT,)), dma((NT,)), dma((NB, 8)), dma((NB, 8)), dma((NT + 1,)), dma((2, NT)), dma((2,))]
    scratch += [dma((2, NT)), dma((NT,)), dma((NT,)), dma((4,)), dma((4,))]
    spec = pl.BlockSpec(memory_space=pltpu.HBM)
    return pl.pallas_call(
        kernel,
        out_shape=pltpu.VMEM((2, 2, BLOCK_ROWS, BLOCK_COLS), f32),
        in_specs=[spec] * 3,
        out_specs=pl.BlockSpec(memory_space=pltpu.VMEM),
        scratch_shapes=scratch,
        compiler_params=pltpu.CompilerParams(
            collective_id=0, has_side_effects=True, vmem_limit_bytes=32 * 1024 * 1024
        ),
        name="cycle",
    )(*(pltpu.with_memory_space_constraint(x, pltpu.HBM) for x in (initial, forcing, guess)))


def solution(mesh):
    in_specs = (P(None, "sx", "sy"), P(None, "sx", "sy"), P("tm", None, "sx", "sy"))
    out_specs = P("tm", None, "sx", "sy")
    return jax.shard_map(body, mesh=mesh, in_specs=in_specs, out_specs=out_specs, check_vma=False)
```

```python
import jax
import jax.numpy as jnp
from jax import lax
from jax.experimental import pallas as pl
from jax.experimental.pallas import tpu as pltpu
from jax.sharding import PartitionSpec as P

VISCOSITY = 0.5
COURANT = 0.7
MESH = pl.DeviceIdType.MESH
NT = 16
BLOCK_ROWS, BLOCK_COLS = 256, 512
ROWS, COLS = 32, 256
HALO = 4
HELD_ROWS, HELD_COLS = ROWS + 2 * HALO, COLS + 128
TILES = HELD_COLS // 128
STEP = COURANT / (NT * (2.0 + 4.0 * VISCOSITY))
BATCH = (2, 4, 4, 7, 2, 2)
NB = len(BATCH)
UP, DOWN, RIGHT, LEFT, UP_RIGHT, DOWN_RIGHT, UP_LEFT, DOWN_LEFT = range(8)


def kernel(initial, forcing, guess, out, *scratch):
    (S, F, R0, T1, G1, G2, G3, G4, Fx, U, prior, block_forcing, col_out, col_in, corner_in, wide) = scratch[:16]
    row_out = scratch[16 : 16 + NB]
    row_in = scratch[16 + NB : 16 + 2 * NB]
    (local_sem, fwd_send, fwd_recv, halo_send, halo_recv, ret_send, ret_recv, ret_local, hand_send, edge_send, edge_recv, end_send, end_recv) = (
        scratch[16 + 2 * NB :]
    )

    me = lax.axis_index("tm")
    sx = lax.axis_index("sx")
    sy = lax.axis_index("sy")
    xl = me // 8
    z = lax.rem(me, 8)

    def mirrored(i):
        return jnp.where(sx == 0, i, 7 - i)

    zz = mirrored(z)

    def beside(vertical, horizontal):
        if vertical == 0:
            nz, nsx = z, sx
        elif vertical == 1:
            nz, nsx = jnp.where(zz < 7, mirrored(zz + 1), z), jnp.where(zz < 7, sx, 1 - sx)
        else:
            nz, nsx = jnp.where(zz > 0, mirrored(zz - 1), z), jnp.where(zz > 0, sx, 1 - sx)
        if horizontal == 0:
            nx, nsy = xl, sy
        elif horizontal == 1:
            nx, nsy = 1 - xl, jnp.where(xl == 0, sy, lax.rem(sy + 1, 8))
        else:
            nx, nsy = 1 - xl, jnp.where(xl == 1, sy, lax.rem(sy + 7, 8))
        return {"tm": nx * 8 + nz, "sx": nsx, "sy": nsy}

    sides = [beside(*v) for v in ((1, 0), (-1, 0), (0, 1), (0, -1), (1, 1), (-1, 1), (1, -1), (-1, -1))]
    block_sides = [{"sx": 1 - sx}, {"sy": lax.rem(sy + 1, 8)}, {"sy": lax.rem(sy + 7, 8)}]

    def rows_of(t):
        return pl.ds(pl.multiple_of(mirrored(lax.rem(t, 8)) * ROWS, ROWS), ROWS)

    def cols_of(t):
        return pl.ds(pl.multiple_of((t // 8) * COLS, COLS), COLS)

    own_rows, own_cols = rows_of(me), cols_of(me)

    def prior_rows(t):
        return pl.ds(pl.multiple_of(8 + mirrored(lax.rem(t, 8)) * ROWS, 8), ROWS)

    def prior_cols(t):
        return pl.ds(pl.multiple_of(128 + (t // 8) * COLS, 128), COLS)

    def core(ref, k):
        return ref.at[k, :, 0:ROWS, 0:COLS]

    barrier = pltpu.get_barrier_semaphore()

    def greet(d, c):
        pl.semaphore_signal(barrier, inc=1, device_id={"tm": lax.rem(me + d, NT)}, device_id_type=MESH)
        return c

    lax.fori_loop(1, NT, greet, 0)
    for side in sides + block_sides:
        pl.semaphore_signal(barrier, inc=1, device_id=side, device_id_type=MESH)

    stage_in = [
        pltpu.make_async_copy(initial.at[:, own_rows, own_cols], core(S, 0), local_sem.at[0]),
        pltpu.make_async_copy(forcing.at[:, own_rows, own_cols], core(F, 0), local_sem.at[1]),
        pltpu.make_async_copy(guess.at[0, :, own_rows, own_cols], core(S, me + 1), local_sem.at[2]),
    ]
    for copy in stage_in:
        copy.start()
    pl.semaphore_wait(barrier, NT - 1 + 8 + 3)

    def forward(peer):
        return pltpu.make_async_remote_copy(
            src_ref=guess.at[0, :, rows_of(peer), cols_of(peer)],
            dst_ref=core(S, me + 1),
            send_sem=fwd_send.at[peer],
            recv_sem=fwd_recv.at[me],
            device_id={"tm": peer},
            device_id_type=MESH,
        )

    def forwarded(peer):
        return pltpu.make_async_remote_copy(
            src_ref=guess.at[0, :, own_rows, own_cols],
            dst_ref=core(S, peer + 1),
            send_sem=fwd_send.at[peer],
            recv_sem=fwd_recv.at[peer],
            device_id={"tm": peer},
            device_id_type=MESH,
        )

    def start_forward(d, c):
        forward(lax.rem(me + d, NT)).start()
        return c

    forward(lax.rem(xl + 1, 2) * 8 + lax.rem(z + 4, 8)).start()
    forward(lax.rem(xl + 0, 2) * 8 + lax.rem(z + 4, 8)).start()
    forward(lax.rem(xl + 1, 2) * 8 + lax.rem(z + 1, 8)).start()
    forward(lax.rem(xl + 1, 2) * 8 + lax.rem(z + 7, 8)).start()
    forward(lax.rem(xl + 1, 2) * 8 + lax.rem(z + 3, 8)).start()
    forward(lax.rem(xl + 1, 2) * 8 + lax.rem(z + 5, 8)).start()
    forward(lax.rem(xl + 0, 2) * 8 + lax.rem(z + 1, 8)).start()
    forward(lax.rem(xl + 0, 2) * 8 + lax.rem(z + 7, 8)).start()
    forward(lax.rem(xl + 0, 2) * 8 + lax.rem(z + 3, 8)).start()
    forward(lax.rem(xl + 0, 2) * 8 + lax.rem(z + 5, 8)).start()
    forward(lax.rem(xl + 1, 2) * 8 + lax.rem(z + 2, 8)).start()
    forward(lax.rem(xl + 1, 2) * 8 + lax.rem(z + 6, 8)).start()
    forward(lax.rem(xl + 0, 2) * 8 + lax.rem(z + 2, 8)).start()
    forward(lax.rem(xl + 0, 2) * 8 + lax.rem(z + 6, 8)).start()
    forward(lax.rem(xl + 1, 2) * 8 + lax.rem(z + 0, 8)).start()
    load = pltpu.make_async_copy(forcing, block_forcing, local_sem.at[3])
    load.start()

    lane = lax.broadcasted_iota(jnp.int32, (HELD_ROWS, 128), 1)
    core_lane = lax.broadcasted_iota(jnp.int32, (ROWS, 128), 1)
    blank = jnp.zeros((ROWS, 128), jnp.float32)

    def lanes(j):
        return slice(128 * j, 128 * (j + 1))

    def halo_copies(b):
        parts = (
            (UP, row_out[b].at[0], row_in[b].at[1]),
            (DOWN, row_out[b].at[1], row_in[b].at[0]),
            (RIGHT, col_out.at[b, 0], col_in.at[b, 0]),
            (LEFT, col_out.at[b, 1], col_in.at[b, 1]),
            (DOWN_RIGHT, col_out.at[b, 0, 0:8], corner_in.at[b, 0, 0]),
            (UP_RIGHT, col_out.at[b, 0, ROWS - 8 : ROWS], corner_in.at[b, 0, 1]),
            (DOWN_LEFT, col_out.at[b, 1, 0:8], corner_in.at[b, 1, 0]),
            (UP_LEFT, col_out.at[b, 1, ROWS - 8 : ROWS], corner_in.at[b, 1, 1]),
        )
        return [
            pltpu.make_async_remote_copy(
                src_ref=src,
                dst_ref=dst,
                send_sem=halo_send.at[b, i],
                recv_sem=halo_recv.at[b, i],
                device_id=sides[to],
                device_id_type=MESH,
            )
            for i, (to, src, dst) in enumerate(parts)
        ]

    def pack(ref, k, b, i, packed):
        last, first = packed
        for c in range(2):
            row_out[b][0, i, c] = ref[k, c, ROWS - HALO : ROWS, 0:COLS]
            row_out[b][1, i, c] = ref[k, c, 0:HALO, 0:COLS]
            index = 8 * i + HALO * c
            mine = jnp.logical_and(core_lane >= index, core_lane < index + HALO)
            tail = ref[k, c, 0:ROWS, COLS - 128 : COLS]
            head = ref[k, c, 0:ROWS, 0:128]
            last = jnp.where(mine, pltpu.roll(tail, lax.rem(index + HALO, 128), 1), last)
            first = jnp.where(mine, pltpu.roll(head, index, 1), first)
        return last, first

    def send_halo(b, packed):
        col_out[b, 0] = packed[0]
        col_out[b, 1] = packed[1]
        for copy in halo_copies(b):
            copy.start()

    def wait_halo(b):
        for copy in halo_copies(b):
            copy.wait_recv()
        for side in range(2):
            wide[b, side, 0:ROWS] = col_in[b, side]
            wide[b, side, ROWS : ROWS + HALO] = corner_in[b, side, 0, 0:HALO]
            wide[b, side, ROWS + HALO : HELD_ROWS] = corner_in[b, side, 1, HALO:8]

    def unpack(ref, k, b, i):
        for c in range(2):
            ref[k, c, ROWS : ROWS + HALO, 0:COLS] = row_in[b][0, i, c]
            ref[k, c, ROWS + HALO : HELD_ROWS, 0:COLS] = row_in[b][1, i, c]
            index = 8 * i + HALO * c
            after = pltpu.roll(wide[b, 1], lax.rem(128 - index, 128), 1)
            before = pltpu.roll(wide[b, 0], lax.rem(256 - HALO - index, 128), 1)
            ref[k, c, :, COLS:HELD_COLS] = jnp.where(lane < 64, after, before)

    def slopes(first, second):
        return (
            0.5 + jnp.maximum(first, 0.0),
            0.5 - jnp.minimum(first, 0.0),
            0.5 + jnp.maximum(second, 0.0),
            0.5 - jnp.minimum(second, 0.0),
        )

    def rates(ref, k):
        w = [[ref[k, c, :, lanes(j)] for c in range(2)] for j in range(TILES)]
        up = [[pltpu.roll(w[j][c], 1, 1) for c in range(2)] for j in range(TILES)]
        down = [[pltpu.roll(w[j][c], 127, 1) for c in range(2)] for j in range(TILES)]
        result = []
        for j in range(TILES):
            west_w, east_w, south_w, north_w = slopes(*w[j])
            pair = []
            for c in range(2):
                x = w[j][c]
                west = pltpu.roll(x, 1, 0)
                east = pltpu.roll(x, HELD_ROWS - 1, 0)
                south = jnp.where(lane == 0, up[j - 1][c], up[j][c])
                north = jnp.where(lane == 127, down[(j + 1) % TILES][c], down[j][c])
                pair.append(
                    west_w * (west - x)
                    + east_w * (east - x)
                    + south_w * (south - x)
                    + north_w * (north - x)
                    + F[0, c, :, lanes(j)]
                )
            result.append(pair)
        return w, result

    def each(halo=True):
        return [(j, c) for j in range(TILES if halo else TILES - 1) for c in range(2)]

    def at(ref, k, c, j):
        return ref[k, c, :, lanes(j)]

    def put(ref, k, c, j, value):
        ref[k, c, :, lanes(j)] = value

    def landing(slot, t):
        if slot == 0:
            return out.at[1, :, rows_of(t), cols_of(t)]
        return prior.at[:, prior_rows(t), prior_cols(t)]

    def first_slot(k, t):
        away = lax.rem(lax.rem(t, 8) - lax.rem(k - 1, 8) + 8, 8)
        return jnp.where(jnp.logical_and(k < NT, jnp.logical_and(away >= 1, away <= 4)), 1, 0)

    def back(slot, k):
        return pltpu.make_async_remote_copy(
            src_ref=core(U, k),
            dst_ref=landing(slot, me),
            send_sem=ret_send.at[k],
            recv_sem=ret_recv.at[slot, me],
            device_id={"tm": k - 1 + slot},
            device_id_type=MESH,
        )

    def own(slot):
        return pltpu.make_async_copy(core(U, me + 1 - slot), landing(slot, me), ret_local.at[slot])

    def send_back(k):
        for slot in range(2):

            @pl.when(first_slot(k, me) == slot)
            def _(slot=slot):
                @pl.when(me == k - 1 + slot)
                def _():
                    own(slot).start()

                @pl.when(me != k - 1 + slot)
                def _():
                    back(slot, k).start()

    def hand_on(slot, t):
        return pltpu.make_async_remote_copy(
            src_ref=landing(slot, t),
            dst_ref=landing(1 - slot, t),
            send_sem=hand_send.at[slot, t],
            recv_sem=ret_recv.at[1 - slot, t],
            device_id={"tm": jnp.clip(me + 1 - 2 * slot, 0, NT - 1)},
            device_id_type=MESH,
        )

    def wait_landed(slot, t, local):
        if local:

            @pl.when(t == me)
            def _():
                own(slot).wait()

        @pl.when(t != me)
        def _():
            pltpu.make_async_remote_copy(
                src_ref=core(U, 1),
                dst_ref=landing(slot, t),
                send_sem=ret_send.at[1],
                recv_sem=ret_recv.at[slot, t],
                device_id={"tm": t},
                device_id_type=MESH,
            ).wait_recv()

    def near(slot, i):
        step = i // 2
        along = lax.rem(z + 8 - step, 8) if slot == 0 else lax.rem(z + step, 8)
        return lax.rem(i, 2) * 8 + along

    def far(slot, i):
        step = 1 + i // 2
        along = lax.rem(z + step, 8) if slot == 0 else lax.rem(z + 8 - step, 8)
        return lax.rem(i, 2) * 8 + along

    for copy in stage_in:
        copy.wait()
    packed = pack(S, 0, 0, 0, (blank, blank))
    send_halo(0, pack(F, 0, 0, 1, packed))

    arrivals = ((1, 1, 4), (5, 2, 4), (9, 3, 7))

    def arrive(first, b):
        def one(i, packed):
            k = first + i

            @pl.when(k - 1 != me)
            def _():
                forwarded(k - 1).wait_recv()

            return pack(S, k, b, i, packed)

        return one

    for first, b, n in arrivals:
        send_halo(b, lax.fori_loop(0, n, arrive(first, b), (blank, blank)))

    @pl.when(me != NT - 1)
    def _():
        forwarded(NT - 1).wait_recv()

    for c in range(2):
        S[NT, c, ROWS:HELD_ROWS, :] = jnp.zeros((HELD_ROWS - ROWS, HELD_COLS), jnp.float32)
        S[NT, c, 0:ROWS, COLS:HELD_COLS] = jnp.zeros((ROWS, 128), jnp.float32)

    wait_halo(0)
    unpack(S, 0, 0, 0)
    unpack(F, 0, 0, 1)

    def coarse_rhs(g, point, image, base):
        residual = g - (point - image)
        return residual + point - base

    def fine(k, relaxes, halo=True):
        w, rate = rates(S, k)
        for j, c in each():
            put(R0, k, c, j, rate[j][c])
            put(T1, k, c, j, w[j][c] + STEP * rate[j][c])
        w, rate = rates(T1, k)
        for j, c in each(halo):
            base = at(S, k, c, j) + 2 * STEP * at(R0, k, c, j)
            g = coarse_rhs(0.0, at(S, k + 1, c, j), w[j][c] + STEP * rate[j][c], base)
            put(G1, k + 1, c, j, g)
            if relaxes:
                put(Fx, k + 1, c, j, base + g)

    def descend(q):
        if q > 0:
            fine(4 * q, True)
        fine(4 * q + 1, False)
        fine(4 * q + 2, True)
        fine(4 * q + 3, False, halo=False)

        for i in range(2):
            m = 2 * q + i
            k = 2 * m
            w, rate = rates(Fx, k + 1)
            for j, c in each(halo=i == 0):
                base = at(S, k, c, j) + 4 * STEP * at(R0, k, c, j)
                g = coarse_rhs(at(G1, k + 2, c, j), at(S, k + 2, c, j), w[j][c] + 2 * STEP * rate[j][c], base)
                put(G2, m + 1, c, j, g)
                if i == 0:
                    put(Fx, k + 2, c, j, base + g)

        k = 4 * q
        w, rate = rates(Fx, k + 2)
        for j, c in each(halo=False):
            base = at(S, k, c, j) + 8 * STEP * at(R0, k, c, j)
            g = coarse_rhs(at(G2, 2 * q + 2, c, j), at(S, k + 4, c, j), w[j][c] + 4 * STEP * rate[j][c], base)
            put(G3, q + 1, c, j, g)
            put(Fx, k + 4, c, j, base + g)
            if q > 0:
                continue
            put(U, k + 1, c, j, at(Fx, k + 1, c, j))
            put(U, k + 2, c, j, w[j][c])
            put(U, k + 3, c, j, w[j][c] + 2 * STEP * rate[j][c] + at(G1, k + 3, c, j))
            put(U, k + 4, c, j, base + g)

    def exchange(b, fields):
        packed = (blank, blank)
        for i, (ref, k) in enumerate(fields):
            packed = pack(ref, k, b, i, packed)
        send_halo(b, packed)

    def exchanged(b, fields):
        wait_halo(b)
        for i, (ref, k) in enumerate(fields):
            unpack(ref, k, b, i)

    def ascend(k, targets, halo=True):
        w, rate = rates(U, k)
        for j, c in each(halo):
            for point, factor, right_side, index in targets:
                put(U, point, c, j, w[j][c] + factor * STEP * rate[j][c] + at(right_side, index, c, j))

    def coarsest(k):
        w, rate = rates(Fx, k + 4)
        for j, c in each(halo=k == 0):
            base = at(S, k, c, j) + 16 * STEP * at(R0, k, c, j)
            index = (k + 8) // 4
            g = coarse_rhs(at(G3, index, c, j), at(S, k + 8, c, j), w[j][c] + 8 * STEP * rate[j][c], base)
            if k == 0:
                put(U, 8, c, j, base + g)
                put(U, 5, c, j, w[j][c] + 2 * STEP * rate[j][c] + at(G1, 5, c, j))
                put(U, 6, c, j, w[j][c] + 4 * STEP * rate[j][c] + at(G2, 3, c, j))
            else:
                put(G4, 0, c, j, g)

    def return_points(first, offsets=(3, -4, 0, -1, 2, -3, 1, -2)):
        for offset in offsets:
            send_back(first + lax.rem(z + offset + 8, 8))

    def halos_of(first, b, n):
        wait_halo(b)

        def one(i, carry):
            unpack(S, first + i, b, i)
            return carry

        lax.fori_loop(0, n, one, 0)

    fields_a = ((Fx, 4), (G3, 2))
    fields_b = ((Fx, 12), (G3, 3))
    fine(0, True)
    halos_of(*arrivals[0])
    descend(0)
    halos_of(*arrivals[1])
    descend(1)
    exchange(4, fields_a)
    halos_of(*arrivals[2])
    descend(2)
    exchange(5, fields_b)
    exchanged(4, fields_a)
    coarsest(0)
    ascend(6, ((7, 2, G1, 7),), halo=False)
    return_points(1)
    descend(3)
    exchanged(5, fields_b)
    coarsest(8)
    ascend(8, ((9, 2, G1, 9), (10, 4, G2, 5), (12, 8, G3, 3), (16, 16, G4, 0)))
    ascend(10, ((11, 2, G1, 11),), halo=False)
    ascend(12, ((13, 2, G1, 13), (14, 4, G2, 7)))
    ascend(14, ((15, 2, G1, 15),), halo=False)
    return_points(9)

    def side_edge(t):
        first = t // 8 == 0
        return pltpu.make_async_remote_copy(
            src_ref=prior.at[:, prior_rows(t), pl.ds(pl.multiple_of(jnp.where(first, 128, BLOCK_COLS), 128), 128)],
            dst_ref=prior.at[:, prior_rows(t), pl.ds(pl.multiple_of(jnp.where(first, 128 + BLOCK_COLS, 0), 128), 128)],
            send_sem=edge_send.at[t],
            recv_sem=edge_recv.at[t],
            device_id={"sy": lax.rem(sy + jnp.where(first, 7, 1), 8)},
            device_id_type=MESH,
        )

    def end_edge(t, last):
        src, dst = (BLOCK_ROWS, 0) if last else (8, 8 + BLOCK_ROWS)
        return pltpu.make_async_remote_copy(
            src_ref=prior.at[:, src : src + 8, prior_cols(t)],
            dst_ref=prior.at[:, dst : dst + 8, prior_cols(t)],
            send_sem=end_send.at[2 * (t // 8) + last],
            recv_sem=end_recv.at[2 * (t // 8) + last],
            device_id=block_sides[0],
            device_id_type=MESH,
        )

    def send_edges(t):
        side_edge(t).start()
        for last in range(2):

            @pl.when(mirrored(lax.rem(t, 8)) == 7 * last)
            def _(last=last):
                end_edge(t, last).start()

    @pl.when(me == 0)
    def _():
        def one(t, carry):
            send_edges(t)
            return carry

        copy = pltpu.make_async_copy(
            initial, prior.at[:, 8 : 8 + BLOCK_ROWS, 128 : 128 + BLOCK_COLS], ret_local.at[1]
        )
        copy.start()
        copy.wait()
        lax.fori_loop(0, NT, one, 0)

    def pass_on(i, carry):
        @pl.when(me < NT - 1)
        def _():
            wait_landed(0, near(0, i), True)
            hand_on(0, near(0, i)).start()

        @pl.when(me > 0)
        def _():
            wait_landed(1, near(1, i), True)
            hand_on(1, near(1, i)).start()
            send_edges(near(1, i))

        return carry

    lax.fori_loop(0, 8, pass_on, 0)

    def rest(slot):
        def one(i, carry):
            wait_landed(slot, far(slot, i), False)
            if slot == 1:
                send_edges(far(slot, i))
            return carry

        lax.fori_loop(0, 8, one, 0)

    @pl.when(me > 0)
    def _():
        rest(1)

    block_tiles = BLOCK_COLS // 128

    def last_step(i, carry):
        along = lax.rem(z + jnp.where(i < 4, i, 11 - i), 8)
        g = mirrored(along)
        side_edge(along).wait_recv()
        side_edge(8 + along).wait_recv()
        for last in range(2):

            @pl.when(g == 7 - 7 * last)
            def _(last=last):
                end_edge(0, last).wait_recv()
                end_edge(8, last).wait_recv()

        around = pl.ds(pl.multiple_of(g * ROWS, ROWS), ROWS + 16)
        rows = pl.ds(pl.multiple_of(g * ROWS, ROWS), ROWS)
        inner = pl.ds(pl.multiple_of(8 + g * ROWS, 8), ROWS)
        y = [[prior[c, around, lanes(j + 1)] for c in range(2)] for j in range(block_tiles)]
        w = [[y[j][c][8 : 8 + ROWS] for c in range(2)] for j in range(block_tiles)]
        up = [[pltpu.roll(w[j][c], 1, 1) for c in range(2)] for j in range(block_tiles)]
        down = [[pltpu.roll(w[j][c], 127, 1) for c in range(2)] for j in range(block_tiles)]
        before = [pltpu.roll(prior[c, inner, lanes(0)], 1, 1) for c in range(2)]
        after = [pltpu.roll(prior[c, inner, lanes(block_tiles + 1)], 127, 1) for c in range(2)]
        for j in range(block_tiles):
            west_w, east_w, south_w, north_w = slopes(*w[j])
            for c in range(2):
                x = w[j][c]
                west = pltpu.roll(y[j][c], 1, 0)[8 : 8 + ROWS]
                east = pltpu.roll(y[j][c], ROWS + 15, 0)[8 : 8 + ROWS]
                south = jnp.where(core_lane == 0, up[j - 1][c] if j > 0 else before[c], up[j][c])
                north = jnp.where(core_lane == 127, down[j + 1][c] if j < block_tiles - 1 else after[c], down[j][c])
                rate = (
                    west_w * (west - x)
                    + east_w * (east - x)
                    + south_w * (south - x)
                    + north_w * (north - x)
                    + block_forcing[c, rows, lanes(j)]
                )
                out[0, c, rows, lanes(j)] = x + STEP * rate
        return carry

    load.wait()
    lax.fori_loop(0, 8, last_step, 0)

    for b in range(NB):
        for copy in halo_copies(b):
            copy.wait_send()
    def finish_edges(t, c):
        side_edge(t).wait_send()
        return c

    lax.fori_loop(0, NT, finish_edges, 0)
    for t in (0, 8):
        for last in range(2):
            end_edge(t, last).wait_send()

    def finish(i, c):
        @pl.when(i != me)
        def _():
            forward(i).wait_send()

        k = i + 1
        for slot in range(2):

            @pl.when(jnp.logical_and(first_slot(k, me) == slot, me != k - 1 + slot))
            def _(slot=slot):
                back(slot, k).wait_send()

        return c

    lax.fori_loop(0, NT, finish, 0)

    def finish_handed(i, c):
        @pl.when(me < NT - 1)
        def _():
            hand_on(0, near(0, i)).wait_send()

        @pl.when(me > 0)
        def _():
            hand_on(1, near(1, i)).wait_send()

        return c

    lax.fori_loop(0, 8, finish_handed, 0)

    @pl.when(me < NT - 1)
    def _():
        rest(0)

    @pl.when(me == NT - 1)
    def _():
        def one(t, c):
            wait_landed(0, t, True)
            return c

        lax.fori_loop(0, NT, one, 0)


def body(initial, forcing, guess):
    f32 = jnp.float32

    def field(n):
        return pltpu.VMEM((n, 2, HELD_ROWS, HELD_COLS), f32)

    scratch = [field(n) for n in (17, 1, 16, 16, 17, 9, 5, 1, 17, 17)]
    scratch += [
        pltpu.VMEM((2, BLOCK_ROWS + 16, BLOCK_COLS + 256), f32),
        pltpu.VMEM((2, BLOCK_ROWS, BLOCK_COLS), f32),
        pltpu.VMEM((NB, 2, ROWS, 128), f32),
        pltpu.VMEM((NB, 2, ROWS, 128), f32),
        pltpu.VMEM((NB, 2, 2, 8, 128), f32),
        pltpu.VMEM((NB, 2, HELD_ROWS, 128), f32),
    ]
    for _ in range(2):
        scratch += [pltpu.VMEM((2, n, 2, HALO, COLS), f32) for n in BATCH]
    dma = pltpu.SemaphoreType.DMA
    scratch += [dma((4,)), dma((NT,)), dma((NT,)), dma((NB, 8)), dma((NB, 8)), dma((NT + 1,)), dma((2, NT)), dma((2,))]
    scratch += [dma((2, NT)), dma((NT,)), dma((NT,)), dma((4,)), dma((4,))]
    spec = pl.BlockSpec(memory_space=pltpu.HBM)
    return pl.pallas_call(
        kernel,
        out_shape=pltpu.VMEM((2, 2, BLOCK_ROWS, BLOCK_COLS), f32),
        in_specs=[spec] * 3,
        out_specs=pl.BlockSpec(memory_space=pltpu.VMEM),
        scratch_shapes=scratch,
        compiler_params=pltpu.CompilerParams(
            collective_id=0, has_side_effects=True, vmem_limit_bytes=32 * 1024 * 1024
        ),
        name="cycle",
    )(*(pltpu.with_memory_space_constraint(x, pltpu.HBM) for x in (initial, forcing, guess)))


def solution(mesh):
    in_specs = (P(None, "sx", "sy"), P(None, "sx", "sy"), P("tm", None, "sx", "sy"))
    out_specs = P("tm", None, "sx", "sy")
    return jax.shard_map(body, mesh=mesh, in_specs=in_specs, out_specs=out_specs, check_vma=False)
```
